32 devices in a mesh: dp: 4 (over x, core), expert: 8 (over z, y).
Axes of the slice: x: 2, y: 2, z: 4, core: 2. Of those that a mesh axis runs over, the one named last changes fastest.
Arguments:
- tokens: bfloat16 [4096, 2048], P(('dp', 'expert')), may hold values from -6 to 6
- routes: int32 [4096, 2], P(('dp', 'expert')), may hold values from 0 to 7, all different within a row; in each aligned block of 128 rows (0 to 127, 128 to 255, ...) at most 48 rows name the same one
- gates: float32 [4096, 2], P(('dp', 'expert')), may hold values from 0.25 to 1
- keep: int32 [4096], P(('dp', 'expert')), may hold values 0 or 1
- cotangent: bfloat16 [4096, 2048], P(('dp', 'expert')), may hold values from -6 to 6
- w_gate: bfloat16 [8, 2048, 768], P('expert'), may hold values from -0.125 to 0.125
- w_up: bfloat16 [8, 2048, 768], P('expert'), may hold values from -0.125 to 0.125
- w_down: bfloat16 [8, 768, 2048], P('expert'), may hold values from -0.21875 to 0.21875
Outputs:
- token_grads: bfloat16 [4096, 2048], P(('dp', 'expert'))
- expert_grads: float32 [8, 2048, 2304], P('expert', 'dp')
The draws below stay inside these ranges and needn't reach their ends.
Inputs may be any that keep to these rules, and one draw needn't show every extreme that they name: `routes`: the 2 experts of a token differ. Among the 128 tokens of one device, no expert is named more than 48 times, a bound that some block reaches.
All inputs are finite; a program needn't handle non-finite values. No bound on the sum of `keep` on one device may be relied on, other than what follows from the above.
Results may differ from the reference program's by a relative error of at most 0.0061.
Values may be sent and summed in bfloat16 or wider, within the bound.
No kernel may reach another device: no remote copies, remote signals or barrier semaphores. Data moves between devices by JAX's collectives and lax.ppermute only.
A program may use at most 128 MiB of HBM per device.

```python
import math
import jax
import jax.numpy as jnp
import numpy as np
from jax import lax

D = 2048
FF = 768
TOPW = 2
TOK_DEV = 128
EXPERTS = 8
CAP = 48
TOKENS = 4096
N_DP = 4
N_EXPERT = 8


def set_ends(values, stream_key, low, high):
    longest = values.shape.index(max(values.shape))
    spots = []
    for shift in (0, 1):
        where = [jax.random.randint(jax.random.fold_in(stream_key, axis), (), 0, length) for axis, length in enumerate(values.shape)]
        where[longest] = (where[longest] + shift) % values.shape[longest]
        spots.append(tuple(where))
    return values.at[spots[0]].set(low).at[spots[1]].set(high)


def level_of(stream_key, dims, shards, smallest, largest):
    level, own = 1.0, jax.random.fold_in(stream_key, 6)
    for position, blocks in shards:
        draws = jnp.exp(jax.random.uniform(jax.random.fold_in(own, position), (blocks,), jnp.float32, smallest / len(shards), largest / len(shards)))
        level = level * jnp.repeat(draws, dims[position] // blocks).reshape([-1 if axis == position else 1 for axis in range(len(dims))])
    return level


def assign_block(stream_key, own, number, rows, amount, top, reach, lean):
    order = jax.random.permutation(stream_key, amount)
    crowded, common = portions_of(amount, rows * top, reach, lean, True), portions_of(amount, rows * top, reach, lean, False)
    places = jnp.arange(amount)

    def named(tallies, turn):
        used = int((tallies > 0).sum())
        fixed = max(1, used // 4)
        passed = fixed + (places - fixed + turn * (used - fixed)) % max(1, amount - fixed)
        return jnp.zeros((amount,), jnp.int32).at[order[jnp.where(places < fixed, places, passed)]].set(jnp.asarray(tallies, jnp.int32))

    tallies = jnp.where(number % 4 == 0, named(crowded, number // 4), named(common, number - number // 4 - 1))
    mixed = jax.random.permutation(jax.random.fold_in(own, 3), amount)
    giver, taker = mixed[0:amount // 2 * 2:2], mixed[1:amount // 2 * 2:2]
    slack = jnp.minimum(tallies[giver] - 1, reach - tallies[taker]) // 2
    slack = jnp.where((giver == order[0]) | (taker == order[0]) | (tallies[taker] == 0), 0, jnp.maximum(slack, 0))
    passed = jax.random.randint(jax.random.fold_in(own, 4), (amount // 2,), 0, 1 << 20) % (slack + 1)
    tallies = tallies.at[giver].add(-passed).at[taker].add(passed)
    members = jnp.searchsorted(jnp.cumsum(tallies), jnp.arange(rows * top), side="right").astype(jnp.int32)
    grid = members.reshape(top, rows).T
    grid = grid[jax.random.permutation(jax.random.fold_in(own, 1), rows)]
    turn = jax.random.randint(jax.random.fold_in(own, 2), (rows, 1), 0, top)
    return jnp.take_along_axis(grid, (jnp.arange(top)[None, :] + turn) % top, axis=1)


def portions_of(count, total, bound, skew, full):
    loads = [(1 << 20) // math.isqrt(standing ** skew) + 1 for standing in range(1, count + 1)]
    largest = bound if full else min(bound, max(-(-total // count), total * loads[0] // sum(loads)))
    least = 1 if total - largest >= count - 1 else 0
    counts, spare = [largest] + [least] * (count - 1), total - largest - least * (count - 1)
    while spare > 0:
        candidates = [i for i in range(1, count) if counts[i] < largest] or [i for i in range(1, count) if counts[i] < bound]
        mass, remaining = sum([loads[i] for i in candidates]), spare
        for i in candidates:
            addition = min(bound - counts[i], max(1, remaining * loads[i] // mass), spare)
            counts[i] = counts[i] + addition
            spare = spare - addition
    return np.array(counts)


def normal_values(stream_key, dims, deviation, limit, cuts=(), kind=jnp.bfloat16):
    gain = level_of(stream_key, dims, cuts, -0.22, 0.18) if cuts else 1.0
    entries = jax.random.normal(stream_key, dims, jnp.float32) * deviation * gain
    return jnp.minimum(jnp.maximum(entries, -limit), limit).astype(kind)


def setup_inputs(seed: int = 0) -> dict:
    streams_of = jax.random.split(jax.random.key(seed), 9)
    tokens = normal_values(streams_of[0], (TOKENS, D), 1.0, 6.0, ((0, 32),))
    routes_keys = jax.random.split(jax.random.fold_in(streams_of[1], 1), TOKENS // TOK_DEV)
    routes_turns = jax.random.permutation(jax.random.fold_in(streams_of[1], 3), TOKENS // TOK_DEV)
    routes = jax.vmap(lambda own, number: assign_block(jax.random.fold_in(streams_of[1], 2), own, number, TOK_DEV, EXPERTS, TOPW, CAP, 1))(routes_keys, routes_turns).reshape((TOKENS, TOPW))
    gates = jnp.clip(0.25 + 0.75 * jax.random.uniform(streams_of[2], (TOKENS, TOPW), jnp.float32) ** level_of(streams_of[2], (TOKENS, TOPW), ((0, 32),), -0.2, 0.2), 0.25, 1.0)
    keep = set_ends((jax.random.randint(streams_of[3], (TOKENS,), 0, 2) < 1).astype(jnp.int32), jax.random.fold_in(streams_of[3], 1), 0, 1)
    cotangent = normal_values(streams_of[4], (TOKENS, D), 1.0, 6.0, ((0, 32),))
    w_gate = normal_values(streams_of[5], (EXPERTS, D, FF), D ** -0.5, 0.125, ((0, 8),))
    w_up = normal_values(streams_of[6], (EXPERTS, D, FF), D ** -0.5, 0.125, ((0, 8),))
    w_down = normal_values(streams_of[7], (EXPERTS, FF, D), FF ** -0.5, 0.21875, ((0, 8),))
    return dict(tokens=tokens, routes=routes, gates=gates, keep=keep, cotangent=cotangent, w_gate=w_gate, w_up=w_up, w_down=w_down)


def logistic_parts(act):
    sigma = jax.nn.sigmoid(act)
    return act * sigma, sigma * (1.0 + act * (1.0 - sigma))


def dot_rows(left, right):
    return lax.dot_general(left, right, (((0,), (0,)), ((), ())), preferred_element_type=jnp.float32)


def dot_back(left, weight):
    return lax.dot_general(left, weight, (((1,), (1,)), ((), ())), preferred_element_type=jnp.float32)


def slot_numbers(routes):
    blocks = routes.reshape(-1, TOK_DEV * TOPW)
    expert_ids = lax.broadcasted_iota(jnp.int32, (1, 1, EXPERTS), 2)
    onehot = (blocks[:, :, None] == expert_ids).astype(jnp.int32)
    before = jnp.cumsum(onehot, axis=1) - onehot
    return jnp.sum(before * onehot, axis=2).reshape(-1, TOPW).astype(jnp.int32)


def reference(tokens, routes, gates, keep, cotangent, w_gate, w_up, w_down):
    slot = slot_numbers(routes)
    tok_ids = lax.broadcasted_iota(jnp.int32, (TOKENS, TOPW), 0)
    device = tok_ids // TOK_DEV
    group = device // N_EXPERT
    source = device % N_EXPERT
    place = (((group * EXPERTS + routes) * N_EXPERT + source) * CAP + slot).reshape(-1).astype(jnp.int32)
    pairs = N_DP * EXPERTS
    per_pair = N_EXPERT * CAP
    repeated = jnp.repeat(tokens, TOPW, axis=0)
    buffer = jnp.zeros((pairs * per_pair, D), tokens.dtype).at[place].set(repeated).reshape(pairs, per_pair, D)
    pair_ids = jnp.arange(pairs, dtype=jnp.int32)

    def expert_hidden(rows, expert):
        gate_act = jnp.dot(rows, w_gate[expert], preferred_element_type=jnp.float32)
        up_act = jnp.dot(rows, w_up[expert], preferred_element_type=jnp.float32)
        silu_val, slope = logistic_parts(gate_act)
        return (silu_val * up_act).astype(jnp.bfloat16)

    def forward(pair):
        expert = pair % EXPERTS
        hidden = expert_hidden(buffer[pair], expert)
        return jnp.dot(hidden, w_down[expert], preferred_element_type=jnp.float32).astype(jnp.bfloat16)

    routed_all = lax.map(forward, pair_ids).reshape(pairs * per_pair, D)
    routed_out = routed_all[place].reshape(TOKENS, TOPW, D).astype(jnp.float32)
    mixed = jnp.sum(gates[:, :, None] * routed_out, axis=1)
    by_device = tokens.reshape(pairs, TOK_DEV, D)

    def local(device_id):
        expert = device_id % EXPERTS
        hidden = expert_hidden(by_device[device_id], expert)
        return jnp.dot(hidden, w_down[expert], preferred_element_type=jnp.float32)

    keep_f = keep.astype(jnp.float32)[:, None]
    local_out = keep_f * lax.map(local, pair_ids).reshape(TOKENS, D)
    difference = mixed - local_out
    upstream = cotangent.astype(jnp.float32) + difference
    routed_cot = (gates[:, :, None] * upstream[:, None, :]).astype(jnp.bfloat16).reshape(-1, D)
    local_cot = (-(keep_f * difference)).astype(jnp.bfloat16).reshape(pairs, TOK_DEV, D)
    cot_buffer = jnp.zeros((pairs * per_pair, D), routed_cot.dtype).at[place].set(routed_cot).reshape(pairs, per_pair, D)

    def backward(carry, group_id):
        def one_expert(expert):
            pair = group_id * EXPERTS + expert
            rows_x = jnp.concatenate([buffer[pair], by_device[pair]], axis=0)
            rows_c = jnp.concatenate([cot_buffer[pair], local_cot[pair]], axis=0)
            gate_act = jnp.dot(rows_x, w_gate[expert], preferred_element_type=jnp.float32)
            up_act = jnp.dot(rows_x, w_up[expert], preferred_element_type=jnp.float32)
            silu_val, slope = logistic_parts(gate_act)
            hidden = (silu_val * up_act).astype(jnp.bfloat16)
            grad_hidden = dot_back(rows_c, w_down[expert])
            gate_back = (grad_hidden * up_act * slope).astype(jnp.bfloat16)
            up_back = (grad_hidden * silu_val).astype(jnp.bfloat16)
            back_rows = dot_back(gate_back, w_gate[expert]) + dot_back(up_back, w_up[expert])
            grads = jnp.concatenate([dot_rows(rows_x, gate_back), dot_rows(rows_x, up_back), dot_rows(rows_c, hidden)], axis=1)
            return back_rows[:per_pair].astype(jnp.bfloat16), back_rows[per_pair:], grads

        routed_back, local_back, grads = lax.map(one_expert, jnp.arange(EXPERTS, dtype=jnp.int32))
        return carry + grads, (routed_back, local_back)

    start = jnp.zeros((EXPERTS, D, 3 * FF), jnp.float32)
    total, outputs = lax.scan(backward, start, jnp.arange(N_DP, dtype=jnp.int32))
    routed_back, local_back = outputs
    picked = routed_back.reshape(pairs * per_pair, D)[place].reshape(TOKENS, TOPW, D).astype(jnp.float32)
    token_grads = (jnp.sum(picked, axis=1) + local_back.reshape(TOKENS, D)).astype(jnp.bfloat16)
    return (token_grads, total * (1.0 / N_DP))
```

```python
import jax
import jax.numpy as jnp
from jax import lax
from jax.sharding import PartitionSpec as P

F32 = jnp.float32
BF16 = jnp.bfloat16


def logistic_parts(act):
    sigma = jax.nn.sigmoid(act)
    return (act * sigma, sigma * (1.0 + act * (1.0 - sigma)))


def dot(left, right):
    return jnp.dot(left, right, preferred_element_type=F32)


def dot_rows(left, right):
    return lax.dot_general(left, right, (((0,), (0,)), ((), ())), preferred_element_type=F32)


def dot_back(left, weight):
    return lax.dot_general(left, weight, (((1,), (1,)), ((), ())), preferred_element_type=F32)


def halves(value):
    high = value.astype(BF16)
    return high, (value - high.astype(F32)).astype(BF16)


def on_device(tokens, routes, gates, keep, cotangent, w_gate, w_up, w_down):
    groups = lax.axis_size("expert")
    replicas = lax.axis_size("dp")
    tok_count, width = tokens.shape
    choose = routes.shape[1]
    capacity = 3 * tok_count * choose // (2 * groups)
    slots = groups * capacity
    cores = 2 if replicas % 2 == 0 else 1
    chips = replicas // cores
    part = width // replicas
    weight_gate, weight_up, weight_down = w_gate[0], w_up[0], w_down[0]

    def exchange(block):
        block = block.reshape(groups, capacity, -1)
        moved = lax.all_to_all(block, "expert", split_axis=0, concat_axis=0, tiled=True)
        return moved.reshape(slots, -1)

    expert_ids = lax.broadcasted_iota(jnp.int32, (tok_count, groups), 1)
    member = sum((routes[:, k : k + 1] == expert_ids).astype(BF16) for k in range(choose))
    lower = lax.broadcasted_iota(jnp.int32, (tok_count, tok_count), 0) > lax.broadcasted_iota(
        jnp.int32, (tok_count, tok_count), 1
    )
    before = dot(lower.astype(BF16), member).astype(jnp.int32)
    slot_ids = lax.broadcasted_iota(jnp.int32, (tok_count, slots), 1)
    hits = []
    for k in range(choose):
        chosen = routes[:, k : k + 1]
        slot = jnp.sum(jnp.where(chosen == expert_ids, before, 0), axis=1, keepdims=True)
        hits.append(slot_ids == chosen * capacity + slot)
    spread = sum(hit.astype(BF16) for hit in hits)
    gated = sum(jnp.where(hit, gates[:, k : k + 1], 0.0) for k, hit in enumerate(hits))
    slot_gate = jnp.sum(gated, axis=0)[:, None]
    gated_high, gated_low = halves(gated)

    rows = exchange(dot_rows(spread, tokens).astype(BF16))

    keep_f = keep.astype(F32)[:, None]
    local_gate = dot(tokens, weight_gate)
    local_up = dot(tokens, weight_up)
    local_silu, local_slope = logistic_parts(local_gate)
    local_hidden = (local_silu * local_up).astype(BF16)
    local_out = keep_f * dot(local_hidden, weight_down)

    gate_act = dot(rows, weight_gate)
    up_act = dot(rows, weight_up)
    silu, slope = logistic_parts(gate_act)
    hidden = (silu * up_act).astype(BF16)
    returned = exchange(dot(hidden, weight_down).astype(BF16))

    mixed = dot(gated_high, returned) + dot(gated_low, returned)
    difference = mixed - local_out
    upstream = cotangent.astype(F32) + difference
    local_cot = (-(keep_f * difference)).astype(BF16)
    up_high, up_low = halves(upstream)
    routed_cot = (slot_gate * (dot_rows(spread, up_high) + dot_rows(spread, up_low))).astype(BF16)
    cots = exchange(routed_cot)

    grad_hidden = dot_back(cots, weight_down)
    gate_back = (grad_hidden * (up_act * slope)).astype(BF16)
    up_back = (grad_hidden * silu).astype(BF16)
    back = dot_back(gate_back, weight_gate) + dot_back(up_back, weight_up)
    returned_back = exchange(back.astype(BF16))

    local_grad = dot_back(local_cot, weight_down)
    local_gate_back = (local_grad * (local_up * local_slope)).astype(BF16)
    local_up_back = (local_grad * local_silu).astype(BF16)
    local_back = dot_back(local_gate_back, weight_gate) + dot_back(local_up_back, weight_up)
    token_grads = (dot(spread, returned_back) + local_back).astype(BF16)

    core = lax.axis_index("dp") % cores
    chip = lax.axis_index("dp") // cores

    def with_sibling(*arrays):
        if cores == 1:
            return [arrays]
        pairs = [(i, i ^ 1) for i in range(replicas)]
        return [arrays, tuple(lax.ppermute(a, "dp", pairs) for a in arrays)]

    x_all = with_sibling(jnp.concatenate([rows, tokens], axis=0))
    h_all = with_sibling(jnp.concatenate([hidden, local_hidden], axis=0))
    c_all = with_sibling(jnp.concatenate([cots, local_cot], axis=0))
    g_all = with_sibling(
        jnp.concatenate([gate_back, local_gate_back], axis=0),
        jnp.concatenate([up_back, local_up_back], axis=0),
    )

    def columns(array, target):
        return lax.dynamic_slice_in_dim(array, (target * cores + core) * part, part, axis=1)

    def sums(target):
        total_gate = total_up = total_down = 0.0
        for (x,), (h,), (c,), (gate, up) in zip(x_all, h_all, c_all, g_all):
            x_part, c_part = columns(x, target), columns(c, target)
            total_gate += dot_rows(x_part, gate)
            total_up += dot_rows(x_part, up)
            total_down += dot_rows(c_part, h)
        return total_gate, total_up, total_down

    received = []
    for shift in range(1, chips):
        moves = [
            (chip_from * cores + i, (chip_from + shift) % chips * cores + i)
            for chip_from in range(chips)
            for i in range(cores)
        ]
        sent = [value.astype(BF16) for value in sums((chip + shift) % chips)]
        received.append([lax.ppermute(value, "dp", moves) for value in sent])
    totals = list(sums(chip))
    for arrays in received:
        totals = [total + value.astype(F32) for total, value in zip(totals, arrays)]
    expert_grads = (jnp.concatenate(totals, axis=1) * (1.0 / replicas))[None]
    return (token_grads, expert_grads)


def solution(mesh):
    return jax.shard_map(
        on_device,
        mesh=mesh,
        in_specs=(
            P(("dp", "expert"), None),
            P(("dp", "expert"), None),
            P(("dp", "expert"), None),
            P(("dp", "expert")),
            P(("dp", "expert"), None),
            P("expert", None, None),
            P("expert", None, None),
            P("expert", None, None),
        ),
        out_specs=(P(("dp", "expert"), None), P("expert", "dp", None)),
        check_vma=False,
    )
```

```python
import math

import jax
import jax.numpy as jnp
from jax import lax
from jax.experimental import pallas as pl
from jax.experimental.pallas import tpu as pltpu
from jax.sharding import PartitionSpec as P

F32 = jnp.float32
BF16 = jnp.bfloat16
MIB = 1 << 20
VMEM = pl.BlockSpec(memory_space=pltpu.VMEM)
SMEM = pl.BlockSpec(memory_space=pltpu.SMEM)
HBM = pl.BlockSpec(memory_space=pltpu.HBM)


def logistic_parts(act):
    sigma = jax.nn.sigmoid(act)
    return (act * sigma, sigma * (1.0 + act * (1.0 - sigma)))


def dot(left, right):
    return jnp.dot(left, right, preferred_element_type=F32)


def dot_rows(left, right):
    return lax.dot_general(left, right, (((0,), (0,)), ((), ())), preferred_element_type=F32)


def dot_back(left, weight):
    return lax.dot_general(left, weight, (((1,), (1,)), ((), ())), preferred_element_type=F32)


def tile_of(size, most):
    tile = most
    while size % tile:
        tile //= 2
    return tile


def held(array):
    return pltpu.with_memory_space_constraint(array, pltpu.HBM)


def pinned(array):
    return pltpu.with_memory_space_constraint(array, pltpu.VMEM)


def room(array):
    return pltpu.VMEM(array.shape, array.dtype)


def on_chip(dims, kind):
    return pltpu.VMEM(tuple(dims), kind)


def in_hbm(dims, kind):
    return pltpu.HBM(tuple(dims), kind)


def call(kernel, outs, operands, specs, flops, limit, scratch=(), name=None, aliases=None):
    total = sum(math.prod(o.shape) * o.dtype.itemsize for o in (*outs, *operands))
    return pl.pallas_call(
        kernel,
        out_shape=tuple(outs),
        in_specs=specs,
        out_specs=tuple(HBM if out.memory_space == pltpu.HBM else VMEM for out in outs),
        scratch_shapes=list(scratch),
        input_output_aliases=aliases or {},
        compiler_params=pltpu.CompilerParams(vmem_limit_bytes=limit * MIB),
        cost_estimate=pl.CostEstimate(flops=int(flops), bytes_accessed=int(total), transcendentals=0),
        name=name,
    )(*operands)


class Copies:
    def __init__(self, sems):
        self.sems, self.count, self.waiting = sems, 0, []

    def start(self, source, target, keep=False):
        copy = pltpu.make_async_copy(source, target, self.sems.at[self.count])
        self.count += 1
        copy.start()
        if keep:
            self.waiting.append(copy)
        return copy

    def finish(self):
        for copy in self.waiting:
            copy.wait()


def split(array, refs, cols):
    size = refs[0].shape[0]
    for i, ref in enumerate(refs):
        ref[:, cols] = array[i * size : (i + 1) * size]


def joined_rows(refs, cols):
    return jnp.concatenate([ref[:, cols] for ref in refs], axis=0) if len(refs) > 1 else refs[0][:, cols]


def place_of(ids_ref, cores, part):
    device = ids_ref[1]
    chip = device // cores
    return device * part, (device - chip * cores) * part, chip


def aligned(begin):
    return pl.multiple_of(begin, 128)


def chip_columns(ids_ref, shift, chips, cores, part):
    _, _, chip = place_of(ids_ref, cores, part)
    other = chip + shift
    return pl.ds(aligned(jnp.where(other >= chips, other - chips, other) * (cores * part)), cores * part)


def home_of(ids_ref, k, n_blocks):
    place = ids_ref[0] - k
    return jnp.where(place < 0, place + n_blocks, place) if n_blocks > 1 else 0


def column_of(row):
    count = row.shape[1]
    same = lax.broadcasted_iota(jnp.int32, (count, count), 0) == lax.broadcasted_iota(
        jnp.int32, (count, count), 1
    )
    return jnp.sum(jnp.where(same, row, 0.0), axis=1, keepdims=True)


def dispatch(ids, tokens, routes_t, groups, capacity, n_blocks):
    tok, width = tokens.shape
    choose = routes_t.shape[0]
    slots = groups * capacity
    pairs = choose * tok
    step = tile_of(width, 512)

    def kernel(ids_ref, tokens_hbm, routes_hbm, *refs):
        blocks, (place_ref, pick_ref, tokens_ref, routes_ref, sems) = refs[:n_blocks], refs[n_blocks:]
        copies = Copies(sems)
        routes_in = copies.start(routes_hbm, routes_ref)
        tokens_in = copies.start(tokens_hbm, tokens_ref)
        routes_in.wait()
        chosen = routes_ref[...]
        near = chosen - ids_ref[0]
        near = jnp.where(near < 0, near + groups, near)
        expert_ids = lax.broadcasted_iota(jnp.int32, (groups, tok), 0)
        member = jnp.zeros((groups, tok), F32)
        for k in range(choose):
            member += (chosen[k : k + 1, :] == expert_ids).astype(F32)
        upper = lax.broadcasted_iota(jnp.int32, (tok, tok), 0) < lax.broadcasted_iota(
            jnp.int32, (tok, tok), 1
        )
        before = dot(member.astype(BF16), upper.astype(F32).astype(BF16))
        slot_ids = lax.broadcasted_iota(jnp.int32, (slots, tok), 0)
        both = jnp.zeros((slots, tok), F32)
        for k in range(choose):
            mine = chosen[k : k + 1, :]
            slot = jnp.sum(jnp.where(mine == expert_ids, before, 0.0), axis=0, keepdims=True).astype(jnp.int32)
            hit = (slot_ids == near[k : k + 1, :] * capacity + slot).astype(F32)
            place_ref[:, k * tok : (k + 1) * tok] = hit.astype(BF16)
            both += hit
            hit = (slot_ids == mine * capacity + slot).astype(F32)
            pick_ref[k * tok : (k + 1) * tok, :] = hit.T.astype(BF16)
        both = both.astype(BF16)
        tokens_in.wait()
        for n in range(0, width, step):
            cols = pl.ds(n, step)
            split(dot(both, tokens_ref[:, cols]).astype(BF16), blocks, cols)

    outs = call(
        kernel,
        [on_chip((slots // n_blocks, width), BF16)] * n_blocks
        + [on_chip((slots, pairs), BF16), on_chip((pairs, slots), BF16)],
        [ids, held(tokens), held(routes_t)],
        [SMEM, HBM, HBM],
        2 * slots * tok * width,
        8,
        [room(tokens), room(routes_t), pltpu.SemaphoreType.DMA((2,))],
        name="dispatch",
    )
    return list(outs[:n_blocks]), *outs[n_blocks:]


def hidden_units(rows, gate_ref, up_ref, hidden_ref, silu_ref, factor_ref, f_tile):
    for j in range(0, gate_ref.shape[1], f_tile):
        cols = pl.ds(j, f_tile)
        gate = dot(rows, gate_ref[:, cols])
        up = dot(rows, up_ref[:, cols])
        silu, slope = logistic_parts(gate)
        silu_ref[:, cols] = silu
        factor_ref[:, cols] = up * slope
        hidden_ref[:, cols] = (silu * up).astype(BF16)


def forward_local(tokens, w_gate, w_up, w_down, keep_row):
    count, width = tokens.shape
    units = w_gate.shape[1]
    f_tile, d_tile = tile_of(units, 256), tile_of(width, 512)

    def kernel(tokens_hbm, gate_hbm, up_hbm, down_hbm, keep_hbm, *refs):
        out_hbm, silu_hbm, factor_hbm, hidden_ref, tokens_ref, gate_ref, up_ref, down_ref = refs[:8]
        keep_ref, out_ref, silu_ref, factor_ref, sems = refs[8:]
        copies = Copies(sems)
        arriving = [
            copies.start(source, target)
            for source, target in (
                (tokens_hbm, tokens_ref),
                (keep_hbm, keep_ref),
                (gate_hbm, gate_ref),
                (up_hbm, up_ref),
                (down_hbm, down_ref),
            )
        ]
        for copy in arriving[:4]:
            copy.wait()
        hidden_units(tokens_ref[...], gate_ref, up_ref, hidden_ref, silu_ref, factor_ref, f_tile)
        copies.start(silu_ref, silu_hbm, True)
        copies.start(factor_ref, factor_hbm, True)
        keep = column_of(keep_ref[...].astype(F32))
        arriving[4].wait()
        for n in range(0, width, d_tile):
            cols = pl.ds(n, d_tile)
            out_ref[:, cols] = keep * dot(hidden_ref[...], down_ref[:, cols])
        copies.start(out_ref, out_hbm, True)
        copies.finish()

    return call(
        kernel,
        [
            in_hbm((count, width), F32),
            in_hbm((count, units), F32),
            in_hbm((count, units), F32),
            on_chip((count, units), BF16),
            on_chip((count, width), BF16),
            on_chip(w_gate.shape, BF16),
            on_chip(w_up.shape, BF16),
            on_chip(w_down.shape, BF16),
        ],
        [held(array) for array in (tokens, w_gate, w_up, w_down, keep_row)],
        [HBM] * 5,
        6 * count * width * units,
        8,
        [
            room(keep_row),
            pltpu.VMEM((count, width), F32),
            pltpu.VMEM((count, units), F32),
            pltpu.VMEM((count, units), F32),
            pltpu.SemaphoreType.DMA((8,)),
        ],
        name="forward_local",
    )


def forward(ids, blocks, tokens, local_hidden, w_gate, w_up, w_down, chips, cores, part):
    n_blocks = len(blocks)
    size, width = blocks[0].shape
    count = n_blocks * size
    total = count + tokens.shape[0]
    units = w_gate.shape[1]
    f_tile, d_tile = tile_of(units, 256), tile_of(width, 512)

    def kernel(ids_ref, *refs):
        ins, refs = refs[:n_blocks], refs[n_blocks:]
        (tokens_ref, local_ref, gate_ref, up_ref, down_ref), refs = refs[:5], refs[5:]
        (out_hbm, rows_hbm, hidden_hbm, silu_hbm, factor_hbm), refs = refs[:5], refs[5:]
        sent, (out_ref, rows_ref, hidden_ref, silu_ref, factor_ref, sems) = refs[: chips - 1], refs[chips - 1 :]
        copies = Copies(sems)
        for i, ref in enumerate(ins):
            rows_ref[i * size : (i + 1) * size, :] = ref[...]
        rows_ref[count:, :] = tokens_ref[...]
        hidden_ref[count:, :] = local_ref[...]
        copies.start(rows_ref, rows_hbm, True)
        routed = pl.ds(0, count)
        hidden_units(
            rows_ref[:count, :], gate_ref, up_ref, hidden_ref.at[routed], silu_ref, factor_ref, f_tile
        )
        copies.start(hidden_ref, hidden_hbm, True)
        copies.start(silu_ref, silu_hbm, True)
        copies.start(factor_ref, factor_hbm, True)
        for n in range(0, width, d_tile):
            cols = pl.ds(n, d_tile)
            out_ref[:, cols] = dot(hidden_ref[:count, :], down_ref[:, cols]).astype(BF16)
            for k in range(n_blocks):
                target = out_hbm.at[pl.ds(home_of(ids_ref, k, n_blocks) * size, size), cols]
                copies.start(out_ref.at[pl.ds(k * size, size), cols], target, True)
        for shift, target in enumerate(sent, 1):
            target[...] = rows_ref[:, chip_columns(ids_ref, shift, chips, cores, part)]
        copies.finish()

    outs = call(
        kernel,
        [
            in_hbm((count, width), BF16),
            in_hbm((total, width), BF16),
            in_hbm((total, units), BF16),
            in_hbm((count, units), F32),
            in_hbm((count, units), F32),
        ]
        + [on_chip((total, cores * part), BF16)] * (chips - 1),
        [ids] + [pinned(array) for array in (*blocks, tokens, local_hidden, w_gate, w_up, w_down)],
        [SMEM] + [VMEM] * (n_blocks + 5),
        6 * count * width * units,
        16,
        [
            pltpu.VMEM((count, width), BF16),
            pltpu.VMEM((total, width), BF16),
            pltpu.VMEM((total, units), BF16),
            pltpu.VMEM((count, units), F32),
            pltpu.VMEM((count, units), F32),
            pltpu.SemaphoreType.DMA((4 + n_blocks * (width // d_tile),)),
        ],
        name="forward",
    )
    return *outs[:5], list(outs[5:])


def mix(returned, place, pick, gates_t, keep_row, cotangent, local_out, n_blocks):
    slots, width = returned.shape
    choose, tok = gates_t.shape
    step = tile_of(width, 512)

    def kernel(returned_ref, *refs):
        sources, refs = refs[:6], refs[6:]
        outs, local_ref, refs = refs[:n_blocks], refs[n_blocks], refs[n_blocks + 1 :]
        targets, sems = refs[:6], refs[6]
        pick_ref, gates_ref, keep_ref, out_ref, cot_ref, place_ref = targets
        copies = Copies(sems)
        arriving = [copies.start(source, target) for source, target in zip(sources, targets)]
        for copy in arriving:
            copy.wait()
        gates = [column_of(gates_ref[k : k + 1, :]) for k in range(choose)]
        keep = column_of(keep_ref[...].astype(F32))
        for n in range(0, width, step):
            cols = pl.ds(n, step)
            picked = dot(pick_ref[...], returned_ref[:, cols])
            mixed = sum(gates[k] * picked[k * tok : (k + 1) * tok] for k in range(choose))
            difference = mixed - out_ref[:, cols]
            upstream = cot_ref[:, cols].astype(F32) + difference
            local_ref[:, cols] = (-(keep * difference)).astype(BF16)
            routed = jnp.concatenate([(gate * upstream).astype(BF16) for gate in gates], axis=0)
            split(dot(place_ref[...], routed).astype(BF16), outs, cols)

    brought = [pick, gates_t, keep_row, local_out, cotangent, place]
    outs = call(
        kernel,
        [on_chip((slots // n_blocks, width), BF16)] * n_blocks + [on_chip((tok, width), BF16)],
        [returned] + [held(array) for array in brought],
        [VMEM] + [HBM] * 6,
        4 * slots * choose * tok * width,
        10,
        [room(array) for array in brought] + [pltpu.SemaphoreType.DMA((6,))],
        name="mix",
    )
    return list(outs[:n_blocks]), outs[n_blocks]


def gradients(cots, silu_ref, factor_ref, down_ref, gate_back, up_back, f_tile):
    for j in range(0, gate_back.shape[1], f_tile):
        cols = pl.ds(j, f_tile)
        grad = dot_back(cots, down_ref[cols, :])
        gate_back[:, cols] = (grad * factor_ref[:, cols]).astype(BF16)
        up_back[:, cols] = (grad * silu_ref[:, cols]).astype(BF16)


def backward_local(ids, cots, silu, factor, w_gate, w_up, w_down, kept, chips, cores, part):
    count, width = cots.shape
    units = w_gate.shape[1]
    f_tile, d_tile = tile_of(units, 256), tile_of(width, 512)
    span = cores * part
    n_kept = len(kept)

    def kernel(ids_ref, cots_ref, silu_hbm, factor_hbm, gate_hbm, up_hbm, down_hbm, *refs):
        kept_hbm, (back_hbm, gate_ref, up_ref, down_ref), refs = refs[:n_kept], refs[n_kept : n_kept + 4], refs[n_kept + 4 :]
        kept_refs, sent, refs = refs[:n_kept], refs[n_kept : n_kept + chips], refs[n_kept + chips :]
        back_ref, silu_ref, factor_ref, gate_back, up_back, sems = refs
        copies = Copies(sems)
        first = [copies.start(s, t) for s, t in ((silu_hbm, silu_ref), (factor_hbm, factor_ref), (down_hbm, down_ref))]
        second = [copies.start(s, t) for s, t in ((gate_hbm, gate_ref), (up_hbm, up_ref))]
        for source, target in zip(kept_hbm, kept_refs):
            copies.start(source, target, True)
        for copy in first:
            copy.wait()
        gradients(cots_ref[...], silu_ref, factor_ref, down_ref, gate_back, up_back, f_tile)
        for shift, target in enumerate(sent):
            target[:, :span] = cots_ref[:, chip_columns(ids_ref, shift, chips, cores, part)]
            target[:, span : span + units] = gate_back[...]
            target[:, span + units :] = up_back[...]
        for copy in second:
            copy.wait()
        for n in range(0, width, d_tile):
            cols = pl.ds(n, d_tile)
            back = dot_back(gate_back[...], gate_ref[cols, :])
            back += dot_back(up_back[...], up_ref[cols, :])
            back_ref[:, cols] = back
        copies.start(back_ref, back_hbm, True)
        copies.finish()

    outs = call(
        kernel,
        [in_hbm((count, width), F32)]
        + [on_chip(array.shape, array.dtype) for array in (w_gate, w_up, w_down, *kept)]
        + [on_chip((count, span + 2 * units), BF16)] * chips,
        [ids, pinned(cots)] + [held(array) for array in (silu, factor, w_gate, w_up, w_down, *kept)],
        [SMEM, VMEM] + [HBM] * (5 + n_kept),
        6 * count * width * units,
        10,
        [
            pltpu.VMEM((count, width), F32),
            room(silu),
            room(factor),
            pltpu.VMEM((count, units), BF16),
            pltpu.VMEM((count, units), BF16),
            pltpu.SemaphoreType.DMA((6 + n_kept,)),
        ],
        name="backward_local",
    )
    return outs[0], outs[1:4], outs[4 : 4 + n_kept], list(outs[4 + n_kept :])


def collect(ids, blocks, chips, cores, part):
    n_blocks = len(blocks)
    size, width = blocks[0].shape
    count, span = n_blocks * size, cores * part

    def kernel(ids_ref, *refs):
        ins, (rows_ref, *sent) = refs[:n_blocks], refs[n_blocks:]
        for i, ref in enumerate(ins):
            rows = pl.ds(i * size, size)
            rows_ref[rows, :] = ref[...]
            for shift, target in enumerate(sent, 1):
                target[rows, :] = ref[:, chip_columns(ids_ref, shift, chips, cores, part)]

    outs = call(
        kernel,
        [on_chip((count, width), BF16)] + [on_chip((count, span), BF16)] * (chips - 1),
        [ids] + [pinned(block) for block in blocks],
        [SMEM] + [VMEM] * n_blocks,
        0,
        8,
        name="collect",
    )
    return outs[0], list(outs[1:])


def backward(ids, cots, silu, factor, w_gate, w_up, w_down, n_blocks):
    count, width = cots.shape
    units = w_gate.shape[1]
    size = count // n_blocks
    f_tile, d_tile = tile_of(units, 256), tile_of(width, 512)

    def kernel(ids_ref, cots_ref, silu_ref, factor_ref, gate_ref, up_ref, down_ref, *refs):
        back_hbm, gate_hbm, up_hbm, back_ref, gate_back, up_back, sems = refs
        copies = Copies(sems)
        gradients(cots_ref[...], silu_ref, factor_ref, down_ref, gate_back, up_back, f_tile)
        copies.start(gate_back, gate_hbm, True)
        copies.start(up_back, up_hbm, True)
        for n in range(0, width, d_tile):
            cols = pl.ds(n, d_tile)
            back = dot_back(gate_back[...], gate_ref[cols, :])
            back += dot_back(up_back[...], up_ref[cols, :])
            back_ref[:, cols] = back.astype(BF16)
            for k in range(n_blocks):
                target = back_hbm.at[pl.ds(home_of(ids_ref, k, n_blocks) * size, size), cols]
                copies.start(back_ref.at[pl.ds(k * size, size), cols], target, True)
        copies.finish()

    return call(
        kernel,
        [in_hbm((count, width), BF16), in_hbm((count, units), BF16), in_hbm((count, units), BF16)],
        [ids] + [pinned(array) for array in (cots, silu, factor, w_gate, w_up, w_down)],
        [SMEM] + [VMEM] * 6,
        6 * count * width * units,
        10,
        [
            pltpu.VMEM((count, width), BF16),
            pltpu.VMEM((count, units), BF16),
            pltpu.VMEM((count, units), BF16),
            pltpu.SemaphoreType.DMA((2 + n_blocks * (width // d_tile),)),
        ],
        name="backward",
    )


WHOLE, CHIP = -1, -2


def weight_sums(ids, cores, part, terms, previous, units, sections, scale):
    step = tile_of(units, 256)
    begun = [] if previous is None else [previous]
    arrays = []
    for left, right, *_ in terms:
        for array, _ in left + right:
            arrays += [] if any(array is other for other in arrays) else [array]
    where = lambda array: next(i for i, other in enumerate(arrays) if other is array)
    rows_of = [sum(array.shape[0] for array, _ in left) for left, *_ in terms]
    n_copies = sum(len(left) + len(right) for left, right, *_ in terms)

    def kernel(ids_ref, *refs):
        sources, refs = refs[: len(arrays)], refs[len(arrays) :]
        begun_hbm, out_hbm, refs = refs[: len(begun)], refs[len(begun)], refs[len(begun) + 1 :]
        lefts, rights, out_ref, sems = refs[: len(terms)], refs[len(terms) : 2 * len(terms)], refs[-2], refs[-1]
        copies = Copies(sems)
        at_whole, at_chip, _ = place_of(ids_ref, cores, part)

        def bring(pieces, target, columns):
            row, started = 0, []
            for array, first in pieces:
                first = aligned(at_whole if first == WHOLE else at_chip) if first < 0 else first
                count = array.shape[0]
                source = sources[where(array)].at[:, pl.ds(first, columns)]
                started.append(copies.start(source, target.at[pl.ds(row, count), :]))
                row += count
            return started

        arriving = []
        for (left, right, _, wide), left_ref, right_ref in zip(terms, lefts, rights):
            arriving += bring(left, left_ref, part) + bring(right, right_ref, wide * units)
        for source in begun_hbm:
            for section in sections:
                cols = pl.ds(section * units, units)
                arriving.append(copies.start(source.at[:, cols], out_ref.at[:, cols]))
        for copy in arriving:
            copy.wait()
        for section in sections:
            for at in range(0, units, step):
                cols = pl.ds(section * units + at, step)
                total = out_ref[:, cols] if begun else None
                for i, (_, _, first, wide) in enumerate(terms):
                    if first <= section < first + wide:
                        begin = (section - first) * units + at
                        term = dot_rows(lefts[i][...], rights[i][:, begin : begin + step])
                        total = term if total is None else total + term
                out_ref[:, cols] = total if scale is None else total * scale
                copies.start(out_ref.at[:, cols], out_hbm.at[:, cols], True)
        copies.finish()

    operands = [ids] + [held(array) for array in (*arrays, *begun)]
    (out,) = call(
        kernel,
        [in_hbm((part, 3 * units), F32)],
        operands,
        [SMEM] + [HBM] * (len(operands) - 1),
        sum(2 * rows * part * wide * units for rows, (*_, wide) in zip(rows_of, terms)),
        20,
        [pltpu.VMEM((rows, part), BF16) for rows in rows_of]
        + [pltpu.VMEM((rows, wide * units), BF16) for rows, (*_, wide) in zip(rows_of, terms)]
        + [
            pltpu.VMEM((part, 3 * units), F32),
            pltpu.SemaphoreType.DMA((n_copies + len(begun) * len(sections) + len(sections) * (units // step),)),
        ],
        name="weight_sums",
        aliases={len(operands) - 1: 0} if begun else None,
    )
    return out


def combine(returned, pick, local_back, choose):
    slots, width = returned.shape
    tok = local_back.shape[0]
    step = tile_of(width, 512)

    def kernel(returned_ref, pick_hbm, local_hbm, out_hbm, pick_ref, local_ref, out_ref, sems):
        copies = Copies(sems)
        pick_in = copies.start(pick_hbm, pick_ref)
        local_in = copies.start(local_hbm, local_ref)
        pick_in.wait()
        local_in.wait()
        both = sum(pick_ref[k * tok : (k + 1) * tok, :].astype(F32) for k in range(choose)).astype(BF16)
        for n in range(0, width, step):
            cols = pl.ds(n, step)
            out_ref[:, cols] = (dot(both, returned_ref[:, cols]) + local_ref[:, cols]).astype(BF16)
            copies.start(out_ref.at[:, cols], out_hbm.at[:, cols], True)
        copies.finish()

    (out,) = call(
        kernel,
        [in_hbm((tok, width), BF16)],
        [returned, held(pick), held(local_back)],
        [VMEM, HBM, HBM],
        2 * slots * tok * width,
        8,
        [
            room(pick),
            room(local_back),
            pltpu.VMEM((tok, width), BF16),
            pltpu.SemaphoreType.DMA((2 + width // step,)),
        ],
        name="combine",
    )
    return out


def on_device(tokens, routes, gates, keep, cotangent, w_gate, w_up, w_down):
    groups = lax.axis_size("expert")
    replicas = lax.axis_size("dp")
    tok_count, width = tokens.shape
    choose = routes.shape[1]
    capacity = 3 * tok_count * choose // (2 * groups)
    slots = groups * capacity
    apart = capacity % 16 == 0 and groups <= 8
    n_blocks = groups if apart else 1
    cores = 2 if replicas % 2 == 0 else 1
    chips = replicas // cores
    part = width // replicas
    span = cores * part
    units = w_gate.shape[2]
    weights = (w_gate[0], w_up[0], w_down[0])
    siblings = [(i, i ^ 1) for i in range(replicas)]
    first = lax.axis_index("expert") if apart else 0
    ids = jnp.stack([jnp.asarray(first, jnp.int32), lax.axis_index("dp").astype(jnp.int32)])
    keep_row = keep[None]
    together = lax.optimization_barrier
    far_first = sorted(range(1, groups), key=lambda k: abs(k - groups / 2))

    def at_once(block):
        block = block.reshape(groups, capacity, -1)
        moved = lax.all_to_all(block, "expert", split_axis=0, concat_axis=0, tiled=True)
        return moved.reshape(slots, -1)

    def step_by_step(blocks):
        if not apart:
            return [at_once(blocks[0])]
        moved = [blocks[0]] + [None] * (groups - 1)
        for k in far_first:
            moved[k] = lax.ppermute(blocks[k], "expert", [(i, (i + k) % groups) for i in range(groups)])
        return moved

    def to_chips(arrays):
        return [
            lax.ppermute(
                array,
                "dp",
                [
                    (start * cores + i, (start + shift) % chips * cores + i)
                    for start in range(chips)
                    for i in range(cores)
                ],
            )
            for shift, array in enumerate(arrays, 1)
        ]

    def from_sibling(arrays):
        return [lax.ppermute(array, "dp", siblings) for array in arrays] if cores == 2 else []

    def to_others(array):
        return to_chips([array] * (chips - 1))

    blocks, place, pick = dispatch(ids, tokens, routes.T, groups, capacity, n_blocks)
    blocks = step_by_step(blocks)
    local_out, local_silu, local_factor, local_hidden, tokens_on, *on = forward_local(tokens, *weights, keep_row)
    out, rows, hidden, silu, factor, x_send = forward(
        ids, blocks, tokens_on, local_hidden, *on, chips, cores, part
    )
    returned = at_once(out)
    x_far = to_chips(x_send)
    h_far = to_others(hidden)
    returned, x_far, h_far = together((returned, x_far, h_far))
    blocks, local_cot = mix(returned, place, pick, gates.T, keep_row, cotangent, local_out, n_blocks)
    blocks = step_by_step(blocks)
    local_back, on, kept, l_send = backward_local(
        ids, local_cot, local_silu, local_factor, *weights, (silu, factor), chips, cores, part
    )
    l_own, l_far = l_send[0], to_chips(l_send[1:])
    blocks, l_far = together((blocks, l_far))
    cots, c_send = collect(ids, blocks, chips, cores, part)
    back, gate_back, up_back = backward(ids, cots, *kept, *on, n_blocks)
    returned = at_once(back)
    c_far = to_chips(c_send)
    g_far = to_others(gate_back)
    u_far = to_others(up_back)

    def terms_x(xs, at, gs, us, ls):
        return [
            ([(x, at)], [(right, 0), (l, span + section * units)], section, 1)
            for x, g, u, l in zip(xs, gs, us, ls)
            for section, right in enumerate((g, u))
        ]

    def terms_c(cs, at, ls, hs):
        return [([(c, at), (l, CHIP)], [(h, 0)], 2, 1) for c, l, h in zip(cs, ls, hs)]

    def both_cores(arrays):
        return arrays + from_sibling(arrays)

    x_near, h_near, l_near = both_cores([rows]), both_cores([hidden]), both_cores([l_own])
    g_near, u_near, c_near = both_cores([gate_back]), both_cores([up_back]), both_cores([cots])
    x_far, h_far, l_far = both_cores(x_far), both_cores(h_far), both_cores(l_far)
    c_far, g_far = both_cores(c_far), both_cores(g_far)
    scale = 1.0 / replicas
    totals = weight_sums(
        ids,
        cores,
        part,
        terms_x(x_near, WHOLE, g_near, u_near, l_near) + terms_c(c_near, WHOLE, l_near, h_near),
        None,
        units,
        (0, 1, 2),
        None,
    )
    if chips > 1:
        totals = weight_sums(
            ids, cores, part, terms_c(c_far, CHIP, l_far, h_far), totals, units, (2,), scale
        )
        u_far, totals = together((u_far, totals))
    u_far = both_cores(u_far)
    totals = weight_sums(
        ids,
        cores,
        part,
        terms_x(x_far, CHIP, g_far, u_far, l_far),
        totals,
        units,
        (0, 1) if chips > 1 else (0, 1, 2),
        scale,
    )
    token_grads = combine(returned, pick, local_back, choose)
    return (token_grads, totals[None])


def solution(mesh):
    return jax.shard_map(
        on_device,
        mesh=mesh,
        in_specs=(
            P(("dp", "expert"), None),
            P(("dp", "expert"), None),
            P(("dp", "expert"), None),
            P(("dp", "expert")),
            P(("dp", "expert"), None),
            P("expert", None, None),
            P("expert", None, None),
            P("expert", None, None),
        ),
        out_specs=(P(("dp", "expert"), None), P("expert", "dp", None)),
        check_vma=False,
    )
```

```python
import jax
import jax.numpy as jnp
from jax import lax
from jax.experimental import pallas as pl
from jax.experimental.pallas import tpu as pltpu
from jax.sharding import PartitionSpec as P

F32 = jnp.float32
BF16 = jnp.bfloat16
MIB = 1 << 20
LONG = 20_000_000_000
VMEM = pl.BlockSpec(memory_space=pltpu.VMEM)
SMEM = pl.BlockSpec(memory_space=pltpu.SMEM)
HBM = pl.BlockSpec(memory_space=pltpu.HBM)


def logistic_parts(act):
    sigma = jax.nn.sigmoid(act)
    return (act * sigma, sigma * (1.0 + act * (1.0 - sigma)))


def dot(left, right):
    return jnp.dot(left, right, preferred_element_type=F32)


def dot_rows(left, right):
    return lax.dot_general(left, right, (((0,), (0,)), ((), ())), preferred_element_type=F32)


def dot_back(left, weight):
    return lax.dot_general(left, weight, (((1,), (1,)), ((), ())), preferred_element_type=F32)


def tile_of(size, most):
    tile = most
    while size % tile:
        tile //= 2
    return tile


def held(array):
    return pltpu.with_memory_space_constraint(array, pltpu.HBM)


def pinned(array):
    return pltpu.with_memory_space_constraint(array, pltpu.VMEM)


def room(array):
    return pltpu.VMEM(array.shape, array.dtype)


def on_chip(dims, kind):
    return pltpu.VMEM(tuple(dims), kind)


def in_hbm(dims, kind):
    return pltpu.HBM(tuple(dims), kind)


def call(kernel, outs, operands, specs, limit, scratch=(), name=None, aliases=None, weight=0):
    return pl.pallas_call(
        kernel,
        out_shape=tuple(outs),
        in_specs=specs,
        out_specs=tuple(HBM if out.memory_space == pltpu.HBM else VMEM for out in outs),
        scratch_shapes=list(scratch),
        input_output_aliases=aliases or {},
        compiler_params=pltpu.CompilerParams(vmem_limit_bytes=limit * MIB),
        cost_estimate=pl.CostEstimate(flops=weight, bytes_accessed=0, transcendentals=0),
        name=name,
    )(*operands)


class Copies:
    def __init__(self, sems):
        self.sems, self.count, self.waiting = sems, 0, []

    def start(self, source, target, keep=False):
        copy = pltpu.make_async_copy(source, target, self.sems.at[self.count])
        self.count += 1
        copy.start()
        if keep:
            self.waiting.append(copy)
        return copy

    def finish(self):
        for copy in self.waiting:
            copy.wait()


def split(array, refs, cols):
    size = refs[0].shape[0]
    for i, ref in enumerate(refs):
        ref[:, cols] = array[i * size : (i + 1) * size]


def joined_rows(refs, cols):
    return jnp.concatenate([ref[:, cols] for ref in refs], axis=0) if len(refs) > 1 else refs[0][:, cols]


def place_of(ids_ref, cores, part):
    device = ids_ref[1]
    chip = device // cores
    return device * part, (device - chip * cores) * part, chip


def aligned(begin):
    return pl.multiple_of(begin, 128)


def chip_columns(ids_ref, shift, chips, cores, part):
    _, _, chip = place_of(ids_ref, cores, part)
    other = chip + shift
    return pl.ds(aligned(jnp.where(other >= chips, other - chips, other) * (cores * part)), cores * part)


def home_of(ids_ref, k, n_blocks):
    place = ids_ref[0] - k
    return jnp.where(place < 0, place + n_blocks, place) if n_blocks > 1 else 0


def column_of(row):
    count = row.shape[1]
    same = lax.broadcasted_iota(jnp.int32, (count, count), 0) == lax.broadcasted_iota(
        jnp.int32, (count, count), 1
    )
    return jnp.sum(jnp.where(same, row, 0.0), axis=1, keepdims=True)


def dispatch(ids, tokens, routes_t, groups, capacity, n_blocks):
    tok, width = tokens.shape
    choose = routes_t.shape[0]
    slots = groups * capacity
    pairs = choose * tok
    step = tile_of(width, 512)

    def kernel(ids_ref, tokens_hbm, routes_hbm, *refs):
        blocks, (place_hbm, pick_hbm, place_ref, pick_ref, tokens_ref, routes_ref, sems) = refs[:n_blocks], refs[n_blocks:]
        copies = Copies(sems)
        routes_in = copies.start(routes_hbm, routes_ref)
        tokens_in = copies.start(tokens_hbm, tokens_ref)
        routes_in.wait()
        chosen = routes_ref[...]
        near = chosen - ids_ref[0]
        near = jnp.where(near < 0, near + groups, near)
        expert_ids = lax.broadcasted_iota(jnp.int32, (groups, tok), 0)
        member = jnp.zeros((groups, tok), F32)
        for k in range(choose):
            member += (chosen[k : k + 1, :] == expert_ids).astype(F32)
        upper = lax.broadcasted_iota(jnp.int32, (tok, tok), 0) < lax.broadcasted_iota(
            jnp.int32, (tok, tok), 1
        )
        before = dot(member.astype(BF16), upper.astype(F32).astype(BF16))
        slot_ids = lax.broadcasted_iota(jnp.int32, (slots, tok), 0)
        both = jnp.zeros((slots, tok), F32)
        for k in range(choose):
            mine = chosen[k : k + 1, :]
            slot = jnp.sum(jnp.where(mine == expert_ids, before, 0.0), axis=0, keepdims=True).astype(jnp.int32)
            hit = (slot_ids == near[k : k + 1, :] * capacity + slot).astype(F32)
            place_ref[:, k * tok : (k + 1) * tok] = hit.astype(BF16)
            both += hit
            hit = (slot_ids == mine * capacity + slot).astype(F32)
            pick_ref[k * tok : (k + 1) * tok, :] = hit.T.astype(BF16)
        copies.start(place_ref, place_hbm, True)
        copies.start(pick_ref, pick_hbm, True)
        both = both.astype(BF16)
        tokens_in.wait()
        for n in range(0, width, step):
            cols = pl.ds(n, step)
            split(dot(both, tokens_ref[:, cols]).astype(BF16), blocks, cols)
        copies.finish()

    outs = call(
        kernel,
        [on_chip((slots // n_blocks, width), BF16)] * n_blocks
        + [in_hbm((slots, pairs), BF16), in_hbm((pairs, slots), BF16)],
        [ids, held(tokens), held(routes_t)],
        [SMEM, HBM, HBM],
        8,
        [
            pltpu.VMEM((slots, pairs), BF16),
            pltpu.VMEM((pairs, slots), BF16),
            room(tokens),
            room(routes_t),
            pltpu.SemaphoreType.DMA((4,)),
        ],
        name="dispatch",
    )
    return list(outs[:n_blocks]), *outs[n_blocks:]


def hidden_units(rows, gate_ref, up_ref, hidden_ref, silu_ref, factor_ref, f_tile):
    for j in range(0, gate_ref.shape[1], f_tile):
        cols = pl.ds(j, f_tile)
        gate = dot(rows, gate_ref[:, cols])
        up = dot(rows, up_ref[:, cols])
        silu, slope = logistic_parts(gate)
        silu_ref[:, cols] = silu
        factor_ref[:, cols] = up * slope
        hidden_ref[:, cols] = (silu * up).astype(BF16)


def forward_local(tokens, w_gate, w_up, w_down, keep_row):
    count, width = tokens.shape
    units = w_gate.shape[1]
    f_tile, d_tile = tile_of(units, 256), tile_of(width, 512)

    def kernel(tokens_hbm, gate_hbm, up_hbm, down_hbm, keep_hbm, *refs):
        out_hbm, silu_hbm, factor_hbm, hidden_ref, tokens_ref, gate_ref, up_ref, down_ref = refs[:8]
        keep_ref, out_ref, silu_ref, factor_ref, sems = refs[8:]
        copies = Copies(sems)
        arriving = [
            copies.start(source, target)
            for source, target in (
                (tokens_hbm, tokens_ref),
                (keep_hbm, keep_ref),
                (gate_hbm, gate_ref),
                (up_hbm, up_ref),
                (down_hbm, down_ref),
            )
        ]
        for copy in arriving[:4]:
            copy.wait()
        hidden_units(tokens_ref[...], gate_ref, up_ref, hidden_ref, silu_ref, factor_ref, f_tile)
        copies.start(silu_ref, silu_hbm, True)
        copies.start(factor_ref, factor_hbm, True)
        keep = column_of(keep_ref[...].astype(F32))
        arriving[4].wait()
        for n in range(0, width, d_tile):
            cols = pl.ds(n, d_tile)
            out_ref[:, cols] = keep * dot(hidden_ref[...], down_ref[:, cols])
        copies.start(out_ref, out_hbm, True)
        copies.finish()

    return call(
        kernel,
        [
            in_hbm((count, width), F32),
            in_hbm((count, units), F32),
            in_hbm((count, units), F32),
            on_chip((count, units), BF16),
            on_chip((count, width), BF16),
            on_chip(w_gate.shape, BF16),
            on_chip(w_up.shape, BF16),
            on_chip(w_down.shape, BF16),
        ],
        [held(array) for array in (tokens, w_gate, w_up, w_down, keep_row)],
        [HBM] * 5,
        8,
        [
            room(keep_row),
            pltpu.VMEM((count, width), F32),
            pltpu.VMEM((count, units), F32),
            pltpu.VMEM((count, units), F32),
            pltpu.SemaphoreType.DMA((8,)),
        ],
        name="forward_local",
        weight=LONG,
    )


def forward(ids, blocks, tokens, local_hidden, w_gate, w_up, w_down, chips, cores, part):
    n_blocks = len(blocks)
    size, width = blocks[0].shape
    count = n_blocks * size
    total = count + tokens.shape[0]
    units = w_gate.shape[1]
    f_tile, d_tile = tile_of(units, 256), tile_of(width, 512)

    def kernel(ids_ref, *refs):
        ins, refs = refs[:n_blocks], refs[n_blocks:]
        (tokens_ref, local_ref, gate_ref, up_ref, down_ref), refs = refs[:5], refs[5:]
        (out_hbm, rows_hbm, hidden_hbm, silu_hbm, factor_hbm), refs = refs[:5], refs[5:]
        sent, (out_ref, rows_ref, hidden_ref, silu_ref, factor_ref, sems) = refs[: chips - 1], refs[chips - 1 :]
        copies = Copies(sems)
        for i, ref in enumerate(ins):
            rows_ref[i * size : (i + 1) * size, :] = ref[...]
        rows_ref[count:, :] = tokens_ref[...]
        hidden_ref[count:, :] = local_ref[...]
        copies.start(rows_ref, rows_hbm, True)
        routed = pl.ds(0, count)
        hidden_units(
            rows_ref[:count, :], gate_ref, up_ref, hidden_ref.at[routed], silu_ref, factor_ref, f_tile
        )
        copies.start(hidden_ref, hidden_hbm, True)
        copies.start(silu_ref, silu_hbm, True)
        copies.start(factor_ref, factor_hbm, True)
        for n in range(0, width, d_tile):
            cols = pl.ds(n, d_tile)
            out_ref[:, cols] = dot(hidden_ref[:count, :], down_ref[:, cols]).astype(BF16)
            for k in range(n_blocks):
                target = out_hbm.at[pl.ds(home_of(ids_ref, k, n_blocks) * size, size), cols]
                copies.start(out_ref.at[pl.ds(k * size, size), cols], target, True)
        for shift, target in enumerate(sent, 1):
            target[...] = rows_ref[:, chip_columns(ids_ref, shift, chips, cores, part)]
        copies.finish()

    outs = call(
        kernel,
        [
            in_hbm((count, width), BF16),
            in_hbm((total, width), BF16),
            in_hbm((total, units), BF16),
            in_hbm((count, units), F32),
            in_hbm((count, units), F32),
        ]
        + [on_chip((total, cores * part), BF16)] * (chips - 1),
        [ids] + [pinned(array) for array in (*blocks, tokens, local_hidden, w_gate, w_up, w_down)],
        [SMEM] + [VMEM] * (n_blocks + 5),
        16,
        [
            pltpu.VMEM((count, width), BF16),
            pltpu.VMEM((total, width), BF16),
            pltpu.VMEM((total, units), BF16),
            pltpu.VMEM((count, units), F32),
            pltpu.VMEM((count, units), F32),
            pltpu.SemaphoreType.DMA((4 + n_blocks * (width // d_tile),)),
        ],
        name="forward",
    )
    return *outs[:5], list(outs[5:])


def mix(returned, place, pick, gates_t, keep_row, cotangent, local_out, n_blocks):
    slots, width = returned.shape
    choose, tok = gates_t.shape
    step = tile_of(width, 512)

    def kernel(returned_ref, *refs):
        sources, refs = refs[:6], refs[6:]
        outs, local_ref, refs = refs[:n_blocks], refs[n_blocks], refs[n_blocks + 1 :]
        targets, sems = refs[:6], refs[6]
        pick_ref, gates_ref, keep_ref, out_ref, cot_ref, place_ref = targets
        copies = Copies(sems)
        arriving = [copies.start(source, target) for source, target in zip(sources, targets)]
        for copy in arriving:
            copy.wait()
        gates = [column_of(gates_ref[k : k + 1, :]) for k in range(choose)]
        keep = column_of(keep_ref[...].astype(F32))
        for n in range(0, width, step):
            cols = pl.ds(n, step)
            picked = dot(pick_ref[...], returned_ref[:, cols])
            mixed = sum(gates[k] * picked[k * tok : (k + 1) * tok] for k in range(choose))
            difference = mixed - out_ref[:, cols]
            upstream = cot_ref[:, cols].astype(F32) + difference
            local_ref[:, cols] = (-(keep * difference)).astype(BF16)
            routed = jnp.concatenate([(gate * upstream).astype(BF16) for gate in gates], axis=0)
            split(dot(place_ref[...], routed).astype(BF16), outs, cols)

    brought = [pick, gates_t, keep_row, local_out, cotangent, place]
    outs = call(
        kernel,
        [on_chip((slots // n_blocks, width), BF16)] * n_blocks + [on_chip((tok, width), BF16)],
        [returned] + [held(array) for array in brought],
        [VMEM] + [HBM] * 6,
        10,
        [room(array) for array in brought] + [pltpu.SemaphoreType.DMA((6,))],
        name="mix",
    )
    return list(outs[:n_blocks]), outs[n_blocks]


def gradients(cots, silu_ref, factor_ref, down_ref, gate_back, up_back, f_tile):
    for j in range(0, gate_back.shape[1], f_tile):
        cols = pl.ds(j, f_tile)
        grad = dot_back(cots, down_ref[cols, :])
        gate_back[:, cols] = (grad * factor_ref[:, cols]).astype(BF16)
        up_back[:, cols] = (grad * silu_ref[:, cols]).astype(BF16)


def backward_local(ids, cots, silu, factor, w_gate, w_up, w_down, kept, chips, cores, part):
    count, width = cots.shape
    units = w_gate.shape[1]
    f_tile, d_tile = tile_of(units, 256), tile_of(width, 512)
    span = cores * part
    n_kept = len(kept)

    def kernel(ids_ref, cots_ref, silu_hbm, factor_hbm, gate_hbm, up_hbm, down_hbm, *refs):
        kept_hbm, (back_hbm, gate_ref, up_ref, down_ref), refs = refs[:n_kept], refs[n_kept : n_kept + 4], refs[n_kept + 4 :]
        kept_refs, sent, refs = refs[:n_kept], refs[n_kept : n_kept + chips], refs[n_kept + chips :]
        back_ref, silu_ref, factor_ref, gate_back, up_back, sems = refs
        copies = Copies(sems)
        first = [copies.start(s, t) for s, t in ((silu_hbm, silu_ref), (factor_hbm, factor_ref), (down_hbm, down_ref))]
        second = [copies.start(s, t) for s, t in ((gate_hbm, gate_ref), (up_hbm, up_ref))]
        for source, target in zip(kept_hbm, kept_refs):
            copies.start(source, target, True)
        for copy in first:
            copy.wait()
        gradients(cots_ref[...], silu_ref, factor_ref, down_ref, gate_back, up_back, f_tile)
        for shift, target in enumerate(sent):
            target[:, :span] = cots_ref[:, chip_columns(ids_ref, shift, chips, cores, part)]
            target[:, span : span + units] = gate_back[...]
            target[:, span + units :] = up_back[...]
        for copy in second:
            copy.wait()
        for n in range(0, width, d_tile):
            cols = pl.ds(n, d_tile)
            back = dot_back(gate_back[...], gate_ref[cols, :])
            back += dot_back(up_back[...], up_ref[cols, :])
            back_ref[:, cols] = back
        copies.start(back_ref, back_hbm, True)
        copies.finish()

    outs = call(
        kernel,
        [in_hbm((count, width), F32)]
        + [on_chip(array.shape, array.dtype) for array in (w_gate, w_up, w_down, *kept)]
        + [on_chip((count, span + 2 * units), BF16)] * chips,
        [ids, pinned(cots)] + [held(array) for array in (silu, factor, w_gate, w_up, w_down, *kept)],
        [SMEM, VMEM] + [HBM] * (5 + n_kept),
        10,
        [
            pltpu.VMEM((count, width), F32),
            room(silu),
            room(factor),
            pltpu.VMEM((count, units), BF16),
            pltpu.VMEM((count, units), BF16),
            pltpu.SemaphoreType.DMA((6 + n_kept,)),
        ],
        name="backward_local",
        weight=LONG,
    )
    return outs[0], outs[1:4], outs[4 : 4 + n_kept], list(outs[4 + n_kept :])


def collect(ids, blocks, chips, cores, part):
    n_blocks = len(blocks)
    size, width = blocks[0].shape
    count, span = n_blocks * size, cores * part

    def kernel(ids_ref, *refs):
        ins, rows_ref, sent, (sent_ref, sems) = refs[:n_blocks], refs[n_blocks], refs[n_blocks + 1 : -2], refs[-2:]
        copies = Copies(sems)
        for i, ref in enumerate(ins):
            rows_ref[i * size : (i + 1) * size, :] = ref[...]
            for shift in range(1, chips):
                sent_ref[shift - 1, i * size : (i + 1) * size, :] = ref[
                    :, chip_columns(ids_ref, shift, chips, cores, part)
                ]
        for shift, target in enumerate(sent):
            copies.start(sent_ref.at[shift], target, True)
        copies.finish()

    outs = call(
        kernel,
        [on_chip((count, width), BF16)] + [in_hbm((count, span), BF16)] * (chips - 1),
        [ids] + [pinned(block) for block in blocks],
        [SMEM] + [VMEM] * n_blocks,
        8,
        [pltpu.VMEM((max(chips - 1, 1), count, span), BF16), pltpu.SemaphoreType.DMA((max(chips - 1, 1),))],
        name="collect",
    )
    return outs[0], list(outs[1:])


def backward(ids, cots, silu, factor, w_gate, w_up, w_down, n_blocks):
    count, width = cots.shape
    units = w_gate.shape[1]
    size = count // n_blocks
    f_tile, d_tile = tile_of(units, 256), tile_of(width, 512)

    def kernel(ids_ref, cots_ref, silu_ref, factor_ref, gate_ref, up_ref, down_ref, *refs):
        back_hbm, gate_hbm, up_hbm, cots_hbm, back_ref, gate_back, up_back, sems = refs
        copies = Copies(sems)
        copies.start(cots_ref, cots_hbm, True)
        gradients(cots_ref[...], silu_ref, factor_ref, down_ref, gate_back, up_back, f_tile)
        copies.start(gate_back, gate_hbm, True)
        copies.start(up_back, up_hbm, True)
        for n in range(0, width, d_tile):
            cols = pl.ds(n, d_tile)
            back = dot_back(gate_back[...], gate_ref[cols, :])
            back += dot_back(up_back[...], up_ref[cols, :])
            back_ref[:, cols] = back.astype(BF16)
            for k in range(n_blocks):
                target = back_hbm.at[pl.ds(home_of(ids_ref, k, n_blocks) * size, size), cols]
                copies.start(back_ref.at[pl.ds(k * size, size), cols], target, True)
        copies.finish()

    return call(
        kernel,
        [
            in_hbm((count, width), BF16),
            in_hbm((count, units), BF16),
            in_hbm((count, units), BF16),
            in_hbm((count, width), BF16),
        ],
        [ids] + [pinned(array) for array in (cots, silu, factor, w_gate, w_up, w_down)],
        [SMEM] + [VMEM] * 6,
        10,
        [
            pltpu.VMEM((count, width), BF16),
            pltpu.VMEM((count, units), BF16),
            pltpu.VMEM((count, units), BF16),
            pltpu.SemaphoreType.DMA((3 + n_blocks * (width // d_tile),)),
        ],
        name="backward",
        weight=LONG,
    )


WHOLE, CHIP = -1, -2


def weight_sums(ids, cores, part, terms, previous, units, sections, scale):
    step = tile_of(units, 256)
    begun = [] if previous is None else [previous]
    arrays = []
    for left, right, *_ in terms:
        for array, _ in left + right:
            arrays += [] if any(array is other for other in arrays) else [array]
    where = lambda array: next(i for i, other in enumerate(arrays) if other is array)
    rows_of = [sum(array.shape[0] for array, _ in left) for left, *_ in terms]
    n_copies = sum(len(left) + len(right) for left, right, *_ in terms)

    def kernel(ids_ref, *refs):
        sources, refs = refs[: len(arrays)], refs[len(arrays) :]
        begun_hbm, out_hbm, refs = refs[: len(begun)], refs[len(begun)], refs[len(begun) + 1 :]
        lefts, rights, out_ref, sems = refs[: len(terms)], refs[len(terms) : 2 * len(terms)], refs[-2], refs[-1]
        copies = Copies(sems)
        at_whole, at_chip, _ = place_of(ids_ref, cores, part)

        def bring(pieces, target, columns):
            row, started = 0, []
            for array, first in pieces:
                first = aligned(at_whole if first == WHOLE else at_chip) if first < 0 else first
                count = array.shape[0]
                source = sources[where(array)].at[:, pl.ds(first, columns)]
                started.append(copies.start(source, target.at[pl.ds(row, count), :]))
                row += count
            return started

        arriving = []
        for (left, right, _, wide), left_ref, right_ref in zip(terms, lefts, rights):
            arriving += bring(left, left_ref, part) + bring(right, right_ref, wide * units)
        for source in begun_hbm:
            for section in sections:
                cols = pl.ds(section * units, units)
                arriving.append(copies.start(source.at[:, cols], out_ref.at[:, cols]))
        for copy in arriving:
            copy.wait()
        for section in sections:
            for at in range(0, units, step):
                cols = pl.ds(section * units + at, step)
                total = out_ref[:, cols] if begun else None
                for i, (_, _, first, wide) in enumerate(terms):
                    if first <= section < first + wide:
                        begin = (section - first) * units + at
                        term = dot_rows(lefts[i][...], rights[i][:, begin : begin + step])
                        total = term if total is None else total + term
                out_ref[:, cols] = total if scale is None else total * scale
                copies.start(out_ref.at[:, cols], out_hbm.at[:, cols], True)
        copies.finish()

    operands = [ids] + [held(array) for array in (*arrays, *begun)]
    (out,) = call(
        kernel,
        [in_hbm((part, 3 * units), F32)],
        operands,
        [SMEM] + [HBM] * (len(operands) - 1),
        20,
        [pltpu.VMEM((rows, part), BF16) for rows in rows_of]
        + [pltpu.VMEM((rows, wide * units), BF16) for rows, (*_, wide) in zip(rows_of, terms)]
        + [
            pltpu.VMEM((part, 3 * units), F32),
            pltpu.SemaphoreType.DMA((n_copies + len(begun) * len(sections) + len(sections) * (units // step),)),
        ],
        name="weight_sums",
        weight=0,
        aliases={len(operands) - 1: 0} if begun else None,
    )
    return out


def combine(returned, pick, local_back, choose):
    slots, width = returned.shape
    tok = local_back.shape[0]
    step = tile_of(width, 512)

    def kernel(returned_ref, pick_hbm, local_hbm, out_hbm, pick_ref, local_ref, out_ref, sems):
        copies = Copies(sems)
        pick_in = copies.start(pick_hbm, pick_ref)
        local_in = copies.start(local_hbm, local_ref)
        pick_in.wait()
        local_in.wait()
        both = sum(pick_ref[k * tok : (k + 1) * tok, :].astype(F32) for k in range(choose)).astype(BF16)
        for n in range(0, width, step):
            cols = pl.ds(n, step)
            out_ref[:, cols] = (dot(both, returned_ref[:, cols]) + local_ref[:, cols]).astype(BF16)
            copies.start(out_ref.at[:, cols], out_hbm.at[:, cols], True)
        copies.finish()

    (out,) = call(
        kernel,
        [in_hbm((tok, width), BF16)],
        [returned, held(pick), held(local_back)],
        [VMEM, HBM, HBM],
        8,
        [
            room(pick),
            room(local_back),
            pltpu.VMEM((tok, width), BF16),
            pltpu.SemaphoreType.DMA((2 + width // step,)),
        ],
        name="combine",
    )
    return out


def on_device(tokens, routes, gates, keep, cotangent, w_gate, w_up, w_down):
    groups = lax.axis_size("expert")
    replicas = lax.axis_size("dp")
    tok_count, width = tokens.shape
    choose = routes.shape[1]
    capacity = 3 * tok_count * choose // (2 * groups)
    slots = groups * capacity
    apart = capacity % 16 == 0 and groups <= 8
    n_blocks = groups if apart else 1
    cores = 2 if replicas % 2 == 0 else 1
    chips = replicas // cores
    part = width // replicas
    span = cores * part
    units = w_gate.shape[2]
    weights = (w_gate[0], w_up[0], w_down[0])
    siblings = [(i, i ^ 1) for i in range(replicas)]
    first = lax.axis_index("expert") if apart else 0
    ids = jnp.stack([jnp.asarray(first, jnp.int32), lax.axis_index("dp").astype(jnp.int32)])
    keep_row = keep[None]
    together = lax.optimization_barrier
    far_first = sorted(range(1, groups), key=lambda k: abs(k - groups / 2))

    def at_once(block):
        block = block.reshape(groups, capacity, -1)
        moved = lax.all_to_all(block, "expert", split_axis=0, concat_axis=0, tiled=True)
        return moved.reshape(slots, -1)

    def step_by_step(blocks):
        if not apart:
            return [at_once(blocks[0])]
        moved = [blocks[0]] + [None] * (groups - 1)
        for k in far_first:
            moved[k] = lax.ppermute(blocks[k], "expert", [(i, (i + k) % groups) for i in range(groups)])
        return moved

    def to_chips(arrays):
        return [
            lax.ppermute(
                array,
                "dp",
                [
                    (start * cores + i, (start + shift) % chips * cores + i)
                    for start in range(chips)
                    for i in range(cores)
                ],
            )
            for shift, array in enumerate(arrays, 1)
        ]

    def from_sibling(arrays):
        return [lax.ppermute(array, "dp", siblings) for array in arrays] if cores == 2 else []

    def to_others(array):
        return to_chips([array] * (chips - 1))

    blocks, place, pick = dispatch(ids, tokens, routes.T, groups, capacity, n_blocks)
    blocks = step_by_step(blocks)
    local_out, local_silu, local_factor, local_hidden, tokens_on, *on = forward_local(tokens, *weights, keep_row)
    out, rows, hidden, silu, factor, x_send = forward(
        ids, blocks, tokens_on, local_hidden, *on, chips, cores, part
    )
    returned = at_once(out)
    x_far = to_chips(x_send)
    h_far = to_others(hidden)
    returned, x_far = together((returned, x_far))
    blocks, local_cot = mix(returned, place, pick, gates.T, keep_row, cotangent, local_out, n_blocks)
    blocks = step_by_step(blocks)
    local_cot, h_far = together((local_cot, h_far))
    local_back, on, kept, l_send = backward_local(
        ids, local_cot, local_silu, local_factor, *weights, (silu, factor), chips, cores, part
    )
    l_own, l_far = l_send[0], to_chips(l_send[1:])
    cots, c_send = collect(ids, blocks, chips, cores, part)
    back, gate_back, up_back, cots = backward(ids, cots, *kept, *on, n_blocks)
    returned = at_once(back)
    c_send, l_far = together((c_send, l_far))
    c_far = to_chips(c_send)
    gate_back, c_far = together((gate_back, c_far))
    g_far = to_others(gate_back)

    def terms_x(xs, at, rights, ls, section):
        return [
            ([(x, at)], [(right, 0), (l, span + section * units)], section, 1)
            for x, right, l in zip(xs, rights, ls)
        ]

    def terms_c(cs, at, ls, hs):
        return [([(c, at), (l, CHIP)], [(h, 0)], 2, 1) for c, l, h in zip(cs, ls, hs)]

    def both_cores(arrays):
        return arrays + from_sibling(arrays)

    x_near, h_near, l_near = both_cores([rows]), both_cores([hidden]), both_cores([l_own])
    g_near, u_near, c_near = both_cores([gate_back]), both_cores([up_back]), both_cores([cots])
    scale = 1.0 / replicas
    token_grads = combine(returned, pick, local_back, choose)
    totals = weight_sums(
        ids,
        cores,
        part,
        terms_x(x_near, WHOLE, g_near, l_near, 0)
        + terms_x(x_near, WHOLE, u_near, l_near, 1)
        + terms_c(c_near, WHOLE, l_near, h_near),
        None,
        units,
        (0, 1, 2),
        None if chips > 1 else scale,
    )
    if chips > 1:
        up_back, g_far, totals = together((up_back, g_far, totals))
        u_far = to_others(up_back)
        x_far, h_far, l_far = both_cores(x_far), both_cores(h_far), both_cores(l_far)
        c_far, g_far = both_cores(c_far), both_cores(g_far)
        totals = weight_sums(
            ids,
            cores,
            part,
            terms_x(x_far, CHIP, g_far, l_far, 0) + terms_c(c_far, CHIP, l_far, h_far),
            totals,
            units,
            (2, 0),
            scale,
        )
        u_far, totals, token_grads = together((u_far, totals, token_grads))
        u_far = both_cores(u_far)
        totals = weight_sums(
            ids, cores, part, terms_x(x_far, CHIP, u_far, l_far, 1), totals, units, (1,), scale
        )
    return (token_grads, totals[None])


def solution(mesh):
    return jax.shard_map(
        on_device,
        mesh=mesh,
        in_specs=(
            P(("dp", "expert"), None),
            P(("dp", "expert"), None),
            P(("dp", "expert"), None),
            P(("dp", "expert")),
            P(("dp", "expert"), None),
            P("expert", None, None),
            P("expert", None, None),
            P("expert", None, None),
        ),
        out_specs=(P(("dp", "expert"), None), P("expert", "dp", None)),
        check_vma=False,
    )
```

```python
import jax
import jax.numpy as jnp
from jax import lax
from jax.experimental import pallas as pl
from jax.experimental.pallas import tpu as pltpu
from jax.sharding import PartitionSpec as P

F32 = jnp.float32
BF16 = jnp.bfloat16
MIB = 1 << 20
LONG = 20_000_000_000
BACK = 2_000_000_000
SUMS = 5_000_000_000
LATE = True
LATE_ONES = (6, 1)
VMEM = pl.BlockSpec(memory_space=pltpu.VMEM)
SMEM = pl.BlockSpec(memory_space=pltpu.SMEM)
HBM = pl.BlockSpec(memory_space=pltpu.HBM)


def logistic_parts(act):
    sigma = jax.nn.sigmoid(act)
    return (act * sigma, sigma * (1.0 + act * (1.0 - sigma)))


def dot(left, right):
    return jnp.dot(left, right, preferred_element_type=F32)


def dot_rows(left, right):
    return lax.dot_general(left, right, (((0,), (0,)), ((), ())), preferred_element_type=F32)


def dot_back(left, weight):
    return lax.dot_general(left, weight, (((1,), (1,)), ((), ())), preferred_element_type=F32)


def tile_of(size, most):
    tile = most
    while size % tile:
        tile //= 2
    return tile


def held(array):
    return pltpu.with_memory_space_constraint(array, pltpu.HBM)


def pinned(array):
    return pltpu.with_memory_space_constraint(array, pltpu.VMEM)


def room(array):
    return pltpu.VMEM(array.shape, array.dtype)


def on_chip(dims, kind):
    return pltpu.VMEM(tuple(dims), kind)


def in_hbm(dims, kind):
    return pltpu.HBM(tuple(dims), kind)


def call(kernel, outs, operands, specs, limit, scratch=(), name=None, aliases=None, weight=0):
    return pl.pallas_call(
        kernel,
        out_shape=tuple(outs),
        in_specs=specs,
        out_specs=tuple(HBM if out.memory_space == pltpu.HBM else VMEM for out in outs),
        scratch_shapes=list(scratch),
        input_output_aliases=aliases or {},
        compiler_params=pltpu.CompilerParams(vmem_limit_bytes=limit * MIB),
        cost_estimate=pl.CostEstimate(flops=weight, bytes_accessed=0, transcendentals=0),
        name=name,
    )(*operands)


class Copies:
    def __init__(self, sems):
        self.sems, self.count, self.waiting = sems, 0, []

    def start(self, source, target, keep=False):
        copy = pltpu.make_async_copy(source, target, self.sems.at[self.count])
        self.count += 1
        copy.start()
        if keep:
            self.waiting.append(copy)
        return copy

    def finish(self):
        for copy in self.waiting:
            copy.wait()


def split(array, refs, cols):
    size = refs[0].shape[0]
    for i, ref in enumerate(refs):
        ref[:, cols] = array[i * size : (i + 1) * size]


def joined_rows(refs, cols):
    return jnp.concatenate([ref[:, cols] for ref in refs], axis=0) if len(refs) > 1 else refs[0][:, cols]


def place_of(ids_ref, cores, part):
    device = ids_ref[1]
    chip = device // cores
    return device * part, (device - chip * cores) * part, chip


def aligned(begin):
    return pl.multiple_of(begin, 128)


def chip_columns(ids_ref, shift, chips, cores, part):
    _, _, chip = place_of(ids_ref, cores, part)
    other = chip + shift
    return pl.ds(aligned(jnp.where(other >= chips, other - chips, other) * (cores * part)), cores * part)


def home_of(ids_ref, k, n_blocks):
    place = ids_ref[0] - k
    return jnp.where(place < 0, place + n_blocks, place) if n_blocks > 1 else 0


def column_of(row):
    count = row.shape[1]
    same = lax.broadcasted_iota(jnp.int32, (count, count), 0) == lax.broadcasted_iota(
        jnp.int32, (count, count), 1
    )
    return jnp.sum(jnp.where(same, row, 0.0), axis=1, keepdims=True)


def dispatch(ids, tokens, routes_t, groups, capacity, n_blocks):
    tok, width = tokens.shape
    choose = routes_t.shape[0]
    slots = groups * capacity
    pairs = choose * tok
    step = tile_of(width, 512)

    def kernel(ids_ref, tokens_hbm, routes_hbm, *refs):
        blocks, (place_hbm, pick_hbm, place_ref, pick_ref, tokens_ref, routes_ref, sems) = refs[:n_blocks], refs[n_blocks:]
        copies = Copies(sems)
        routes_in = copies.start(routes_hbm, routes_ref)
        tokens_in = copies.start(tokens_hbm, tokens_ref)
        routes_in.wait()
        chosen = routes_ref[...]
        near = chosen - ids_ref[0]
        near = jnp.where(near < 0, near + groups, near)
        expert_ids = lax.broadcasted_iota(jnp.int32, (groups, tok), 0)
        member = jnp.zeros((groups, tok), F32)
        for k in range(choose):
            member += (chosen[k : k + 1, :] == expert_ids).astype(F32)
        upper = lax.broadcasted_iota(jnp.int32, (tok, tok), 0) < lax.broadcasted_iota(
            jnp.int32, (tok, tok), 1
        )
        before = dot(member.astype(BF16), upper.astype(F32).astype(BF16))
        slot_ids = lax.broadcasted_iota(jnp.int32, (slots, tok), 0)
        both = jnp.zeros((slots, tok), F32)
        for k in range(choose):
            mine = chosen[k : k + 1, :]
            slot = jnp.sum(jnp.where(mine == expert_ids, before, 0.0), axis=0, keepdims=True).astype(jnp.int32)
            hit = (slot_ids == near[k : k + 1, :] * capacity + slot).astype(F32)
            place_ref[:, k * tok : (k + 1) * tok] = hit.astype(BF16)
            both += hit
            hit = (slot_ids == mine * capacity + slot).astype(F32)
            pick_ref[k * tok : (k + 1) * tok, :] = hit.T.astype(BF16)
        copies.start(place_ref, place_hbm, True)
        copies.start(pick_ref, pick_hbm, True)
        both = both.astype(BF16)
        tokens_in.wait()
        for n in range(0, width, step):
            cols = pl.ds(n, step)
            split(dot(both, tokens_ref[:, cols]).astype(BF16), blocks, cols)
        copies.finish()

    outs = call(
        kernel,
        [on_chip((slots // n_blocks, width), BF16)] * n_blocks
        + [in_hbm((slots, pairs), BF16), in_hbm((pairs, slots), BF16)],
        [ids, held(tokens), held(routes_t)],
        [SMEM, HBM, HBM],
        8,
        [
            pltpu.VMEM((slots, pairs), BF16),
            pltpu.VMEM((pairs, slots), BF16),
            room(tokens),
            room(routes_t),
            pltpu.SemaphoreType.DMA((4,)),
        ],
        name="dispatch",
    )
    return list(outs[:n_blocks]), *outs[n_blocks:]


def hidden_units(rows, gate_ref, up_ref, hidden_ref, silu_ref, factor_ref, f_tile):
    for j in range(0, gate_ref.shape[1], f_tile):
        cols = pl.ds(j, f_tile)
        gate = dot(rows, gate_ref[:, cols])
        up = dot(rows, up_ref[:, cols])
        silu, slope = logistic_parts(gate)
        silu_ref[:, cols] = silu
        factor_ref[:, cols] = up * slope
        hidden_ref[:, cols] = (silu * up).astype(BF16)


def forward_local(tokens, w_gate, w_up, w_down, keep_row):
    count, width = tokens.shape
    units = w_gate.shape[1]
    f_tile, d_tile = tile_of(units, 256), tile_of(width, 512)

    def kernel(tokens_hbm, gate_hbm, up_hbm, down_hbm, keep_hbm, *refs):
        out_hbm, silu_hbm, factor_hbm, hidden_ref, tokens_ref, gate_ref, up_ref, down_ref = refs[:8]
        keep_ref, out_ref, silu_ref, factor_ref, sems = refs[8:]
        copies = Copies(sems)
        arriving = [
            copies.start(source, target)
            for source, target in (
                (tokens_hbm, tokens_ref),
                (keep_hbm, keep_ref),
                (gate_hbm, gate_ref),
                (up_hbm, up_ref),
                (down_hbm, down_ref),
            )
        ]
        for copy in arriving[:4]:
            copy.wait()
        hidden_units(tokens_ref[...], gate_ref, up_ref, hidden_ref, silu_ref, factor_ref, f_tile)
        copies.start(silu_ref, silu_hbm, True)
        copies.start(factor_ref, factor_hbm, True)
        keep = column_of(keep_ref[...].astype(F32))
        arriving[4].wait()
        for n in range(0, width, d_tile):
            cols = pl.ds(n, d_tile)
            out_ref[:, cols] = keep * dot(hidden_ref[...], down_ref[:, cols])
        copies.start(out_ref, out_hbm, True)
        copies.finish()

    return call(
        kernel,
        [
            in_hbm((count, width), F32),
            in_hbm((count, units), F32),
            in_hbm((count, units), F32),
            on_chip((count, units), BF16),
            on_chip((count, width), BF16),
            on_chip(w_gate.shape, BF16),
            on_chip(w_up.shape, BF16),
            on_chip(w_down.shape, BF16),
        ],
        [held(array) for array in (tokens, w_gate, w_up, w_down, keep_row)],
        [HBM] * 5,
        8,
        [
            room(keep_row),
            pltpu.VMEM((count, width), F32),
            pltpu.VMEM((count, units), F32),
            pltpu.VMEM((count, units), F32),
            pltpu.SemaphoreType.DMA((8,)),
        ],
        name="forward_local",
        weight=LONG,
    )


def forward(ids, blocks, tokens, local_hidden, w_gate, w_up, w_down, chips, cores, part):
    n_blocks = len(blocks)
    size, width = blocks[0].shape
    count = n_blocks * size
    total = count + tokens.shape[0]
    units = w_gate.shape[1]
    f_tile, d_tile = tile_of(units, 256), tile_of(width, 512)

    def kernel(ids_ref, *refs):
        ins, refs = refs[:n_blocks], refs[n_blocks:]
        (tokens_ref, local_ref, gate_ref, up_ref, down_ref), refs = refs[:5], refs[5:]
        (out_hbm, rows_hbm, hidden_hbm, silu_hbm, factor_hbm), refs = refs[:5], refs[5:]
        sent, (out_ref, rows_ref, hidden_ref, silu_ref, factor_ref, sems) = refs[: chips - 1], refs[chips - 1 :]
        copies = Copies(sems)
        for i, ref in enumerate(ins):
            rows_ref[i * size : (i + 1) * size, :] = ref[...]
        rows_ref[count:, :] = tokens_ref[...]
        hidden_ref[count:, :] = local_ref[...]
        copies.start(rows_ref, rows_hbm, True)
        routed = pl.ds(0, count)
        hidden_units(
            rows_ref[:count, :], gate_ref, up_ref, hidden_ref.at[routed], silu_ref, factor_ref, f_tile
        )
        copies.start(hidden_ref, hidden_hbm, True)
        copies.start(silu_ref, silu_hbm, True)
        copies.start(factor_ref, factor_hbm, True)
        for n in range(0, width, d_tile):
            cols = pl.ds(n, d_tile)
            out_ref[:, cols] = dot(hidden_ref[:count, :], down_ref[:, cols]).astype(BF16)
            for k in range(n_blocks):
                target = out_hbm.at[pl.ds(home_of(ids_ref, k, n_blocks) * size, size), cols]
                copies.start(out_ref.at[pl.ds(k * size, size), cols], target, True)
        for shift, target in enumerate(sent, 1):
            target[...] = rows_ref[:, chip_columns(ids_ref, shift, chips, cores, part)]
        copies.finish()

    outs = call(
        kernel,
        [
            in_hbm((count, width), BF16),
            in_hbm((total, width), BF16),
            in_hbm((total, units), BF16),
            in_hbm((count, units), F32),
            in_hbm((count, units), F32),
        ]
        + [on_chip((total, cores * part), BF16)] * (chips - 1),
        [ids] + [pinned(array) for array in (*blocks, tokens, local_hidden, w_gate, w_up, w_down)],
        [SMEM] + [VMEM] * (n_blocks + 5),
        16,
        [
            pltpu.VMEM((count, width), BF16),
            pltpu.VMEM((total, width), BF16),
            pltpu.VMEM((total, units), BF16),
            pltpu.VMEM((count, units), F32),
            pltpu.VMEM((count, units), F32),
            pltpu.SemaphoreType.DMA((4 + n_blocks * (width // d_tile),)),
        ],
        name="forward",
    )
    return *outs[:5], list(outs[5:])


def mix(returned, place, pick, gates_t, keep_row, cotangent, local_out, n_blocks):
    slots, width = returned.shape
    choose, tok = gates_t.shape
    step = tile_of(width, 512)

    def kernel(returned_ref, *refs):
        sources, refs = refs[:6], refs[6:]
        outs, local_ref, refs = refs[:n_blocks], refs[n_blocks], refs[n_blocks + 1 :]
        targets, sems = refs[:6], refs[6]
        pick_ref, gates_ref, keep_ref, out_ref, cot_ref, place_ref = targets
        copies = Copies(sems)
        arriving = [copies.start(source, target) for source, target in zip(sources, targets)]
        for copy in arriving:
            copy.wait()
        gates = [column_of(gates_ref[k : k + 1, :]) for k in range(choose)]
        keep = column_of(keep_ref[...].astype(F32))
        for n in range(0, width, step):
            cols = pl.ds(n, step)
            picked = dot(pick_ref[...], returned_ref[:, cols])
            mixed = sum(gates[k] * picked[k * tok : (k + 1) * tok] for k in range(choose))
            difference = mixed - out_ref[:, cols]
            upstream = cot_ref[:, cols].astype(F32) + difference
            local_ref[:, cols] = (-(keep * difference)).astype(BF16)
            routed = jnp.concatenate([(gate * upstream).astype(BF16) for gate in gates], axis=0)
            split(dot(place_ref[...], routed).astype(BF16), outs, cols)

    brought = [pick, gates_t, keep_row, local_out, cotangent, place]
    outs = call(
        kernel,
        [on_chip((slots // n_blocks, width), BF16)] * n_blocks + [on_chip((tok, width), BF16)],
        [returned] + [held(array) for array in brought],
        [VMEM] + [HBM] * 6,
        10,
        [room(array) for array in brought] + [pltpu.SemaphoreType.DMA((6,))],
        name="mix",
    )
    return list(outs[:n_blocks]), outs[n_blocks]


def gradients(cots, silu_ref, factor_ref, down_ref, gate_back, up_back, f_tile):
    for j in range(0, gate_back.shape[1], f_tile):
        cols = pl.ds(j, f_tile)
        grad = dot_back(cots, down_ref[cols, :])
        gate_back[:, cols] = (grad * factor_ref[:, cols]).astype(BF16)
        up_back[:, cols] = (grad * silu_ref[:, cols]).astype(BF16)


def backward_local(ids, cots, silu, factor, w_gate, w_up, w_down, kept, chips, cores, part):
    count, width = cots.shape
    units = w_gate.shape[1]
    f_tile, d_tile = tile_of(units, 256), tile_of(width, 512)
    span = cores * part
    n_kept = len(kept)

    def kernel(ids_ref, cots_ref, silu_hbm, factor_hbm, gate_hbm, up_hbm, down_hbm, *refs):
        kept_hbm, (back_hbm, gate_ref, up_ref, down_ref), refs = refs[:n_kept], refs[n_kept : n_kept + 4], refs[n_kept + 4 :]
        kept_refs, sent, refs = refs[:n_kept], refs[n_kept : n_kept + chips], refs[n_kept + chips :]
        back_ref, silu_ref, factor_ref, gate_back, up_back, sems = refs
        copies = Copies(sems)
        first = [copies.start(s, t) for s, t in ((silu_hbm, silu_ref), (factor_hbm, factor_ref), (down_hbm, down_ref))]
        second = [copies.start(s, t) for s, t in ((gate_hbm, gate_ref), (up_hbm, up_ref))]
        for source, target in zip(kept_hbm, kept_refs):
            copies.start(source, target, True)
        for copy in first:
            copy.wait()
        gradients(cots_ref[...], silu_ref, factor_ref, down_ref, gate_back, up_back, f_tile)
        for shift, target in enumerate(sent):
            target[:, :span] = cots_ref[:, chip_columns(ids_ref, shift, chips, cores, part)]
            target[:, span : span + units] = gate_back[...]
            target[:, span + units :] = up_back[...]
        for copy in second:
            copy.wait()
        for n in range(0, width, d_tile):
            cols = pl.ds(n, d_tile)
            back = dot_back(gate_back[...], gate_ref[cols, :])
            back += dot_back(up_back[...], up_ref[cols, :])
            back_ref[:, cols] = back
        copies.start(back_ref, back_hbm, True)
        copies.finish()

    outs = call(
        kernel,
        [in_hbm((count, width), F32)]
        + [on_chip(array.shape, array.dtype) for array in (w_gate, w_up, w_down, *kept)]
        + [on_chip((count, span + 2 * units), BF16)] * chips,
        [ids, pinned(cots)] + [held(array) for array in (silu, factor, w_gate, w_up, w_down, *kept)],
        [SMEM, VMEM] + [HBM] * (5 + n_kept),
        10,
        [
            pltpu.VMEM((count, width), F32),
            room(silu),
            room(factor),
            pltpu.VMEM((count, units), BF16),
            pltpu.VMEM((count, units), BF16),
            pltpu.SemaphoreType.DMA((6 + n_kept,)),
        ],
        name="backward_local",
        weight=LONG,
    )
    return outs[0], outs[1:4], outs[4 : 4 + n_kept], list(outs[4 + n_kept :])


def cut(ids, blocks, chips, cores, part):
    n_blocks = len(blocks)
    size, width = blocks[0].shape
    count, span = n_blocks * size, cores * part
    if chips == 1:
        return []

    def kernel(ids_ref, *refs):
        ins, sent, (sent_ref, sems) = refs[:n_blocks], refs[n_blocks:-2], refs[-2:]
        copies = Copies(sems)
        for shift, target in enumerate(sent, 1):
            for i, ref in enumerate(ins):
                columns = chip_columns(ids_ref, shift, chips, cores, part)
                sent_ref[shift - 1, i * size : (i + 1) * size, :] = ref[:, columns]
            copies.start(sent_ref.at[shift - 1], target, True)
        copies.finish()

    return list(
        call(
            kernel,
            [in_hbm((count, span), BF16)] * (chips - 1),
            [ids] + [pinned(block) for block in blocks],
            [SMEM] + [VMEM] * n_blocks,
            8,
            [pltpu.VMEM((chips - 1, count, span), BF16), pltpu.SemaphoreType.DMA((chips - 1,))],
            name="cut",
        )
    )


def backward(ids, blocks, silu, factor, w_gate, w_up, w_down):
    n_blocks = len(blocks)
    size, width = blocks[0].shape
    count = n_blocks * size
    units = w_gate.shape[1]
    f_tile, d_tile = tile_of(units, 256), tile_of(width, 512)

    def kernel(ids_ref, *refs):
        ins, refs = refs[:n_blocks], refs[n_blocks:]
        silu_ref, factor_ref, gate_ref, up_ref, down_ref, back_hbm, gate_hbm, up_hbm, cots_hbm = refs[:9]
        cots_ref, back_ref, gate_back, up_back, sems = refs[9:]
        copies = Copies(sems)
        for i, ref in enumerate(ins):
            cots_ref[i * size : (i + 1) * size, :] = ref[...]
        copies.start(cots_ref, cots_hbm, True)
        gradients(cots_ref[...], silu_ref, factor_ref, down_ref, gate_back, up_back, f_tile)
        copies.start(gate_back, gate_hbm, True)
        copies.start(up_back, up_hbm, True)
        for n in range(0, width, d_tile):
            cols = pl.ds(n, d_tile)
            back = dot_back(gate_back[...], gate_ref[cols, :])
            back += dot_back(up_back[...], up_ref[cols, :])
            back_ref[:, cols] = back.astype(BF16)
            for k in range(n_blocks):
                target = back_hbm.at[pl.ds(home_of(ids_ref, k, n_blocks) * size, size), cols]
                copies.start(back_ref.at[pl.ds(k * size, size), cols], target, True)
        copies.finish()

    return call(
        kernel,
        [
            in_hbm((count, width), BF16),
            in_hbm((count, units), BF16),
            in_hbm((count, units), BF16),
            in_hbm((count, width), BF16),
        ],
        [ids] + [pinned(array) for array in (*blocks, silu, factor, w_gate, w_up, w_down)],
        [SMEM] + [VMEM] * (n_blocks + 5),
        12,
        [
            pltpu.VMEM((count, width), BF16),
            pltpu.VMEM((count, width), BF16),
            pltpu.VMEM((count, units), BF16),
            pltpu.VMEM((count, units), BF16),
            pltpu.SemaphoreType.DMA((3 + n_blocks * (width // d_tile),)),
        ],
        name="backward",
        weight=BACK,
    )


WHOLE, CHIP = -1, -2


def weight_sums(ids, cores, part, terms, previous, units, sections, scale, at_hand=()):
    step = tile_of(units, 256)
    begun = [] if previous is None else [previous]
    arrays = []
    for left, right, *_ in terms:
        for array, _ in left + right:
            arrays += [] if any(array is other for other in arrays) else [array]
    where = lambda array: next(i for i, other in enumerate(arrays) if other is array)
    rows_of = [sum(array.shape[0] for array, _ in left) for left, *_ in terms]
    n_copies = sum(len(left) + len(right) for left, right, *_ in terms)

    def kernel(ids_ref, *refs):
        sources, refs = refs[: len(arrays)], refs[len(arrays) :]
        begun_hbm, out_hbm, refs = refs[: len(begun)], refs[len(begun)], refs[len(begun) + 1 :]
        lefts, rights, out_ref, sems = refs[: len(terms)], refs[len(terms) : 2 * len(terms)], refs[-2], refs[-1]
        copies = Copies(sems)
        at_whole, at_chip, _ = place_of(ids_ref, cores, part)

        def bring(pieces, target, columns):
            row, started = 0, []
            for array, first in pieces:
                first = aligned(at_whole if first == WHOLE else at_chip) if first < 0 else first
                count = array.shape[0]
                source = sources[where(array)].at[:, pl.ds(first, columns)]
                started.append(copies.start(source, target.at[pl.ds(row, count), :]))
                row += count
            return started

        arriving = []
        for (left, right, _, wide), left_ref, right_ref in zip(terms, lefts, rights):
            arriving += bring(left, left_ref, part) + bring(right, right_ref, wide * units)
        for source in begun_hbm:
            for section in sections:
                cols = pl.ds(section * units, units)
                arriving.append(copies.start(source.at[:, cols], out_ref.at[:, cols]))
        for copy in arriving:
            copy.wait()
        for section in sections:
            for at in range(0, units, step):
                cols = pl.ds(section * units + at, step)
                total = out_ref[:, cols] if begun else None
                for i, (_, _, first, wide) in enumerate(terms):
                    if first <= section < first + wide:
                        begin = (section - first) * units + at
                        term = dot_rows(lefts[i][...], rights[i][:, begin : begin + step])
                        total = term if total is None else total + term
                out_ref[:, cols] = total if scale is None else total * scale
                copies.start(out_ref.at[:, cols], out_hbm.at[:, cols], True)
        copies.finish()

    here = [any(array is other for other in at_hand) for array in (*arrays, *begun)]
    operands = [ids] + [pinned(a) if on else held(a) for a, on in zip((*arrays, *begun), here)]
    (out,) = call(
        kernel,
        [in_hbm((part, 3 * units), F32)],
        operands,
        [SMEM] + [VMEM if on else HBM for on in here],
        20,
        [pltpu.VMEM((rows, part), BF16) for rows in rows_of]
        + [pltpu.VMEM((rows, wide * units), BF16) for rows, (*_, wide) in zip(rows_of, terms)]
        + [
            pltpu.VMEM((part, 3 * units), F32),
            pltpu.SemaphoreType.DMA((n_copies + len(begun) * len(sections) + len(sections) * (units // step),)),
        ],
        name="weight_sums",
        weight=SUMS if len(sections) > 1 else 0,
        aliases={len(operands) - 1: 0} if begun else None,
    )
    return out


def combine(returned, pick, local_back, choose):
    slots, width = returned.shape
    tok = local_back.shape[0]
    step = tile_of(width, 512)

    def kernel(returned_ref, pick_hbm, local_hbm, out_hbm, pick_ref, local_ref, out_ref, sems):
        copies = Copies(sems)
        pick_in = copies.start(pick_hbm, pick_ref)
        local_in = copies.start(local_hbm, local_ref)
        pick_in.wait()
        local_in.wait()
        both = sum(pick_ref[k * tok : (k + 1) * tok, :].astype(F32) for k in range(choose)).astype(BF16)
        for n in range(0, width, step):
            cols = pl.ds(n, step)
            out_ref[:, cols] = (dot(both, returned_ref[:, cols]) + local_ref[:, cols]).astype(BF16)
            copies.start(out_ref.at[:, cols], out_hbm.at[:, cols], True)
        copies.finish()

    (out,) = call(
        kernel,
        [in_hbm((tok, width), BF16)],
        [returned, held(pick), held(local_back)],
        [VMEM, HBM, HBM],
        8,
        [
            room(pick),
            room(local_back),
            pltpu.VMEM((tok, width), BF16),
            pltpu.SemaphoreType.DMA((2 + width // step,)),
        ],
        name="combine",
    )
    return out


def on_device(tokens, routes, gates, keep, cotangent, w_gate, w_up, w_down):
    groups = lax.axis_size("expert")
    replicas = lax.axis_size("dp")
    tok_count, width = tokens.shape
    choose = routes.shape[1]
    capacity = 3 * tok_count * choose // (2 * groups)
    slots = groups * capacity
    apart = capacity % 16 == 0 and groups <= 8
    n_blocks = groups if apart else 1
    cores = 2 if replicas % 2 == 0 else 1
    chips = replicas // cores
    part = width // replicas
    span = cores * part
    units = w_gate.shape[2]
    weights = (w_gate[0], w_up[0], w_down[0])
    siblings = [(i, i ^ 1) for i in range(replicas)]
    first = lax.axis_index("expert") if apart else 0
    ids = jnp.stack([jnp.asarray(first, jnp.int32), lax.axis_index("dp").astype(jnp.int32)])
    keep_row = keep[None]
    together = lax.optimization_barrier
    far_first = sorted(range(1, groups), key=lambda k: abs(k - groups / 2))
    late = [k for k in LATE_ONES if k < groups - 1]

    def at_once(block):
        block = block.reshape(groups, capacity, -1)
        moved = lax.all_to_all(block, "expert", split_axis=0, concat_axis=0, tiled=True)
        return moved.reshape(slots, -1)

    def steps(blocks, ks):
        return {
            k: lax.ppermute(blocks[k], "expert", [(i, (i + k) % groups) for i in range(groups)]) for k in ks
        }

    def arranged(own, moved):
        return [own] + [moved[k] for k in range(1, groups)]

    def to_chips(arrays):
        return [
            lax.ppermute(
                array,
                "dp",
                [
                    (start * cores + i, (start + shift) % chips * cores + i)
                    for start in range(chips)
                    for i in range(cores)
                ],
            )
            for shift, array in enumerate(arrays, 1)
        ]

    def from_sibling(arrays):
        return [lax.ppermute(array, "dp", siblings) for array in arrays] if cores == 2 else []

    def to_others(array):
        return to_chips([array] * (chips - 1))

    blocks, place, pick = dispatch(ids, tokens, routes.T, groups, capacity, n_blocks)
    blocks = arranged(blocks[0], steps(blocks, far_first)) if apart else [at_once(blocks[0])]
    local_out, local_silu, local_factor, local_hidden, tokens_on, *on = forward_local(tokens, *weights, keep_row)
    out, rows, hidden, silu, factor, x_send = forward(
        ids, blocks, tokens_on, local_hidden, *on, chips, cores, part
    )
    returned = at_once(out)
    x_far = to_chips(x_send)
    h_far = to_others(hidden)
    returned, x_far = together((returned, x_far))
    blocks, local_cot = mix(returned, place, pick, gates.T, keep_row, cotangent, local_out, n_blocks)
    if apart:
        moved = steps(blocks, [k for k in far_first if k not in late])
        local_cot, h_far, moved[groups - 1] = together((local_cot, h_far, moved[groups - 1]))
    else:
        local_cot, h_far = together((local_cot, h_far))
    local_back, on, kept, l_send = backward_local(
        ids, local_cot, local_silu, local_factor, *weights, (silu, factor), chips, cores, part
    )
    if apart:
        if LATE:
            l_send, later = together((l_send, {k: blocks[k] for k in late}))
        else:
            later = blocks
        blocks = arranged(blocks[0], moved | steps(later, late))
    else:
        blocks = [at_once(blocks[0])]
    l_own, l_far = l_send[0], to_chips(l_send[1:])
    c_send = cut(ids, blocks, chips, cores, part)
    back, gate_back, up_back, cots = backward(ids, blocks, *kept, *on)
    returned = at_once(back)
    c_send, l_far = together((c_send, l_far))
    c_far = to_chips(c_send)
    gate_back, c_far = together((gate_back, c_far))
    g_far = to_others(gate_back)

    def terms_x(xs, at, rights, ls, section):
        return [
            ([(x, at)], [(right, 0), (l, span + section * units)], section, 1)
            for x, right, l in zip(xs, rights, ls)
        ]

    def terms_c(cs, at, ls, hs):
        return [([(c, at), (l, CHIP)], [(h, 0)], 2, 1) for c, l, h in zip(cs, ls, hs)]

    def both_cores(arrays):
        return arrays + from_sibling(arrays)

    x_near, h_near, l_near = both_cores([rows]), both_cores([hidden]), both_cores([l_own])
    g_near, u_near, c_near = both_cores([gate_back]), both_cores([up_back]), both_cores([cots])
    scale = 1.0 / replicas
    token_grads = combine(returned, pick, local_back, choose)
    totals = weight_sums(
        ids,
        cores,
        part,
        terms_x(x_near, WHOLE, g_near, l_near, 0)
        + terms_x(x_near, WHOLE, u_near, l_near, 1)
        + terms_c(c_near, WHOLE, l_near, h_near),
        None,
        units,
        (0, 1, 2),
        None if chips > 1 else scale,
    )
    if chips > 1:
        up_back, g_far, totals = together((up_back, g_far, totals))
        u_far = to_others(up_back)
        x_far, h_far, l_far = both_cores(x_far), both_cores(h_far), both_cores(l_far)
        c_far, g_far = both_cores(c_far), both_cores(g_far)
        totals = weight_sums(
            ids,
            cores,
            part,
            terms_x(x_far, CHIP, g_far, l_far, 0) + terms_c(c_far, CHIP, l_far, h_far),
            totals,
            units,
            (2, 0),
            scale,
        )
        u_far, totals, token_grads = together((u_far, totals, token_grads))
        u_other = from_sibling(u_far)
        u_far = u_far + u_other
        totals = weight_sums(
            ids, cores, part, terms_x(x_far, CHIP, u_far, l_far, 1), totals, units, (1,), scale, u_other
        )
    return (token_grads, totals[None])


def solution(mesh):
    return jax.shard_map(
        on_device,
        mesh=mesh,
        in_specs=(
            P(("dp", "expert"), None),
            P(("dp", "expert"), None),
            P(("dp", "expert"), None),
            P(("dp", "expert")),
            P(("dp", "expert"), None),
            P("expert", None, None),
            P("expert", None, None),
            P("expert", None, None),
        ),
        out_specs=(P(("dp", "expert"), None), P("expert", "dp", None)),
        check_vma=False,
    )
```

```python
import jax
import jax.numpy as jnp
from jax import lax
from jax.experimental import pallas as pl
from jax.experimental.pallas import tpu as pltpu
from jax.sharding import PartitionSpec as P

F32 = jnp.float32
BF16 = jnp.bfloat16
MIB = 1 << 20
LONG = 20_000_000_000
BACK = 20_000_000_000
SUMS = 4_000_000_000
LATE = True
CUT = True
LATE_ONES = (6, 1)
VMEM = pl.BlockSpec(memory_space=pltpu.VMEM)
SMEM = pl.BlockSpec(memory_space=pltpu.SMEM)
HBM = pl.BlockSpec(memory_space=pltpu.HBM)


def logistic_parts(act):
    sigma = jax.nn.sigmoid(act)
    return (act * sigma, sigma * (1.0 + act * (1.0 - sigma)))


def dot(left, right):
    return jnp.dot(left, right, preferred_element_type=F32)


def dot_rows(left, right):
    return lax.dot_general(left, right, (((0,), (0,)), ((), ())), preferred_element_type=F32)


def dot_back(left, weight):
    return lax.dot_general(left, weight, (((1,), (1,)), ((), ())), preferred_element_type=F32)


def tile_of(size, most):
    tile = most
    while size % tile:
        tile //= 2
    return tile


def held(array):
    return pltpu.with_memory_space_constraint(array, pltpu.HBM)


def pinned(array):
    return pltpu.with_memory_space_constraint(array, pltpu.VMEM)


def room(array):
    return pltpu.VMEM(array.shape, array.dtype)


def on_chip(dims, kind):
    return pltpu.VMEM(tuple(dims), kind)


def in_hbm(dims, kind):
    return pltpu.HBM(tuple(dims), kind)


def call(kernel, outs, operands, specs, limit, scratch=(), name=None, aliases=None, weight=0):
    return pl.pallas_call(
        kernel,
        out_shape=tuple(outs),
        in_specs=specs,
        out_specs=tuple(HBM if out.memory_space == pltpu.HBM else VMEM for out in outs),
        scratch_shapes=list(scratch),
        input_output_aliases=aliases or {},
        compiler_params=pltpu.CompilerParams(vmem_limit_bytes=limit * MIB),
        cost_estimate=pl.CostEstimate(flops=weight, bytes_accessed=0, transcendentals=0),
        name=name,
    )(*operands)


class Copies:
    def __init__(self, sems):
        self.sems, self.count, self.waiting = sems, 0, []

    def start(self, source, target, keep=False):
        copy = pltpu.make_async_copy(source, target, self.sems.at[self.count])
        self.count += 1
        copy.start()
        if keep:
            self.waiting.append(copy)
        return copy

    def finish(self):
        for copy in self.waiting:
            copy.wait()


def split(array, refs, cols):
    size = refs[0].shape[0]
    for i, ref in enumerate(refs):
        ref[:, cols] = array[i * size : (i + 1) * size]


def joined_rows(refs, cols):
    return jnp.concatenate([ref[:, cols] for ref in refs], axis=0) if len(refs) > 1 else refs[0][:, cols]


def place_of(ids_ref, cores, part):
    device = ids_ref[1]
    chip = device // cores
    return device * part, (device - chip * cores) * part, chip


def aligned(begin):
    return pl.multiple_of(begin, 128)


def chip_columns(ids_ref, shift, chips, cores, part):
    _, _, chip = place_of(ids_ref, cores, part)
    other = chip + shift
    return pl.ds(aligned(jnp.where(other >= chips, other - chips, other) * (cores * part)), cores * part)


def home_of(ids_ref, k, n_blocks):
    place = ids_ref[0] - k
    return jnp.where(place < 0, place + n_blocks, place) if n_blocks > 1 else 0


def column_of(row):
    count = row.shape[1]
    same = lax.broadcasted_iota(jnp.int32, (count, count), 0) == lax.broadcasted_iota(
        jnp.int32, (count, count), 1
    )
    return jnp.sum(jnp.where(same, row, 0.0), axis=1, keepdims=True)


def dispatch(ids, tokens, routes_t, groups, capacity, n_blocks):
    tok, width = tokens.shape
    choose = routes_t.shape[0]
    slots = groups * capacity
    pairs = choose * tok
    step = tile_of(width, 512)

    def kernel(ids_ref, tokens_hbm, routes_hbm, *refs):
        blocks, (place_hbm, pick_hbm, place_ref, pick_ref, tokens_ref, routes_ref, sems) = refs[:n_blocks], refs[n_blocks:]
        copies = Copies(sems)
        routes_in = copies.start(routes_hbm, routes_ref)
        tokens_in = copies.start(tokens_hbm, tokens_ref)
        routes_in.wait()
        chosen = routes_ref[...]
        near = chosen - ids_ref[0]
        near = jnp.where(near < 0, near + groups, near)
        expert_ids = lax.broadcasted_iota(jnp.int32, (groups, tok), 0)
        member = jnp.zeros((groups, tok), F32)
        for k in range(choose):
            member += (chosen[k : k + 1, :] == expert_ids).astype(F32)
        upper = lax.broadcasted_iota(jnp.int32, (tok, tok), 0) < lax.broadcasted_iota(
            jnp.int32, (tok, tok), 1
        )
        before = dot(member.astype(BF16), upper.astype(F32).astype(BF16))
        slot_ids = lax.broadcasted_iota(jnp.int32, (slots, tok), 0)
        both = jnp.zeros((slots, tok), F32)
        for k in range(choose):
            mine = chosen[k : k + 1, :]
            slot = jnp.sum(jnp.where(mine == expert_ids, before, 0.0), axis=0, keepdims=True).astype(jnp.int32)
            hit = (slot_ids == near[k : k + 1, :] * capacity + slot).astype(F32)
            place_ref[:, k * tok : (k + 1) * tok] = hit.astype(BF16)
            both += hit
            hit = (slot_ids == mine * capacity + slot).astype(F32)
            pick_ref[k * tok : (k + 1) * tok, :] = hit.T.astype(BF16)
        copies.start(place_ref, place_hbm, True)
        copies.start(pick_ref, pick_hbm, True)
        both = both.astype(BF16)
        tokens_in.wait()
        for n in range(0, width, step):
            cols = pl.ds(n, step)
            split(dot(both, tokens_ref[:, cols]).astype(BF16), blocks, cols)
        copies.finish()

    outs = call(
        kernel,
        [on_chip((slots // n_blocks, width), BF16)] * n_blocks
        + [in_hbm((slots, pairs), BF16), in_hbm((pairs, slots), BF16)],
        [ids, held(tokens), held(routes_t)],
        [SMEM, HBM, HBM],
        8,
        [
            pltpu.VMEM((slots, pairs), BF16),
            pltpu.VMEM((pairs, slots), BF16),
            room(tokens),
            room(routes_t),
            pltpu.SemaphoreType.DMA((4,)),
        ],
        name="dispatch",
    )
    return list(outs[:n_blocks]), *outs[n_blocks:]


def hidden_units(rows, gate_ref, up_ref, hidden_ref, silu_ref, factor_ref, f_tile):
    for j in range(0, gate_ref.shape[1], f_tile):
        cols = pl.ds(j, f_tile)
        gate = dot(rows, gate_ref[:, cols])
        up = dot(rows, up_ref[:, cols])
        silu, slope = logistic_parts(gate)
        silu_ref[:, cols] = silu
        factor_ref[:, cols] = up * slope
        hidden_ref[:, cols] = (silu * up).astype(BF16)


def forward_local(tokens, w_gate, w_up, w_down, keep_row):
    count, width = tokens.shape
    units = w_gate.shape[1]
    f_tile, d_tile = tile_of(units, 256), tile_of(width, 512)

    def kernel(tokens_hbm, gate_hbm, up_hbm, down_hbm, keep_hbm, *refs):
        out_hbm, silu_hbm, factor_hbm, hidden_ref, tokens_ref, gate_ref, up_ref, down_ref = refs[:8]
        keep_ref, out_ref, silu_ref, factor_ref, sems = refs[8:]
        copies = Copies(sems)
        arriving = [
            copies.start(source, target)
            for source, target in (
                (tokens_hbm, tokens_ref),
                (keep_hbm, keep_ref),
                (gate_hbm, gate_ref),
                (up_hbm, up_ref),
                (down_hbm, down_ref),
            )
        ]
        for copy in arriving[:4]:
            copy.wait()
        hidden_units(tokens_ref[...], gate_ref, up_ref, hidden_ref, silu_ref, factor_ref, f_tile)
        copies.start(silu_ref, silu_hbm, True)
        copies.start(factor_ref, factor_hbm, True)
        keep = column_of(keep_ref[...].astype(F32))
        arriving[4].wait()
        for n in range(0, width, d_tile):
            cols = pl.ds(n, d_tile)
            out_ref[:, cols] = keep * dot(hidden_ref[...], down_ref[:, cols])
        copies.start(out_ref, out_hbm, True)
        copies.finish()

    return call(
        kernel,
        [
            in_hbm((count, width), F32),
            in_hbm((count, units), F32),
            in_hbm((count, units), F32),
            on_chip((count, units), BF16),
            on_chip((count, width), BF16),
            on_chip(w_gate.shape, BF16),
            on_chip(w_up.shape, BF16),
            on_chip(w_down.shape, BF16),
        ],
        [held(array) for array in (tokens, w_gate, w_up, w_down, keep_row)],
        [HBM] * 5,
        8,
        [
            room(keep_row),
            pltpu.VMEM((count, width), F32),
            pltpu.VMEM((count, units), F32),
            pltpu.VMEM((count, units), F32),
            pltpu.SemaphoreType.DMA((8,)),
        ],
        name="forward_local",
        weight=LONG,
    )


def forward(ids, blocks, tokens, local_hidden, w_gate, w_up, w_down, chips, cores, part):
    n_blocks = len(blocks)
    size, width = blocks[0].shape
    count = n_blocks * size
    total = count + tokens.shape[0]
    units = w_gate.shape[1]
    f_tile, d_tile = tile_of(units, 256), tile_of(width, 512)

    def kernel(ids_ref, *refs):
        ins, refs = refs[:n_blocks], refs[n_blocks:]
        (tokens_ref, local_ref, gate_ref, up_ref, down_ref), refs = refs[:5], refs[5:]
        (out_hbm, rows_hbm, hidden_hbm, silu_hbm, factor_hbm), refs = refs[:5], refs[5:]
        sent, (out_ref, rows_ref, hidden_ref, silu_ref, factor_ref, sems) = refs[: chips - 1], refs[chips - 1 :]
        copies = Copies(sems)
        for i, ref in enumerate(ins):
            rows_ref[i * size : (i + 1) * size, :] = ref[...]
        rows_ref[count:, :] = tokens_ref[...]
        hidden_ref[count:, :] = local_ref[...]
        copies.start(rows_ref, rows_hbm, True)
        routed = pl.ds(0, count)
        hidden_units(
            rows_ref[:count, :], gate_ref, up_ref, hidden_ref.at[routed], silu_ref, factor_ref, f_tile
        )
        copies.start(hidden_ref, hidden_hbm, True)
        copies.start(silu_ref, silu_hbm, True)
        copies.start(factor_ref, factor_hbm, True)
        for n in range(0, width, d_tile):
            cols = pl.ds(n, d_tile)
            out_ref[:, cols] = dot(hidden_ref[:count, :], down_ref[:, cols]).astype(BF16)
            for k in range(n_blocks):
                target = out_hbm.at[pl.ds(home_of(ids_ref, k, n_blocks) * size, size), cols]
                copies.start(out_ref.at[pl.ds(k * size, size), cols], target, True)
        for shift, target in enumerate(sent, 1):
            target[...] = rows_ref[:, chip_columns(ids_ref, shift, chips, cores, part)]
        copies.finish()

    outs = call(
        kernel,
        [
            in_hbm((count, width), BF16),
            in_hbm((total, width), BF16),
            in_hbm((total, units), BF16),
            in_hbm((count, units), F32),
            in_hbm((count, units), F32),
        ]
        + [on_chip((total, cores * part), BF16)] * (chips - 1),
        [ids] + [pinned(array) for array in (*blocks, tokens, local_hidden, w_gate, w_up, w_down)],
        [SMEM] + [VMEM] * (n_blocks + 5),
        16,
        [
            pltpu.VMEM((count, width), BF16),
            pltpu.VMEM((total, width), BF16),
            pltpu.VMEM((total, units), BF16),
            pltpu.VMEM((count, units), F32),
            pltpu.VMEM((count, units), F32),
            pltpu.SemaphoreType.DMA((4 + n_blocks * (width // d_tile),)),
        ],
        name="forward",
    )
    return *outs[:5], list(outs[5:])


def mix(returned, place, pick, gates_t, keep_row, cotangent, local_out, n_blocks):
    slots, width = returned.shape
    choose, tok = gates_t.shape
    step = tile_of(width, 512)

    def kernel(returned_ref, *refs):
        sources, refs = refs[:6], refs[6:]
        outs, local_ref, refs = refs[:n_blocks], refs[n_blocks], refs[n_blocks + 1 :]
        targets, sems = refs[:6], refs[6]
        pick_ref, gates_ref, keep_ref, out_ref, cot_ref, place_ref = targets
        copies = Copies(sems)
        arriving = [copies.start(source, target) for source, target in zip(sources, targets)]
        for copy in arriving:
            copy.wait()
        gates = [column_of(gates_ref[k : k + 1, :]) for k in range(choose)]
        keep = column_of(keep_ref[...].astype(F32))
        for n in range(0, width, step):
            cols = pl.ds(n, step)
            picked = dot(pick_ref[...], returned_ref[:, cols])
            mixed = sum(gates[k] * picked[k * tok : (k + 1) * tok] for k in range(choose))
            difference = mixed - out_ref[:, cols]
            upstream = cot_ref[:, cols].astype(F32) + difference
            local_ref[:, cols] = (-(keep * difference)).astype(BF16)
            routed = jnp.concatenate([(gate * upstream).astype(BF16) for gate in gates], axis=0)
            split(dot(place_ref[...], routed).astype(BF16), outs, cols)

    brought = [pick, gates_t, keep_row, local_out, cotangent, place]
    outs = call(
        kernel,
        [on_chip((slots // n_blocks, width), BF16)] * n_blocks + [on_chip((tok, width), BF16)],
        [returned] + [held(array) for array in brought],
        [VMEM] + [HBM] * 6,
        10,
        [room(array) for array in brought] + [pltpu.SemaphoreType.DMA((6,))],
        name="mix",
    )
    return list(outs[:n_blocks]), outs[n_blocks]


def gradients(cots, silu_ref, factor_ref, down_ref, gate_back, up_back, f_tile):
    for j in range(0, gate_back.shape[1], f_tile):
        cols = pl.ds(j, f_tile)
        grad = dot_back(cots, down_ref[cols, :])
        gate_back[:, cols] = (grad * factor_ref[:, cols]).astype(BF16)
        up_back[:, cols] = (grad * silu_ref[:, cols]).astype(BF16)


def backward_local(ids, cots, silu, factor, w_gate, w_up, w_down, kept, chips, cores, part):
    count, width = cots.shape
    units = w_gate.shape[1]
    f_tile, d_tile = tile_of(units, 256), tile_of(width, 512)
    span = cores * part
    n_kept = len(kept)

    def kernel(ids_ref, cots_ref, silu_hbm, factor_hbm, gate_hbm, up_hbm, down_hbm, *refs):
        kept_hbm, (back_hbm, gate_ref, up_ref, down_ref), refs = refs[:n_kept], refs[n_kept : n_kept + 4], refs[n_kept + 4 :]
        kept_refs, sent, refs = refs[:n_kept], refs[n_kept : n_kept + chips], refs[n_kept + chips :]
        back_ref, silu_ref, factor_ref, gate_back, up_back, sems = refs
        copies = Copies(sems)
        first = [copies.start(s, t) for s, t in ((silu_hbm, silu_ref), (factor_hbm, factor_ref), (down_hbm, down_ref))]
        second = [copies.start(s, t) for s, t in ((gate_hbm, gate_ref), (up_hbm, up_ref))]
        for source, target in zip(kept_hbm, kept_refs):
            copies.start(source, target, True)
        for copy in first:
            copy.wait()
        gradients(cots_ref[...], silu_ref, factor_ref, down_ref, gate_back, up_back, f_tile)
        for shift, target in enumerate(sent):
            target[:, :span] = cots_ref[:, chip_columns(ids_ref, shift, chips, cores, part)]
            target[:, span : span + units] = gate_back[...]
            target[:, span + units :] = up_back[...]
        for copy in second:
            copy.wait()
        for n in range(0, width, d_tile):
            cols = pl.ds(n, d_tile)
            back = dot_back(gate_back[...], gate_ref[cols, :])
            back += dot_back(up_back[...], up_ref[cols, :])
            back_ref[:, cols] = back
        copies.start(back_ref, back_hbm, True)
        copies.finish()

    outs = call(
        kernel,
        [in_hbm((count, width), F32)]
        + [on_chip(array.shape, array.dtype) for array in (w_gate, w_up, w_down, *kept)]
        + [on_chip((count, span + 2 * units), BF16)] * chips,
        [ids, pinned(cots)] + [held(array) for array in (silu, factor, w_gate, w_up, w_down, *kept)],
        [SMEM, VMEM] + [HBM] * (5 + n_kept),
        10,
        [
            pltpu.VMEM((count, width), F32),
            room(silu),
            room(factor),
            pltpu.VMEM((count, units), BF16),
            pltpu.VMEM((count, units), BF16),
            pltpu.SemaphoreType.DMA((6 + n_kept,)),
        ],
        name="backward_local",
        weight=LONG,
    )
    return outs[0], outs[1:4], outs[4 : 4 + n_kept], list(outs[4 + n_kept :])


def cut(ids, blocks, chips, cores, part):
    n_blocks = len(blocks)
    size, width = blocks[0].shape
    count, span = n_blocks * size, cores * part
    if chips == 1:
        return []

    def kernel(ids_ref, *refs):
        ins, sent, (sent_ref, sems) = refs[:n_blocks], refs[n_blocks:-2], refs[-2:]
        copies = Copies(sems)
        for shift, target in enumerate(sent, 1):
            for i, ref in enumerate(ins):
                columns = chip_columns(ids_ref, shift, chips, cores, part)
                sent_ref[shift - 1, i * size : (i + 1) * size, :] = ref[:, columns]
            copies.start(sent_ref.at[shift - 1], target, True)
        copies.finish()

    return list(
        call(
            kernel,
            [in_hbm((count, span), BF16)] * (chips - 1),
            [ids] + [pinned(block) for block in blocks],
            [SMEM] + [VMEM] * n_blocks,
            8,
            [pltpu.VMEM((chips - 1, count, span), BF16), pltpu.SemaphoreType.DMA((chips - 1,))],
            name="cut",
        )
    )


def backward(ids, blocks, silu, factor, w_gate, w_up, w_down):
    n_blocks = len(blocks)
    size, width = blocks[0].shape
    count = n_blocks * size
    units = w_gate.shape[1]
    f_tile, d_tile = tile_of(units, 256), tile_of(width, 512)

    def kernel(ids_ref, *refs):
        ins, refs = refs[:n_blocks], refs[n_blocks:]
        silu_ref, factor_ref, gate_ref, up_ref, down_ref, back_hbm, gate_hbm, up_hbm, cots_hbm = refs[:9]
        cots_ref, back_ref, gate_back, up_back, sems = refs[9:]
        copies = Copies(sems)
        for i, ref in enumerate(ins):
            cots_ref[i * size : (i + 1) * size, :] = ref[...]
        copies.start(cots_ref, cots_hbm, True)
        gradients(cots_ref[...], silu_ref, factor_ref, down_ref, gate_back, up_back, f_tile)
        copies.start(gate_back, gate_hbm, True)
        copies.start(up_back, up_hbm, True)
        for n in range(0, width, d_tile):
            cols = pl.ds(n, d_tile)
            back = dot_back(gate_back[...], gate_ref[cols, :])
            back += dot_back(up_back[...], up_ref[cols, :])
            back_ref[:, cols] = back.astype(BF16)
            for k in range(n_blocks):
                target = back_hbm.at[pl.ds(home_of(ids_ref, k, n_blocks) * size, size), cols]
                copies.start(back_ref.at[pl.ds(k * size, size), cols], target, True)
        copies.finish()

    return call(
        kernel,
        [
            in_hbm((count, width), BF16),
            in_hbm((count, units), BF16),
            in_hbm((count, units), BF16),
            in_hbm((count, width), BF16),
        ],
        [ids] + [pinned(array) for array in (*blocks, silu, factor, w_gate, w_up, w_down)],
        [SMEM] + [VMEM] * (n_blocks + 5),
        12,
        [
            pltpu.VMEM((count, width), BF16),
            pltpu.VMEM((count, width), BF16),
            pltpu.VMEM((count, units), BF16),
            pltpu.VMEM((count, units), BF16),
            pltpu.SemaphoreType.DMA((3 + n_blocks * (width // d_tile),)),
        ],
        name="backward",
        weight=BACK,
    )


WHOLE, CHIP = -1, -2


def weight_sums(ids, cores, part, terms, previous, units, sections, scale, at_hand=()):
    step = tile_of(units, 256)
    begun = [] if previous is None else [previous]
    arrays = []
    for left, right, *_ in terms:
        for array, _ in left + right:
            arrays += [] if any(array is other for other in arrays) else [array]
    where = lambda array: next(i for i, other in enumerate(arrays) if other is array)
    rows_of = [sum(array.shape[0] for array, _ in left) for left, *_ in terms]
    n_copies = sum(len(left) + len(right) for left, right, *_ in terms)

    def kernel(ids_ref, *refs):
        sources, refs = refs[: len(arrays)], refs[len(arrays) :]
        begun_hbm, out_hbm, refs = refs[: len(begun)], refs[len(begun)], refs[len(begun) + 1 :]
        lefts, rights, out_ref, sems = refs[: len(terms)], refs[len(terms) : 2 * len(terms)], refs[-2], refs[-1]
        copies = Copies(sems)
        at_whole, at_chip, _ = place_of(ids_ref, cores, part)

        def bring(pieces, target, columns):
            row, started = 0, []
            for array, first in pieces:
                first = aligned(at_whole if first == WHOLE else at_chip) if first < 0 else first
                count = array.shape[0]
                source = sources[where(array)].at[:, pl.ds(first, columns)]
                started.append(copies.start(source, target.at[pl.ds(row, count), :]))
                row += count
            return started

        arriving = []
        for (left, right, _, wide), left_ref, right_ref in zip(terms, lefts, rights):
            arriving += bring(left, left_ref, part) + bring(right, right_ref, wide * units)
        for source in begun_hbm:
            for section in sections:
                cols = pl.ds(section * units, units)
                arriving.append(copies.start(source.at[:, cols], out_ref.at[:, cols]))
        for copy in arriving:
            copy.wait()
        for section in sections:
            for at in range(0, units, step):
                cols = pl.ds(section * units + at, step)
                total = out_ref[:, cols] if begun else None
                for i, (_, _, first, wide) in enumerate(terms):
                    if first <= section < first + wide:
                        begin = (section - first) * units + at
                        term = dot_rows(lefts[i][...], rights[i][:, begin : begin + step])
                        total = term if total is None else total + term
                out_ref[:, cols] = total if scale is None else total * scale
                copies.start(out_ref.at[:, cols], out_hbm.at[:, cols], True)
        copies.finish()

    here = [any(array is other for other in at_hand) for array in (*arrays, *begun)]
    operands = [ids] + [pinned(a) if on else held(a) for a, on in zip((*arrays, *begun), here)]
    (out,) = call(
        kernel,
        [in_hbm((part, 3 * units), F32)],
        operands,
        [SMEM] + [VMEM if on else HBM for on in here],
        20,
        [pltpu.VMEM((rows, part), BF16) for rows in rows_of]
        + [pltpu.VMEM((rows, wide * units), BF16) for rows, (*_, wide) in zip(rows_of, terms)]
        + [
            pltpu.VMEM((part, 3 * units), F32),
            pltpu.SemaphoreType.DMA((n_copies + len(begun) * len(sections) + len(sections) * (units // step),)),
        ],
        name="weight_sums",
        weight=SUMS if len(sections) > 1 else 0,
        aliases={len(operands) - 1: 0} if begun else None,
    )
    return out


def combine(returned, pick, local_back, choose):
    slots, width = returned.shape
    tok = local_back.shape[0]
    step = tile_of(width, 512)

    def kernel(returned_ref, pick_hbm, local_hbm, out_hbm, pick_ref, local_ref, out_ref, sems):
        copies = Copies(sems)
        pick_in = copies.start(pick_hbm, pick_ref)
        local_in = copies.start(local_hbm, local_ref)
        pick_in.wait()
        local_in.wait()
        both = sum(pick_ref[k * tok : (k + 1) * tok, :].astype(F32) for k in range(choose)).astype(BF16)
        for n in range(0, width, step):
            cols = pl.ds(n, step)
            out_ref[:, cols] = (dot(both, returned_ref[:, cols]) + local_ref[:, cols]).astype(BF16)
            copies.start(out_ref.at[:, cols], out_hbm.at[:, cols], True)
        copies.finish()

    (out,) = call(
        kernel,
        [in_hbm((tok, width), BF16)],
        [returned, held(pick), held(local_back)],
        [VMEM, HBM, HBM],
        8,
        [
            room(pick),
            room(local_back),
            pltpu.VMEM((tok, width), BF16),
            pltpu.SemaphoreType.DMA((2 + width // step,)),
        ],
        name="combine",
    )
    return out


def on_device(tokens, routes, gates, keep, cotangent, w_gate, w_up, w_down):
    groups = lax.axis_size("expert")
    replicas = lax.axis_size("dp")
    tok_count, width = tokens.shape
    choose = routes.shape[1]
    capacity = 3 * tok_count * choose // (2 * groups)
    slots = groups * capacity
    apart = capacity % 16 == 0 and groups <= 8
    n_blocks = groups if apart else 1
    cores = 2 if replicas % 2 == 0 else 1
    chips = replicas // cores
    part = width // replicas
    span = cores * part
    units = w_gate.shape[2]
    weights = (w_gate[0], w_up[0], w_down[0])
    siblings = [(i, i ^ 1) for i in range(replicas)]
    first = lax.axis_index("expert") if apart else 0
    ids = jnp.stack([jnp.asarray(first, jnp.int32), lax.axis_index("dp").astype(jnp.int32)])
    keep_row = keep[None]
    together = lax.optimization_barrier
    far_first = sorted(range(1, groups), key=lambda k: abs(k - groups / 2))
    late = [k for k in LATE_ONES if k < groups - 1]

    def at_once(block):
        block = block.reshape(groups, capacity, -1)
        moved = lax.all_to_all(block, "expert", split_axis=0, concat_axis=0, tiled=True)
        return moved.reshape(slots, -1)

    def steps(blocks, ks):
        return {
            k: lax.ppermute(blocks[k], "expert", [(i, (i + k) % groups) for i in range(groups)]) for k in ks
        }

    def arranged(own, moved):
        return [own] + [moved[k] for k in range(1, groups)]

    def to_chips(arrays):
        return [
            lax.ppermute(
                array,
                "dp",
                [
                    (start * cores + i, (start + shift) % chips * cores + i)
                    for start in range(chips)
                    for i in range(cores)
                ],
            )
            for shift, array in enumerate(arrays, 1)
        ]

    def from_sibling(arrays):
        return [lax.ppermute(array, "dp", siblings) for array in arrays] if cores == 2 else []

    def to_others(array):
        return to_chips([array] * (chips - 1))

    blocks, place, pick = dispatch(ids, tokens, routes.T, groups, capacity, n_blocks)
    blocks = arranged(blocks[0], steps(blocks, far_first)) if apart else [at_once(blocks[0])]
    local_out, local_silu, local_factor, local_hidden, tokens_on, *on = forward_local(tokens, *weights, keep_row)
    out, rows, hidden, silu, factor, x_send = forward(
        ids, blocks, tokens_on, local_hidden, *on, chips, cores, part
    )
    returned = at_once(out)
    x_far = to_chips(x_send)
    h_far = to_others(hidden)
    returned, x_far = together((returned, x_far))
    blocks, local_cot = mix(returned, place, pick, gates.T, keep_row, cotangent, local_out, n_blocks)
    if apart:
        moved = steps(blocks, [k for k in far_first if k not in late])
        local_cot, h_far, moved[groups - 1] = together((local_cot, h_far, moved[groups - 1]))
    else:
        local_cot, h_far = together((local_cot, h_far))
    local_back, on, kept, l_send = backward_local(
        ids, local_cot, local_silu, local_factor, *weights, (silu, factor), chips, cores, part
    )
    if apart:
        if LATE:
            l_send, later = together((l_send, {k: blocks[k] for k in late}))
        else:
            later = blocks
        blocks = arranged(blocks[0], moved | steps(later, late))
    else:
        blocks = [at_once(blocks[0])]
    l_own, l_far = l_send[0], to_chips(l_send[1:])
    c_send = cut(ids, blocks, chips, cores, part)
    blocks, c_send = together((blocks, c_send)) if CUT else (blocks, c_send)
    back, gate_back, up_back, cots = backward(ids, blocks, *kept, *on)
    returned = at_once(back)
    c_send, l_far = together((c_send, l_far))
    c_far = to_chips(c_send)
    gate_back, c_far = together((gate_back, c_far))
    g_far = to_others(gate_back)

    def terms_x(xs, at, rights, ls, section):
        return [
            ([(x, at)], [(right, 0), (l, span + section * units)], section, 1)
            for x, right, l in zip(xs, rights, ls)
        ]

    def terms_c(cs, at, ls, hs):
        return [([(c, at), (l, CHIP)], [(h, 0)], 2, 1) for c, l, h in zip(cs, ls, hs)]

    def both_cores(arrays):
        return arrays + from_sibling(arrays)

    x_near, h_near, l_near = both_cores([rows]), both_cores([hidden]), both_cores([l_own])
    g_near, u_near, c_near = both_cores([gate_back]), both_cores([up_back]), both_cores([cots])
    scale = 1.0 / replicas
    token_grads = combine(returned, pick, local_back, choose)
    totals = weight_sums(
        ids,
        cores,
        part,
        terms_x(x_near, WHOLE, g_near, l_near, 0)
        + terms_x(x_near, WHOLE, u_near, l_near, 1)
        + terms_c(c_near, WHOLE, l_near, h_near),
        None,
        units,
        (0, 1, 2),
        None if chips > 1 else scale,
    )
    if chips > 1:
        up_back, g_far, totals = together((up_back, g_far, totals))
        u_far = to_others(up_back)
        x_far, h_far, l_far = both_cores(x_far), both_cores(h_far), both_cores(l_far)
        c_far, g_far = both_cores(c_far), both_cores(g_far)
        totals = weight_sums(
            ids,
            cores,
            part,
            terms_x(x_far, CHIP, g_far, l_far, 0) + terms_c(c_far, CHIP, l_far, h_far),
            totals,
            units,
            (2, 0),
            scale,
        )
        u_far, totals, token_grads = together((u_far, totals, token_grads))
        u_other = from_sibling(u_far)
        u_far = u_far + u_other
        totals = weight_sums(
            ids, cores, part, terms_x(x_far, CHIP, u_far, l_far, 1), totals, units, (1,), scale, u_other
        )
    return (token_grads, totals[None])


def solution(mesh):
    return jax.shard_map(
        on_device,
        mesh=mesh,
        in_specs=(
            P(("dp", "expert"), None),
            P(("dp", "expert"), None),
            P(("dp", "expert"), None),
            P(("dp", "expert")),
            P(("dp", "expert"), None),
            P("expert", None, None),
            P("expert", None, None),
            P("expert", None, None),
        ),
        out_specs=(P(("dp", "expert"), None), P("expert", "dp", None)),
        check_vma=False,
    )
```

```python
import jax
import jax.numpy as jnp
from jax import lax
from jax.experimental import pallas as pl
from jax.experimental.pallas import tpu as pltpu
from jax.sharding import PartitionSpec as P

F32 = jnp.float32
BF16 = jnp.bfloat16
MIB = 1 << 20
LONG = 20_000_000_000
SUMS = 4_500_000_000
VMEM = pl.BlockSpec(memory_space=pltpu.VMEM)
SMEM = pl.BlockSpec(memory_space=pltpu.SMEM)
HBM = pl.BlockSpec(memory_space=pltpu.HBM)


def logistic_parts(act):
    sigma = jax.nn.sigmoid(act)
    return (act * sigma, sigma * (1.0 + act * (1.0 - sigma)))


def dot(left, right):
    return jnp.dot(left, right, preferred_element_type=F32)


def dot_rows(left, right):
    return lax.dot_general(left, right, (((0,), (0,)), ((), ())), preferred_element_type=F32)


def dot_back(left, weight):
    return lax.dot_general(left, weight, (((1,), (1,)), ((), ())), preferred_element_type=F32)


def tile_of(size, most):
    tile = most
    while size % tile:
        tile //= 2
    return tile


def held(array):
    return pltpu.with_memory_space_constraint(array, pltpu.HBM)


def pinned(array):
    return pltpu.with_memory_space_constraint(array, pltpu.VMEM)


def room(array):
    return pltpu.VMEM(array.shape, array.dtype)


def on_chip(dims, kind):
    return pltpu.VMEM(tuple(dims), kind)


def in_hbm(dims, kind):
    return pltpu.HBM(tuple(dims), kind)


def call(kernel, outs, operands, specs, limit, scratch=(), name=None, aliases=None, weight=0):
    return pl.pallas_call(
        kernel,
        out_shape=tuple(outs),
        in_specs=specs,
        out_specs=tuple(HBM if out.memory_space == pltpu.HBM else VMEM for out in outs),
        scratch_shapes=list(scratch),
        input_output_aliases=aliases or {},
        compiler_params=pltpu.CompilerParams(vmem_limit_bytes=limit * MIB),
        cost_estimate=pl.CostEstimate(flops=weight, bytes_accessed=0, transcendentals=0),
        name=name,
    )(*operands)


class Copies:
    def __init__(self, sems):
        self.sems, self.count, self.waiting = sems, 0, []

    def start(self, source, target, keep=False):
        copy = pltpu.make_async_copy(source, target, self.sems.at[self.count])
        self.count += 1
        copy.start()
        if keep:
            self.waiting.append(copy)
        return copy

    def finish(self):
        for copy in self.waiting:
            copy.wait()


def split(array, refs, cols):
    size = refs[0].shape[0]
    for i, ref in enumerate(refs):
        ref[:, cols] = array[i * size : (i + 1) * size]


def joined_rows(refs, cols):
    return jnp.concatenate([ref[:, cols] for ref in refs], axis=0) if len(refs) > 1 else refs[0][:, cols]


def place_of(ids_ref, cores, part):
    device = ids_ref[1]
    chip = device // cores
    return device * part, (device - chip * cores) * part, chip


def aligned(begin):
    return pl.multiple_of(begin, 128)


def chip_columns(ids_ref, shift, chips, cores, part):
    _, _, chip = place_of(ids_ref, cores, part)
    other = chip + shift
    return pl.ds(aligned(jnp.where(other >= chips, other - chips, other) * (cores * part)), cores * part)


def home_of(ids_ref, k, n_blocks):
    place = ids_ref[0] - k
    return jnp.where(place < 0, place + n_blocks, place) if n_blocks > 1 else 0


def column_of(row):
    count = row.shape[1]
    same = lax.broadcasted_iota(jnp.int32, (count, count), 0) == lax.broadcasted_iota(
        jnp.int32, (count, count), 1
    )
    return jnp.sum(jnp.where(same, row, 0.0), axis=1, keepdims=True)


def dispatch(ids, tokens, routes_t, groups, capacity, n_blocks):
    tok, width = tokens.shape
    choose = routes_t.shape[0]
    slots = groups * capacity
    pairs = choose * tok
    step = tile_of(width, 512)

    def kernel(ids_ref, tokens_hbm, routes_hbm, *refs):
        blocks, (place_hbm, pick_hbm, place_ref, pick_ref, tokens_ref, routes_ref, sems) = refs[:n_blocks], refs[n_blocks:]
        copies = Copies(sems)
        routes_in = copies.start(routes_hbm, routes_ref)
        tokens_in = copies.start(tokens_hbm, tokens_ref)
        routes_in.wait()
        chosen = routes_ref[...]
        near = chosen - ids_ref[0]
        near = jnp.where(near < 0, near + groups, near)
        expert_ids = lax.broadcasted_iota(jnp.int32, (groups, tok), 0)
        member = jnp.zeros((groups, tok), F32)
        for k in range(choose):
            member += (chosen[k : k + 1, :] == expert_ids).astype(F32)
        upper = lax.broadcasted_iota(jnp.int32, (tok, tok), 0) < lax.broadcasted_iota(
            jnp.int32, (tok, tok), 1
        )
        before = dot(member.astype(BF16), upper.astype(F32).astype(BF16))
        slot_ids = lax.broadcasted_iota(jnp.int32, (slots, tok), 0)
        both = jnp.zeros((slots, tok), F32)
        for k in range(choose):
            mine = chosen[k : k + 1, :]
            slot = jnp.sum(jnp.where(mine == expert_ids, before, 0.0), axis=0, keepdims=True).astype(jnp.int32)
            hit = (slot_ids == near[k : k + 1, :] * capacity + slot).astype(F32)
            place_ref[:, k * tok : (k + 1) * tok] = hit.astype(BF16)
            both += hit
            hit = (slot_ids == mine * capacity + slot).astype(F32)
            pick_ref[k * tok : (k + 1) * tok, :] = hit.T.astype(BF16)
        copies.start(place_ref, place_hbm, True)
        copies.start(pick_ref, pick_hbm, True)
        both = both.astype(BF16)
        tokens_in.wait()
        for n in range(0, width, step):
            cols = pl.ds(n, step)
            split(dot(both, tokens_ref[:, cols]).astype(BF16), blocks, cols)
        copies.finish()

    outs = call(
        kernel,
        [on_chip((slots // n_blocks, width), BF16)] * n_blocks
        + [in_hbm((slots, pairs), BF16), in_hbm((pairs, slots), BF16)],
        [ids, held(tokens), held(routes_t)],
        [SMEM, HBM, HBM],
        8,
        [
            pltpu.VMEM((slots, pairs), BF16),
            pltpu.VMEM((pairs, slots), BF16),
            room(tokens),
            room(routes_t),
            pltpu.SemaphoreType.DMA((4,)),
        ],
        name="dispatch",
    )
    return list(outs[:n_blocks]), *outs[n_blocks:]


def hidden_units(rows, gate_ref, up_ref, hidden_ref, silu_ref, factor_ref, f_tile):
    for j in range(0, gate_ref.shape[1], f_tile):
        cols = pl.ds(j, f_tile)
        gate = dot(rows, gate_ref[:, cols])
        up = dot(rows, up_ref[:, cols])
        silu, slope = logistic_parts(gate)
        silu_ref[:, cols] = silu
        factor_ref[:, cols] = up * slope
        hidden_ref[:, cols] = (silu * up).astype(BF16)


def forward_local(tokens, w_gate, w_up, w_down, keep_row):
    count, width = tokens.shape
    units = w_gate.shape[1]
    f_tile, d_tile = tile_of(units, 256), tile_of(width, 512)

    def kernel(tokens_hbm, gate_hbm, up_hbm, down_hbm, keep_hbm, *refs):
        out_hbm, silu_hbm, factor_hbm, hidden_ref, tokens_ref, gate_ref, up_ref, down_ref = refs[:8]
        keep_ref, out_ref, silu_ref, factor_ref, sems = refs[8:]
        copies = Copies(sems)
        arriving = [
            copies.start(source, target)
            for source, target in (
                (tokens_hbm, tokens_ref),
                (keep_hbm, keep_ref),
                (gate_hbm, gate_ref),
                (up_hbm, up_ref),
                (down_hbm, down_ref),
            )
        ]
        for copy in arriving[:4]:
            copy.wait()
        hidden_units(tokens_ref[...], gate_ref, up_ref, hidden_ref, silu_ref, factor_ref, f_tile)
        copies.start(silu_ref, silu_hbm, True)
        copies.start(factor_ref, factor_hbm, True)
        keep = column_of(keep_ref[...].astype(F32))
        arriving[4].wait()
        for n in range(0, width, d_tile):
            cols = pl.ds(n, d_tile)
            out_ref[:, cols] = keep * dot(hidden_ref[...], down_ref[:, cols])
        copies.start(out_ref, out_hbm, True)
        copies.finish()

    return call(
        kernel,
        [
            in_hbm((count, width), F32),
            in_hbm((count, units), F32),
            in_hbm((count, units), F32),
            on_chip((count, units), BF16),
            on_chip((count, width), BF16),
            on_chip(w_gate.shape, BF16),
            on_chip(w_up.shape, BF16),
            on_chip(w_down.shape, BF16),
        ],
        [held(array) for array in (tokens, w_gate, w_up, w_down, keep_row)],
        [HBM] * 5,
        8,
        [
            room(keep_row),
            pltpu.VMEM((count, width), F32),
            pltpu.VMEM((count, units), F32),
            pltpu.VMEM((count, units), F32),
            pltpu.SemaphoreType.DMA((8,)),
        ],
        name="forward_local",
        weight=LONG,
    )


def forward(ids, blocks, tokens, local_hidden, w_gate, w_up, w_down, chips, cores, part):
    n_blocks = len(blocks)
    size, width = blocks[0].shape
    count = n_blocks * size
    total = count + tokens.shape[0]
    units = w_gate.shape[1]
    f_tile, d_tile = tile_of(units, 256), tile_of(width, 512)

    def kernel(ids_ref, *refs):
        ins, refs = refs[:n_blocks], refs[n_blocks:]
        (tokens_ref, local_ref, gate_ref, up_ref, down_ref), refs = refs[:5], refs[5:]
        (out_hbm, rows_hbm, hidden_hbm, silu_hbm, factor_hbm), refs = refs[:5], refs[5:]
        sent, (out_ref, rows_ref, hidden_ref, silu_ref, factor_ref, sems) = refs[: chips - 1], refs[chips - 1 :]
        copies = Copies(sems)
        for i, ref in enumerate(ins):
            rows_ref[i * size : (i + 1) * size, :] = ref[...]
        rows_ref[count:, :] = tokens_ref[...]
        hidden_ref[count:, :] = local_ref[...]
        copies.start(rows_ref, rows_hbm, True)
        routed = pl.ds(0, count)
        hidden_units(
            rows_ref[:count, :], gate_ref, up_ref, hidden_ref.at[routed], silu_ref, factor_ref, f_tile
        )
        copies.start(hidden_ref, hidden_hbm, True)
        copies.start(silu_ref, silu_hbm, True)
        copies.start(factor_ref, factor_hbm, True)
        for n in range(0, width, d_tile):
            cols = pl.ds(n, d_tile)
            out_ref[:, cols] = dot(hidden_ref[:count, :], down_ref[:, cols]).astype(BF16)
            for k in range(n_blocks):
                target = out_hbm.at[pl.ds(home_of(ids_ref, k, n_blocks) * size, size), cols]
                copies.start(out_ref.at[pl.ds(k * size, size), cols], target, True)
        for shift, target in enumerate(sent, 1):
            target[...] = rows_ref[:, chip_columns(ids_ref, shift, chips, cores, part)]
        copies.finish()

    outs = call(
        kernel,
        [
            in_hbm((count, width), BF16),
            in_hbm((total, width), BF16),
            in_hbm((total, units), BF16),
            in_hbm((count, units), F32),
            in_hbm((count, units), F32),
        ]
        + [on_chip((total, cores * part), BF16)] * (chips - 1),
        [ids] + [pinned(array) for array in (*blocks, tokens, local_hidden, w_gate, w_up, w_down)],
        [SMEM] + [VMEM] * (n_blocks + 5),
        16,
        [
            pltpu.VMEM((count, width), BF16),
            pltpu.VMEM((total, width), BF16),
            pltpu.VMEM((total, units), BF16),
            pltpu.VMEM((count, units), F32),
            pltpu.VMEM((count, units), F32),
            pltpu.SemaphoreType.DMA((4 + n_blocks * (width // d_tile),)),
        ],
        name="forward",
    )
    return *outs[:5], list(outs[5:])


def mix(returned, place, pick, gates_t, keep_row, cotangent, local_out, n_blocks):
    slots, width = returned.shape
    choose, tok = gates_t.shape
    step = tile_of(width, 512)

    def kernel(returned_ref, *refs):
        sources, refs = refs[:6], refs[6:]
        outs, local_ref, refs = refs[:n_blocks], refs[n_blocks], refs[n_blocks + 1 :]
        targets, sems = refs[:6], refs[6]
        pick_ref, gates_ref, keep_ref, out_ref, cot_ref, place_ref = targets
        copies = Copies(sems)
        arriving = [copies.start(source, target) for source, target in zip(sources, targets)]
        for copy in arriving[:3]:
            copy.wait()
        gates = [column_of(gates_ref[k : k + 1, :]) for k in range(choose)]
        keep = column_of(keep_ref[...].astype(F32))
        for n in range(0, width, step):
            cols = pl.ds(n, step)
            picked = dot(pick_ref[...], returned_ref[:, cols])
            for copy in arriving[3:] if n == 0 else []:
                copy.wait()
            mixed = sum(gates[k] * picked[k * tok : (k + 1) * tok] for k in range(choose))
            difference = mixed - out_ref[:, cols]
            upstream = cot_ref[:, cols].astype(F32) + difference
            local_ref[:, cols] = (-(keep * difference)).astype(BF16)
            routed = jnp.concatenate([(gate * upstream).astype(BF16) for gate in gates], axis=0)
            split(dot(place_ref[...], routed).astype(BF16), outs, cols)

    brought = [pick, gates_t, keep_row, local_out, cotangent, place]
    outs = call(
        kernel,
        [on_chip((slots // n_blocks, width), BF16)] * n_blocks + [on_chip((tok, width), BF16)],
        [returned] + [held(array) for array in brought],
        [VMEM] + [HBM] * 6,
        10,
        [room(array) for array in brought] + [pltpu.SemaphoreType.DMA((6,))],
        name="mix",
    )
    return list(outs[:n_blocks]), outs[n_blocks]


def gradients(cots, silu_ref, factor_ref, down_ref, gate_back, up_back, f_tile):
    for j in range(0, gate_back.shape[1], f_tile):
        cols = pl.ds(j, f_tile)
        grad = dot_back(cots, down_ref[cols, :])
        gate_back[:, cols] = (grad * factor_ref[:, cols]).astype(BF16)
        up_back[:, cols] = (grad * silu_ref[:, cols]).astype(BF16)


def backward_local(ids, cots, silu, factor, w_gate, w_up, w_down, kept, chips, cores, part):
    count, width = cots.shape
    units = w_gate.shape[1]
    f_tile, d_tile = tile_of(units, 256), tile_of(width, 512)
    span = cores * part
    n_kept = len(kept)

    def kernel(ids_ref, cots_ref, silu_hbm, factor_hbm, gate_hbm, up_hbm, down_hbm, *refs):
        kept_hbm, (back_hbm, gate_ref, up_ref, down_ref), refs = refs[:n_kept], refs[n_kept : n_kept + 4], refs[n_kept + 4 :]
        kept_refs, sent, refs = refs[:n_kept], refs[n_kept : n_kept + chips], refs[n_kept + chips :]
        back_ref, silu_ref, factor_ref, gate_back, up_back, sems = refs
        copies = Copies(sems)
        first = [copies.start(s, t) for s, t in ((silu_hbm, silu_ref), (factor_hbm, factor_ref), (down_hbm, down_ref))]
        second = [copies.start(s, t) for s, t in ((gate_hbm, gate_ref), (up_hbm, up_ref))]
        for source, target in zip(kept_hbm, kept_refs):
            copies.start(source, target, True)
        for copy in first:
            copy.wait()
        gradients(cots_ref[...], silu_ref, factor_ref, down_ref, gate_back, up_back, f_tile)
        for shift, target in enumerate(sent):
            target[:, :span] = cots_ref[:, chip_columns(ids_ref, shift, chips, cores, part)]
            target[:, span : span + units] = gate_back[...]
            target[:, span + units :] = up_back[...]
        for copy in second:
            copy.wait()
        for n in range(0, width, d_tile):
            cols = pl.ds(n, d_tile)
            back = dot_back(gate_back[...], gate_ref[cols, :])
            back += dot_back(up_back[...], up_ref[cols, :])
            back_ref[:, cols] = back
        copies.start(back_ref, back_hbm, True)
        copies.finish()

    outs = call(
        kernel,
        [in_hbm((count, width), F32)]
        + [on_chip(array.shape, array.dtype) for array in (w_gate, w_up, w_down, *kept)]
        + [on_chip((count, span + 2 * units), BF16)] * chips,
        [ids, pinned(cots)] + [held(array) for array in (silu, factor, w_gate, w_up, w_down, *kept)],
        [SMEM, VMEM] + [HBM] * (5 + n_kept),
        10,
        [
            pltpu.VMEM((count, width), F32),
            room(silu),
            room(factor),
            pltpu.VMEM((count, units), BF16),
            pltpu.VMEM((count, units), BF16),
            pltpu.SemaphoreType.DMA((6 + n_kept,)),
        ],
        name="backward_local",
        weight=LONG,
    )
    return outs[0], outs[1:4], outs[4 : 4 + n_kept], list(outs[4 + n_kept :])


def cut(ids, blocks, chips, cores, part):
    n_blocks = len(blocks)
    size, width = blocks[0].shape
    count, span = n_blocks * size, cores * part
    if chips == 1:
        return []

    def kernel(ids_ref, *refs):
        ins, sent, (sent_ref, sems) = refs[:n_blocks], refs[n_blocks:-2], refs[-2:]
        copies = Copies(sems)
        for shift, target in enumerate(sent, 1):
            for i, ref in enumerate(ins):
                columns = chip_columns(ids_ref, shift, chips, cores, part)
                sent_ref[shift - 1, i * size : (i + 1) * size, :] = ref[:, columns]
            copies.start(sent_ref.at[shift - 1], target, True)
        copies.finish()

    return list(
        call(
            kernel,
            [in_hbm((count, span), BF16)] * (chips - 1),
            [ids] + [pinned(block) for block in blocks],
            [SMEM] + [VMEM] * n_blocks,
            8,
            [pltpu.VMEM((chips - 1, count, span), BF16), pltpu.SemaphoreType.DMA((chips - 1,))],
            name="cut",
        )
    )


def backward(ids, blocks, silu, factor, w_gate, w_up, w_down):
    n_blocks = len(blocks)
    size, width = blocks[0].shape
    count = n_blocks * size
    units = w_gate.shape[1]
    f_tile, d_tile = tile_of(units, 256), tile_of(width, 512)

    def kernel(ids_ref, *refs):
        ins, refs = refs[:n_blocks], refs[n_blocks:]
        silu_ref, factor_ref, gate_ref, up_ref, down_ref, back_hbm, gate_hbm, up_hbm, cots_hbm = refs[:9]
        cots_ref, back_ref, gate_back, up_back, sems = refs[9:]
        copies = Copies(sems)
        for i, ref in enumerate(ins):
            cots_ref[i * size : (i + 1) * size, :] = ref[...]
        copies.start(cots_ref, cots_hbm, True)
        gradients(cots_ref[...], silu_ref, factor_ref, down_ref, gate_back, up_back, f_tile)
        copies.start(gate_back, gate_hbm, True)
        copies.start(up_back, up_hbm, True)
        for n in range(0, width, d_tile):
            cols = pl.ds(n, d_tile)
            back = dot_back(gate_back[...], gate_ref[cols, :])
            back += dot_back(up_back[...], up_ref[cols, :])
            back_ref[:, cols] = back.astype(BF16)
            for k in range(n_blocks):
                target = back_hbm.at[pl.ds(home_of(ids_ref, k, n_blocks) * size, size), cols]
                copies.start(back_ref.at[pl.ds(k * size, size), cols], target, True)
        copies.finish()

    return call(
        kernel,
        [
            in_hbm((count, width), BF16),
            in_hbm((count, units), BF16),
            in_hbm((count, units), BF16),
            in_hbm((count, width), BF16),
        ],
        [ids] + [pinned(array) for array in (*blocks, silu, factor, w_gate, w_up, w_down)],
        [SMEM] + [VMEM] * (n_blocks + 5),
        12,
        [
            pltpu.VMEM((count, width), BF16),
            pltpu.VMEM((count, width), BF16),
            pltpu.VMEM((count, units), BF16),
            pltpu.VMEM((count, units), BF16),
            pltpu.SemaphoreType.DMA((3 + n_blocks * (width // d_tile),)),
        ],
        name="backward",
        weight=LONG,
    )


WHOLE, CHIP = -1, -2


def weight_sums(ids, cores, part, terms, previous, units, sections, scale, at_hand=()):
    step = tile_of(units, 256)
    begun = [] if previous is None else [previous]
    arrays = []
    for left, right, *_ in terms:
        for array, _ in left + right:
            arrays += [] if any(array is other for other in arrays) else [array]
    where = lambda array: next(i for i, other in enumerate(arrays) if other is array)
    rows_of = [sum(array.shape[0] for array, _ in left) for left, *_ in terms]
    n_copies = sum(len(left) + len(right) for left, right, *_ in terms)

    def kernel(ids_ref, *refs):
        sources, refs = refs[: len(arrays)], refs[len(arrays) :]
        begun_hbm, out_hbm, refs = refs[: len(begun)], refs[len(begun)], refs[len(begun) + 1 :]
        lefts, rights, out_ref, sems = refs[: len(terms)], refs[len(terms) : 2 * len(terms)], refs[-2], refs[-1]
        copies = Copies(sems)
        at_whole, at_chip, _ = place_of(ids_ref, cores, part)

        def bring(pieces, target, columns):
            row, started = 0, []
            for array, first in pieces:
                first = aligned(at_whole if first == WHOLE else at_chip) if first < 0 else first
                count = array.shape[0]
                source = sources[where(array)].at[:, pl.ds(first, columns)]
                started.append(copies.start(source, target.at[pl.ds(row, count), :]))
                row += count
            return started

        arriving = []
        for (left, right, _, wide), left_ref, right_ref in zip(terms, lefts, rights):
            arriving += bring(left, left_ref, part) + bring(right, right_ref, wide * units)
        for source in begun_hbm:
            for section in sections:
                cols = pl.ds(section * units, units)
                arriving.append(copies.start(source.at[:, cols], out_ref.at[:, cols]))
        for copy in arriving:
            copy.wait()
        for section in sections:
            for at in range(0, units, step):
                cols = pl.ds(section * units + at, step)
                total = out_ref[:, cols] if begun else None
                for i, (_, _, first, wide) in enumerate(terms):
                    if first <= section < first + wide:
                        begin = (section - first) * units + at
                        term = dot_rows(lefts[i][...], rights[i][:, begin : begin + step])
                        total = term if total is None else total + term
                out_ref[:, cols] = total if scale is None else total * scale
                copies.start(out_ref.at[:, cols], out_hbm.at[:, cols], True)
        copies.finish()

    here = [any(array is other for other in at_hand) for array in (*arrays, *begun)]
    operands = [ids] + [pinned(a) if on else held(a) for a, on in zip((*arrays, *begun), here)]
    (out,) = call(
        kernel,
        [in_hbm((part, 3 * units), F32)],
        operands,
        [SMEM] + [VMEM if on else HBM for on in here],
        20,
        [pltpu.VMEM((rows, part), BF16) for rows in rows_of]
        + [pltpu.VMEM((rows, wide * units), BF16) for rows, (*_, wide) in zip(rows_of, terms)]
        + [
            pltpu.VMEM((part, 3 * units), F32),
            pltpu.SemaphoreType.DMA((n_copies + len(begun) * len(sections) + len(sections) * (units // step),)),
        ],
        name="weight_sums",
        weight=SUMS if len(sections) > 1 else 0,
        aliases={len(operands) - 1: 0} if begun else None,
    )
    return out


def combine(returned, pick, local_back, choose):
    slots, width = returned.shape
    tok = local_back.shape[0]
    step = tile_of(width, 512)

    def kernel(returned_ref, pick_hbm, local_hbm, out_hbm, pick_ref, local_ref, out_ref, sems):
        copies = Copies(sems)
        pick_in = copies.start(pick_hbm, pick_ref)
        local_in = copies.start(local_hbm, local_ref)
        pick_in.wait()
        local_in.wait()
        both = sum(pick_ref[k * tok : (k + 1) * tok, :].astype(F32) for k in range(choose)).astype(BF16)
        for n in range(0, width, step):
            cols = pl.ds(n, step)
            out_ref[:, cols] = (dot(both, returned_ref[:, cols]) + local_ref[:, cols]).astype(BF16)
            copies.start(out_ref.at[:, cols], out_hbm.at[:, cols], True)
        copies.finish()

    (out,) = call(
        kernel,
        [in_hbm((tok, width), BF16)],
        [returned, held(pick), held(local_back)],
        [VMEM, HBM, HBM],
        8,
        [
            room(pick),
            room(local_back),
            pltpu.VMEM((tok, width), BF16),
            pltpu.SemaphoreType.DMA((2 + width // step,)),
        ],
        name="combine",
    )
    return out


def on_device(tokens, routes, gates, keep, cotangent, w_gate, w_up, w_down):
    groups = lax.axis_size("expert")
    replicas = lax.axis_size("dp")
    tok_count, width = tokens.shape
    choose = routes.shape[1]
    capacity = 3 * tok_count * choose // (2 * groups)
    slots = groups * capacity
    apart = capacity % 16 == 0 and groups <= 8
    n_blocks = groups if apart else 1
    cores = 2 if replicas % 2 == 0 else 1
    chips = replicas // cores
    part = width // replicas
    span = cores * part
    units = w_gate.shape[2]
    weights = (w_gate[0], w_up[0], w_down[0])
    siblings = [(i, i ^ 1) for i in range(replicas)]
    first = lax.axis_index("expert") if apart else 0
    ids = jnp.stack([jnp.asarray(first, jnp.int32), lax.axis_index("dp").astype(jnp.int32)])
    keep_row = keep[None]
    together = lax.optimization_barrier
    far_first = sorted(range(1, groups), key=lambda k: abs(k - groups / 2))
    late = [k for k in (groups - 2, 1) if 0 < k < groups - 1]

    def at_once(block):
        block = block.reshape(groups, capacity, -1)
        moved = lax.all_to_all(block, "expert", split_axis=0, concat_axis=0, tiled=True)
        return moved.reshape(slots, -1)

    def steps(blocks, ks):
        return {
            k: lax.ppermute(blocks[k], "expert", [(i, (i + k) % groups) for i in range(groups)]) for k in ks
        }

    def arranged(own, moved):
        return [own] + [moved[k] for k in range(1, groups)]

    def to_chips(arrays):
        return [
            lax.ppermute(
                array,
                "dp",
                [
                    (start * cores + i, (start + shift) % chips * cores + i)
                    for start in range(chips)
                    for i in range(cores)
                ],
            )
            for shift, array in enumerate(arrays, 1)
        ]

    def from_sibling(arrays):
        return [lax.ppermute(array, "dp", siblings) for array in arrays] if cores == 2 else []

    def to_others(array):
        return to_chips([array] * (chips - 1))

    blocks, place, pick = dispatch(ids, tokens, routes.T, groups, capacity, n_blocks)
    blocks = arranged(blocks[0], steps(blocks, far_first)) if apart else [at_once(blocks[0])]
    local_out, local_silu, local_factor, local_hidden, tokens_on, *on = forward_local(tokens, *weights, keep_row)
    out, rows, hidden, silu, factor, x_send = forward(
        ids, blocks, tokens_on, local_hidden, *on, chips, cores, part
    )
    returned = at_once(out)
    x_far = to_chips(x_send)
    h_far = to_others(hidden)
    returned, x_far = together((returned, x_far))
    blocks, local_cot = mix(returned, place, pick, gates.T, keep_row, cotangent, local_out, n_blocks)
    if apart:
        moved = steps(blocks, [k for k in far_first if k not in late])
        local_cot, h_far, moved[groups - 1] = together((local_cot, h_far, moved[groups - 1]))
    else:
        local_cot, h_far = together((local_cot, h_far))
    local_back, on, kept, l_send = backward_local(
        ids, local_cot, local_silu, local_factor, *weights, (silu, factor), chips, cores, part
    )
    if apart:
        l_send, later = together((l_send, {k: blocks[k] for k in late}))
        blocks = arranged(blocks[0], moved | steps(later, late))
    else:
        blocks = [at_once(blocks[0])]
    l_own, l_far = l_send[0], to_chips(l_send[1:])
    c_send = cut(ids, blocks, chips, cores, part)
    blocks, c_send = together((blocks, c_send))
    back, gate_back, up_back, cots = backward(ids, blocks, *kept, *on)
    returned = at_once(back)
    c_send, l_far = together((c_send, l_far))
    c_far = to_chips(c_send)
    gate_back, c_far = together((gate_back, c_far))
    g_far = to_others(gate_back)

    def terms_x(xs, at, rights, ls, section):
        return [
            ([(x, at)], [(right, 0), (l, span + section * units)], section, 1)
            for x, right, l in zip(xs, rights, ls)
        ]

    def terms_c(cs, at, ls, hs):
        return [([(c, at), (l, CHIP)], [(h, 0)], 2, 1) for c, l, h in zip(cs, ls, hs)]

    def both_cores(arrays):
        return arrays + from_sibling(arrays)

    x_near, h_near, l_near = both_cores([rows]), both_cores([hidden]), both_cores([l_own])
    g_near, u_near, c_near = both_cores([gate_back]), both_cores([up_back]), both_cores([cots])
    scale = 1.0 / replicas
    token_grads = combine(returned, pick, local_back, choose)
    totals = weight_sums(
        ids,
        cores,
        part,
        terms_x(x_near, WHOLE, g_near, l_near, 0)
        + terms_x(x_near, WHOLE, u_near, l_near, 1)
        + terms_c(c_near, WHOLE, l_near, h_near),
        None,
        units,
        (0, 1, 2),
        None if chips > 1 else scale,
    )
    if chips > 1:
        up_back, g_far, totals = together((up_back, g_far, totals))
        u_far = to_others(up_back)
        x_far, h_far, l_far = both_cores(x_far), both_cores(h_far), both_cores(l_far)
        c_far, g_far = both_cores(c_far), both_cores(g_far)
        totals = weight_sums(
            ids,
            cores,
            part,
            terms_x(x_far, CHIP, g_far, l_far, 0) + terms_c(c_far, CHIP, l_far, h_far),
            totals,
            units,
            (2, 0),
            scale,
        )
        u_far, totals, token_grads = together((u_far, totals, token_grads))
        u_other = from_sibling(u_far)
        u_far = u_far + u_other
        totals = weight_sums(
            ids, cores, part, terms_x(x_far, CHIP, u_far, l_far, 1), totals, units, (1,), scale, u_other
        )
    return (token_grads, totals[None])


def solution(mesh):
    return jax.shard_map(
        on_device,
        mesh=mesh,
        in_specs=(
            P(("dp", "expert"), None),
            P(("dp", "expert"), None),
            P(("dp", "expert"), None),
            P(("dp", "expert")),
            P(("dp", "expert"), None),
            P("expert", None, None),
            P("expert", None, None),
            P("expert", None, None),
        ),
        out_specs=(P(("dp", "expert"), None), P("expert", "dp", None)),
        check_vma=False,
    )
```

```python
import jax
import jax.numpy as jnp
from jax import lax
from jax.experimental import pallas as pl
from jax.experimental.pallas import tpu as pltpu
from jax.sharding import PartitionSpec as P

F32 = jnp.float32
BF16 = jnp.bfloat16
MIB = 1 << 20
LONG = 20_000_000_000
SUMS = 4_500_000_000
VMEM = pl.BlockSpec(memory_space=pltpu.VMEM)
SMEM = pl.BlockSpec(memory_space=pltpu.SMEM)
HBM = pl.BlockSpec(memory_space=pltpu.HBM)


def logistic_parts(act):
    sigma = jax.nn.sigmoid(act)
    return (act * sigma, sigma * (1.0 + act * (1.0 - sigma)))


def dot(left, right):
    return jnp.dot(left, right, preferred_element_type=F32)


def dot_rows(left, right):
    return lax.dot_general(left, right, (((0,), (0,)), ((), ())), preferred_element_type=F32)


def dot_back(left, weight):
    return lax.dot_general(left, weight, (((1,), (1,)), ((), ())), preferred_element_type=F32)


def tile_of(size, most):
    tile = most
    while size % tile:
        tile //= 2
    return tile


def held(array):
    return pltpu.with_memory_space_constraint(array, pltpu.HBM)


def pinned(array):
    return pltpu.with_memory_space_constraint(array, pltpu.VMEM)


def room(array):
    return pltpu.VMEM(array.shape, array.dtype)


def on_chip(dims, kind):
    return pltpu.VMEM(tuple(dims), kind)


def in_hbm(dims, kind):
    return pltpu.HBM(tuple(dims), kind)


def call(kernel, outs, operands, specs, limit, scratch=(), name=None, aliases=None, weight=0):
    return pl.pallas_call(
        kernel,
        out_shape=tuple(outs),
        in_specs=specs,
        out_specs=tuple(HBM if out.memory_space == pltpu.HBM else VMEM for out in outs),
        scratch_shapes=list(scratch),
        input_output_aliases=aliases or {},
        compiler_params=pltpu.CompilerParams(vmem_limit_bytes=limit * MIB),
        cost_estimate=pl.CostEstimate(flops=weight, bytes_accessed=0, transcendentals=0),
        name=name,
    )(*operands)


class Copies:
    def __init__(self, sems):
        self.sems, self.count, self.waiting = sems, 0, []

    def start(self, source, target, keep=False):
        copy = pltpu.make_async_copy(source, target, self.sems.at[self.count])
        self.count += 1
        copy.start()
        if keep:
            self.waiting.append(copy)
        return copy

    def finish(self):
        for copy in self.waiting:
            copy.wait()


def split(array, refs, cols):
    size = refs[0].shape[0]
    for i, ref in enumerate(refs):
        ref[:, cols] = array[i * size : (i + 1) * size]


def joined_rows(refs, cols):
    return jnp.concatenate([ref[:, cols] for ref in refs], axis=0) if len(refs) > 1 else refs[0][:, cols]


def place_of(ids_ref, cores, part):
    device = ids_ref[1]
    chip = device // cores
    return device * part, (device - chip * cores) * part, chip


def aligned(begin):
    return pl.multiple_of(begin, 128)


def chip_columns(ids_ref, shift, chips, cores, part):
    _, _, chip = place_of(ids_ref, cores, part)
    other = chip + shift
    return pl.ds(aligned(jnp.where(other >= chips, other - chips, other) * (cores * part)), cores * part)


def home_of(ids_ref, k, n_blocks):
    place = ids_ref[0] - k
    return jnp.where(place < 0, place + n_blocks, place) if n_blocks > 1 else 0


def column_of(row):
    count = row.shape[1]
    same = lax.broadcasted_iota(jnp.int32, (count, count), 0) == lax.broadcasted_iota(
        jnp.int32, (count, count), 1
    )
    return jnp.sum(jnp.where(same, row, 0.0), axis=1, keepdims=True)


def dispatch(ids, tokens, routes_t, groups, capacity, n_blocks):
    tok, width = tokens.shape
    choose = routes_t.shape[0]
    slots = groups * capacity
    pairs = choose * tok
    step = tile_of(width, 512)

    def kernel(ids_ref, tokens_hbm, routes_hbm, *refs):
        blocks, (place_hbm, pick_hbm, place_ref, pick_ref, tokens_ref, routes_ref, sems) = refs[:n_blocks], refs[n_blocks:]
        copies = Copies(sems)
        routes_in = copies.start(routes_hbm, routes_ref)
        tokens_in = copies.start(tokens_hbm, tokens_ref)
        routes_in.wait()
        chosen = routes_ref[...]
        near = chosen - ids_ref[0]
        near = jnp.where(near < 0, near + groups, near)
        expert_ids = lax.broadcasted_iota(jnp.int32, (groups, tok), 0)
        member = jnp.zeros((groups, tok), F32)
        for k in range(choose):
            member += (chosen[k : k + 1, :] == expert_ids).astype(F32)
        upper = lax.broadcasted_iota(jnp.int32, (tok, tok), 0) < lax.broadcasted_iota(
            jnp.int32, (tok, tok), 1
        )
        before = dot(member.astype(BF16), upper.astype(F32).astype(BF16))
        slot_ids = lax.broadcasted_iota(jnp.int32, (slots, tok), 0)
        both = jnp.zeros((slots, tok), F32)
        for k in range(choose):
            mine = chosen[k : k + 1, :]
            slot = jnp.sum(jnp.where(mine == expert_ids, before, 0.0), axis=0, keepdims=True).astype(jnp.int32)
            hit = (slot_ids == near[k : k + 1, :] * capacity + slot).astype(F32)
            place_ref[:, k * tok : (k + 1) * tok] = hit.astype(BF16)
            both += hit
            hit = (slot_ids == mine * capacity + slot).astype(F32)
            pick_ref[k * tok : (k + 1) * tok, :] = hit.T.astype(BF16)
        copies.start(place_ref, place_hbm, True)
        copies.start(pick_ref, pick_hbm, True)
        both = both.astype(BF16)
        tokens_in.wait()
        for n in range(0, width, step):
            cols = pl.ds(n, step)
            split(dot(both, tokens_ref[:, cols]).astype(BF16), blocks, cols)
        copies.finish()

    outs = call(
        kernel,
        [on_chip((slots // n_blocks, width), BF16)] * n_blocks
        + [in_hbm((slots, pairs), BF16), in_hbm((pairs, slots), BF16)],
        [ids, held(tokens), held(routes_t)],
        [SMEM, HBM, HBM],
        8,
        [
            pltpu.VMEM((slots, pairs), BF16),
            pltpu.VMEM((pairs, slots), BF16),
            room(tokens),
            room(routes_t),
            pltpu.SemaphoreType.DMA((4,)),
        ],
        name="dispatch",
    )
    return list(outs[:n_blocks]), *outs[n_blocks:]


def hidden_units(rows, gate_ref, up_ref, hidden_ref, silu_ref, factor_ref, f_tile):
    for j in range(0, gate_ref.shape[1], f_tile):
        cols = pl.ds(j, f_tile)
        gate = dot(rows, gate_ref[:, cols])
        up = dot(rows, up_ref[:, cols])
        silu, slope = logistic_parts(gate)
        silu_ref[:, cols] = silu
        factor_ref[:, cols] = up * slope
        hidden_ref[:, cols] = (silu * up).astype(BF16)


def forward_local(tokens, w_gate, w_up, w_down, keep_row):
    count, width = tokens.shape
    units = w_gate.shape[1]
    f_tile, d_tile = tile_of(units, 256), tile_of(width, 512)

    def kernel(tokens_hbm, gate_hbm, up_hbm, down_hbm, keep_hbm, *refs):
        out_hbm, silu_hbm, factor_hbm, hidden_ref, tokens_ref, gate_ref, up_ref, down_ref = refs[:8]
        keep_ref, out_ref, silu_ref, factor_ref, sems = refs[8:]
        copies = Copies(sems)
        arriving = [
            copies.start(source, target)
            for source, target in (
                (tokens_hbm, tokens_ref),
                (keep_hbm, keep_ref),
                (gate_hbm, gate_ref),
                (up_hbm, up_ref),
                (down_hbm, down_ref),
            )
        ]
        for copy in arriving[:4]:
            copy.wait()
        hidden_units(tokens_ref[...], gate_ref, up_ref, hidden_ref, silu_ref, factor_ref, f_tile)
        copies.start(silu_ref, silu_hbm, True)
        copies.start(factor_ref, factor_hbm, True)
        keep = column_of(keep_ref[...].astype(F32))
        arriving[4].wait()
        for n in range(0, width, d_tile):
            cols = pl.ds(n, d_tile)
            out_ref[:, cols] = keep * dot(hidden_ref[...], down_ref[:, cols])
        copies.start(out_ref, out_hbm, True)
        copies.finish()

    return call(
        kernel,
        [
            in_hbm((count, width), F32),
            in_hbm((count, units), F32),
            in_hbm((count, units), F32),
            on_chip((count, units), BF16),
            on_chip((count, width), BF16),
            on_chip(w_gate.shape, BF16),
            on_chip(w_up.shape, BF16),
            on_chip(w_down.shape, BF16),
        ],
        [held(array) for array in (tokens, w_gate, w_up, w_down, keep_row)],
        [HBM] * 5,
        8,
        [
            room(keep_row),
            pltpu.VMEM((count, width), F32),
            pltpu.VMEM((count, units), F32),
            pltpu.VMEM((count, units), F32),
            pltpu.SemaphoreType.DMA((8,)),
        ],
        name="forward_local",
        weight=LONG,
    )


def forward(ids, blocks, tokens, local_hidden, w_gate, w_up, w_down, chips, cores, part):
    n_blocks = len(blocks)
    size, width = blocks[0].shape
    count = n_blocks * size
    total = count + tokens.shape[0]
    units = w_gate.shape[1]
    f_tile, d_tile = tile_of(units, 256), tile_of(width, 512)

    def kernel(ids_ref, *refs):
        ins, refs = refs[:n_blocks], refs[n_blocks:]
        (tokens_ref, local_ref, gate_ref, up_ref, down_ref), refs = refs[:5], refs[5:]
        (out_hbm, rows_hbm, hidden_hbm, silu_hbm, factor_hbm), refs = refs[:5], refs[5:]
        sent, (out_ref, rows_ref, hidden_ref, silu_ref, factor_ref, sems) = refs[: chips - 1], refs[chips - 1 :]
        copies = Copies(sems)
        for i, ref in enumerate(ins):
            rows_ref[i * size : (i + 1) * size, :] = ref[...]
        rows_ref[count:, :] = tokens_ref[...]
        hidden_ref[count:, :] = local_ref[...]
        copies.start(rows_ref, rows_hbm, True)
        routed = pl.ds(0, count)
        hidden_units(
            rows_ref[:count, :], gate_ref, up_ref, hidden_ref.at[routed], silu_ref, factor_ref, f_tile
        )
        copies.start(hidden_ref, hidden_hbm, True)
        copies.start(silu_ref, silu_hbm, True)
        copies.start(factor_ref, factor_hbm, True)
        for n in range(0, width, d_tile):
            cols = pl.ds(n, d_tile)
            out_ref[:, cols] = dot(hidden_ref[:count, :], down_ref[:, cols]).astype(BF16)
            for k in range(n_blocks):
                target = out_hbm.at[pl.ds(home_of(ids_ref, k, n_blocks) * size, size), cols]
                copies.start(out_ref.at[pl.ds(k * size, size), cols], target, True)
        for shift, target in enumerate(sent, 1):
            target[...] = rows_ref[:, chip_columns(ids_ref, shift, chips, cores, part)]
        copies.finish()

    outs = call(
        kernel,
        [
            in_hbm((count, width), BF16),
            in_hbm((total, width), BF16),
            in_hbm((total, units), BF16),
            in_hbm((count, units), F32),
            in_hbm((count, units), F32),
        ]
        + [on_chip((total, cores * part), BF16)] * (chips - 1),
        [ids] + [pinned(array) for array in (*blocks, tokens, local_hidden, w_gate, w_up, w_down)],
        [SMEM] + [VMEM] * (n_blocks + 5),
        16,
        [
            pltpu.VMEM((count, width), BF16),
            pltpu.VMEM((total, width), BF16),
            pltpu.VMEM((total, units), BF16),
            pltpu.VMEM((count, units), F32),
            pltpu.VMEM((count, units), F32),
            pltpu.SemaphoreType.DMA((4 + n_blocks * (width // d_tile),)),
        ],
        name="forward",
    )
    return *outs[:5], list(outs[5:])


def mix(returned, place, pick, gates_t, keep_row, cotangent, local_out, n_blocks):
    slots, width = returned.shape
    choose, tok = gates_t.shape
    step = tile_of(width, 512)

    def kernel(returned_ref, *refs):
        sources, refs = refs[:6], refs[6:]
        outs, local_ref, refs = refs[:n_blocks], refs[n_blocks], refs[n_blocks + 1 :]
        targets, sems = refs[:6], refs[6]
        pick_ref, gates_ref, keep_ref, out_ref, cot_ref, place_ref = targets
        copies = Copies(sems)
        arriving = [copies.start(source, target) for source, target in zip(sources, targets)]
        for copy in arriving[:3]:
            copy.wait()
        gates = [column_of(gates_ref[k : k + 1, :]) for k in range(choose)]
        keep = column_of(keep_ref[...].astype(F32))
        for n in range(0, width, step):
            cols = pl.ds(n, step)
            picked = dot(pick_ref[...], returned_ref[:, cols])
            for copy in arriving[3:] if n == 0 else []:
                copy.wait()
            mixed = sum(gates[k] * picked[k * tok : (k + 1) * tok] for k in range(choose))
            difference = mixed - out_ref[:, cols]
            upstream = cot_ref[:, cols].astype(F32) + difference
            local_ref[:, cols] = (-(keep * difference)).astype(BF16)
            routed = jnp.concatenate([(gate * upstream).astype(BF16) for gate in gates], axis=0)
            split(dot(place_ref[...], routed).astype(BF16), outs, cols)

    brought = [pick, gates_t, keep_row, local_out, cotangent, place]
    outs = call(
        kernel,
        [on_chip((slots // n_blocks, width), BF16)] * n_blocks + [on_chip((tok, width), BF16)],
        [returned] + [held(array) for array in brought],
        [VMEM] + [HBM] * 6,
        10,
        [room(array) for array in brought] + [pltpu.SemaphoreType.DMA((6,))],
        name="mix",
    )
    return list(outs[:n_blocks]), outs[n_blocks]


def gradients(cots, silu_ref, factor_ref, down_ref, gate_back, up_back, f_tile):
    for j in range(0, gate_back.shape[1], f_tile):
        cols = pl.ds(j, f_tile)
        grad = dot_back(cots, down_ref[cols, :])
        gate_back[:, cols] = (grad * factor_ref[:, cols]).astype(BF16)
        up_back[:, cols] = (grad * silu_ref[:, cols]).astype(BF16)


def backward_local(ids, cots, silu, factor, w_gate, w_up, w_down, kept, chips, cores, part):
    count, width = cots.shape
    units = w_gate.shape[1]
    f_tile, d_tile = tile_of(units, 256), tile_of(width, 512)
    span = cores * part
    n_kept = len(kept)

    def kernel(ids_ref, cots_ref, silu_hbm, factor_hbm, gate_hbm, up_hbm, down_hbm, *refs):
        kept_hbm, (back_hbm, gate_ref, up_ref, down_ref), refs = refs[:n_kept], refs[n_kept : n_kept + 4], refs[n_kept + 4 :]
        kept_refs, sent, refs = refs[:n_kept], refs[n_kept : n_kept + chips], refs[n_kept + chips :]
        back_ref, silu_ref, factor_ref, gate_back, up_back, sems = refs
        copies = Copies(sems)
        first = [copies.start(s, t) for s, t in ((silu_hbm, silu_ref), (factor_hbm, factor_ref), (down_hbm, down_ref))]
        second = [copies.start(s, t) for s, t in ((gate_hbm, gate_ref), (up_hbm, up_ref))]
        for source, target in zip(kept_hbm, kept_refs):
            copies.start(source, target, True)
        for copy in first:
            copy.wait()
        gradients(cots_ref[...], silu_ref, factor_ref, down_ref, gate_back, up_back, f_tile)
        for shift, target in enumerate(sent):
            target[:, :span] = cots_ref[:, chip_columns(ids_ref, shift, chips, cores, part)]
            target[:, span : span + units] = gate_back[...]
            target[:, span + units :] = up_back[...]
        for copy in second:
            copy.wait()
        for n in range(0, width, d_tile):
            cols = pl.ds(n, d_tile)
            back = dot_back(gate_back[...], gate_ref[cols, :])
            back += dot_back(up_back[...], up_ref[cols, :])
            back_ref[:, cols] = back
        copies.start(back_ref, back_hbm, True)
        copies.finish()

    outs = call(
        kernel,
        [in_hbm((count, width), F32)]
        + [on_chip(array.shape, array.dtype) for array in (w_gate, w_up, w_down, *kept)]
        + [on_chip((count, span + 2 * units), BF16)] * chips,
        [ids, pinned(cots)] + [held(array) for array in (silu, factor, w_gate, w_up, w_down, *kept)],
        [SMEM, VMEM] + [HBM] * (5 + n_kept),
        10,
        [
            pltpu.VMEM((count, width), F32),
            room(silu),
            room(factor),
            pltpu.VMEM((count, units), BF16),
            pltpu.VMEM((count, units), BF16),
            pltpu.SemaphoreType.DMA((6 + n_kept,)),
        ],
        name="backward_local",
        weight=LONG,
    )
    return outs[0], outs[1:4], outs[4 : 4 + n_kept], list(outs[4 + n_kept :])


def cut(ids, blocks, chips, cores, part):
    n_blocks = len(blocks)
    size, width = blocks[0].shape
    count, span = n_blocks * size, cores * part
    if chips == 1:
        return []

    def kernel(ids_ref, *refs):
        ins, sent, (sent_ref, sems) = refs[:n_blocks], refs[n_blocks:-2], refs[-2:]
        copies = Copies(sems)
        for shift, target in enumerate(sent, 1):
            for i, ref in enumerate(ins):
                columns = chip_columns(ids_ref, shift, chips, cores, part)
                sent_ref[shift - 1, i * size : (i + 1) * size, :] = ref[:, columns]
            copies.start(sent_ref.at[shift - 1], target, True)
        copies.finish()

    return list(
        call(
            kernel,
            [in_hbm((count, span), BF16)] * (chips - 1),
            [ids] + [pinned(block) for block in blocks],
            [SMEM] + [VMEM] * n_blocks,
            8,
            [pltpu.VMEM((chips - 1, count, span), BF16), pltpu.SemaphoreType.DMA((chips - 1,))],
            name="cut",
        )
    )


def backward(ids, blocks, silu, factor, w_gate, w_up, w_down):
    n_blocks = len(blocks)
    size, width = blocks[0].shape
    count = n_blocks * size
    units = w_gate.shape[1]
    f_tile, d_tile = tile_of(units, 256), tile_of(width, 512)

    def kernel(ids_ref, *refs):
        ins, refs = refs[:n_blocks], refs[n_blocks:]
        silu_ref, factor_ref, gate_ref, up_ref, down_ref, back_hbm, gate_hbm, up_hbm, cots_hbm = refs[:9]
        cots_ref, back_ref, gate_back, up_back, sems = refs[9:]
        copies = Copies(sems)
        for i, ref in enumerate(ins):
            cots_ref[i * size : (i + 1) * size, :] = ref[...]
        copies.start(cots_ref, cots_hbm, True)
        gradients(cots_ref[...], silu_ref, factor_ref, down_ref, gate_back, up_back, f_tile)
        copies.start(gate_back, gate_hbm, True)
        copies.start(up_back, up_hbm, True)
        for n in range(0, width, d_tile):
            cols = pl.ds(n, d_tile)
            back = dot_back(gate_back[...], gate_ref[cols, :])
            back += dot_back(up_back[...], up_ref[cols, :])
            back_ref[:, cols] = back.astype(BF16)
            for k in range(n_blocks):
                target = back_hbm.at[pl.ds(home_of(ids_ref, k, n_blocks) * size, size), cols]
                copies.start(back_ref.at[pl.ds(k * size, size), cols], target, True)
        copies.finish()

    return call(
        kernel,
        [
            in_hbm((count, width), BF16),
            in_hbm((count, units), BF16),
            in_hbm((count, units), BF16),
            in_hbm((count, width), BF16),
        ],
        [ids] + [pinned(array) for array in (*blocks, silu, factor, w_gate, w_up, w_down)],
        [SMEM] + [VMEM] * (n_blocks + 5),
        12,
        [
            pltpu.VMEM((count, width), BF16),
            pltpu.VMEM((count, width), BF16),
            pltpu.VMEM((count, units), BF16),
            pltpu.VMEM((count, units), BF16),
            pltpu.SemaphoreType.DMA((3 + n_blocks * (width // d_tile),)),
        ],
        name="backward",
        weight=LONG,
    )


WHOLE, CHIP = -1, -2


def weight_sums(ids, cores, part, terms, previous, units, sections, scale, at_hand=()):
    step = tile_of(units, 256)
    begun = [] if previous is None else [previous]
    arrays = []
    for left, right, *_ in terms:
        for array, _ in left + right:
            arrays += [] if any(array is other for other in arrays) else [array]
    where = lambda array: next(i for i, other in enumerate(arrays) if other is array)
    rows_of = [sum(array.shape[0] for array, _ in left) for left, *_ in terms]
    n_copies = sum(len(left) + len(right) for left, right, *_ in terms)

    def kernel(ids_ref, *refs):
        sources, refs = refs[: len(arrays)], refs[len(arrays) :]
        begun_hbm, out_hbm, refs = refs[: len(begun)], refs[len(begun)], refs[len(begun) + 1 :]
        lefts, rights, out_ref, sems = refs[: len(terms)], refs[len(terms) : 2 * len(terms)], refs[-2], refs[-1]
        copies = Copies(sems)
        at_whole, at_chip, _ = place_of(ids_ref, cores, part)

        def bring(pieces, target, columns):
            row, started = 0, []
            for array, first in pieces:
                first = aligned(at_whole if first == WHOLE else at_chip) if first < 0 else first
                count = array.shape[0]
                source = sources[where(array)].at[:, pl.ds(first, columns)]
                started.append(copies.start(source, target.at[pl.ds(row, count), :]))
                row += count
            return started

        arriving = [
            bring(left, left_ref, part) + bring(right, right_ref, wide * units)
            for (left, right, _, wide), left_ref, right_ref in zip(terms, lefts, rights)
        ]
        started = {}
        for source in begun_hbm:
            for section in sections:
                cols = pl.ds(section * units, units)
                started[section] = copies.start(source.at[:, cols], out_ref.at[:, cols])
        for section in sections:
            for at in range(0, units, step):
                cols = pl.ds(section * units + at, step)
                total = None
                for i, (_, _, first, wide) in enumerate(terms):
                    if first <= section < first + wide:
                        begin = (section - first) * units + at
                        while arriving[i]:
                            arriving[i].pop().wait()
                        term = dot_rows(lefts[i][...], rights[i][:, begin : begin + step])
                        total = term if total is None else total + term
                if begun:
                    if at == 0:
                        started[section].wait()
                    total = out_ref[:, cols] if total is None else total + out_ref[:, cols]
                out_ref[:, cols] = total if scale is None else total * scale
                copies.start(out_ref.at[:, cols], out_hbm.at[:, cols], True)
        copies.finish()

    here = [any(array is other for other in at_hand) for array in (*arrays, *begun)]
    operands = [ids] + [pinned(a) if on else held(a) for a, on in zip((*arrays, *begun), here)]
    (out,) = call(
        kernel,
        [in_hbm((part, 3 * units), F32)],
        operands,
        [SMEM] + [VMEM if on else HBM for on in here],
        20,
        [pltpu.VMEM((rows, part), BF16) for rows in rows_of]
        + [pltpu.VMEM((rows, wide * units), BF16) for rows, (*_, wide) in zip(rows_of, terms)]
        + [
            pltpu.VMEM((part, 3 * units), F32),
            pltpu.SemaphoreType.DMA((n_copies + len(begun) * len(sections) + len(sections) * (units // step),)),
        ],
        name="weight_sums",
        weight=SUMS if len(sections) > 1 else 0,
        aliases={len(operands) - 1: 0} if begun else None,
    )
    return out


def combine(returned, pick, local_back, choose):
    slots, width = returned.shape
    tok = local_back.shape[0]
    step = tile_of(width, 512)

    def kernel(returned_ref, pick_hbm, local_hbm, out_hbm, pick_ref, local_ref, out_ref, sems):
        copies = Copies(sems)
        pick_in = copies.start(pick_hbm, pick_ref)
        local_in = copies.start(local_hbm, local_ref)
        pick_in.wait()
        local_in.wait()
        both = sum(pick_ref[k * tok : (k + 1) * tok, :].astype(F32) for k in range(choose)).astype(BF16)
        for n in range(0, width, step):
            cols = pl.ds(n, step)
            out_ref[:, cols] = (dot(both, returned_ref[:, cols]) + local_ref[:, cols]).astype(BF16)
            copies.start(out_ref.at[:, cols], out_hbm.at[:, cols], True)
        copies.finish()

    (out,) = call(
        kernel,
        [in_hbm((tok, width), BF16)],
        [returned, held(pick), held(local_back)],
        [VMEM, HBM, HBM],
        8,
        [
            room(pick),
            room(local_back),
            pltpu.VMEM((tok, width), BF16),
            pltpu.SemaphoreType.DMA((2 + width // step,)),
        ],
        name="combine",
    )
    return out


def on_device(tokens, routes, gates, keep, cotangent, w_gate, w_up, w_down):
    groups = lax.axis_size("expert")
    replicas = lax.axis_size("dp")
    tok_count, width = tokens.shape
    choose = routes.shape[1]
    capacity = 3 * tok_count * choose // (2 * groups)
    slots = groups * capacity
    apart = capacity % 16 == 0 and groups <= 8
    n_blocks = groups if apart else 1
    cores = 2 if replicas % 2 == 0 else 1
    chips = replicas // cores
    part = width // replicas
    span = cores * part
    units = w_gate.shape[2]
    weights = (w_gate[0], w_up[0], w_down[0])
    siblings = [(i, i ^ 1) for i in range(replicas)]
    first = lax.axis_index("expert") if apart else 0
    ids = jnp.stack([jnp.asarray(first, jnp.int32), lax.axis_index("dp").astype(jnp.int32)])
    keep_row = keep[None]
    together = lax.optimization_barrier
    far_first = sorted(range(1, groups), key=lambda k: abs(k - groups / 2))
    late = [k for k in (groups - 2, 1) if 0 < k < groups - 1]

    def at_once(block):
        block = block.reshape(groups, capacity, -1)
        moved = lax.all_to_all(block, "expert", split_axis=0, concat_axis=0, tiled=True)
        return moved.reshape(slots, -1)

    def steps(blocks, ks):
        return {
            k: lax.ppermute(blocks[k], "expert", [(i, (i + k) % groups) for i in range(groups)]) for k in ks
        }

    def arranged(own, moved):
        return [own] + [moved[k] for k in range(1, groups)]

    def to_chips(arrays):
        return [
            lax.ppermute(
                array,
                "dp",
                [
                    (start * cores + i, (start + shift) % chips * cores + i)
                    for start in range(chips)
                    for i in range(cores)
                ],
            )
            for shift, array in enumerate(arrays, 1)
        ]

    def from_sibling(arrays):
        return [lax.ppermute(array, "dp", siblings) for array in arrays] if cores == 2 else []

    def to_others(array):
        return to_chips([array] * (chips - 1))

    blocks, place, pick = dispatch(ids, tokens, routes.T, groups, capacity, n_blocks)
    blocks = arranged(blocks[0], steps(blocks, far_first)) if apart else [at_once(blocks[0])]
    local_out, local_silu, local_factor, local_hidden, tokens_on, *on = forward_local(tokens, *weights, keep_row)
    out, rows, hidden, silu, factor, x_send = forward(
        ids, blocks, tokens_on, local_hidden, *on, chips, cores, part
    )
    returned = at_once(out)
    x_far = to_chips(x_send)
    h_far = to_others(hidden)
    returned, x_far = together((returned, x_far))
    blocks, local_cot = mix(returned, place, pick, gates.T, keep_row, cotangent, local_out, n_blocks)
    if apart:
        moved = steps(blocks, [k for k in far_first if k not in late])
        local_cot, h_far, moved[groups - 1] = together((local_cot, h_far, moved[groups - 1]))
    else:
        local_cot, h_far = together((local_cot, h_far))
    local_back, on, kept, l_send = backward_local(
        ids, local_cot, local_silu, local_factor, *weights, (silu, factor), chips, cores, part
    )
    if apart:
        l_send, later = together((l_send, {k: blocks[k] for k in late}))
        blocks = arranged(blocks[0], moved | steps(later, late))
    else:
        blocks = [at_once(blocks[0])]
    l_own, l_far = l_send[0], to_chips(l_send[1:])
    c_send = cut(ids, blocks, chips, cores, part)
    blocks, c_send = together((blocks, c_send))
    back, gate_back, up_back, cots = backward(ids, blocks, *kept, *on)
    returned = at_once(back)
    c_send, l_far = together((c_send, l_far))
    c_far = to_chips(c_send)
    gate_back, c_far = together((gate_back, c_far))
    g_far = to_others(gate_back)

    def terms_x(xs, at, rights, ls, section):
        return [
            ([(x, at)], [(right, 0), (l, span + section * units)], section, 1)
            for x, right, l in zip(xs, rights, ls)
        ]

    def terms_c(cs, at, ls, hs):
        return [([(c, at), (l, CHIP)], [(h, 0)], 2, 1) for c, l, h in zip(cs, ls, hs)]

    def both_cores(arrays):
        return arrays + from_sibling(arrays)

    x_near, h_near, l_near = both_cores([rows]), both_cores([hidden]), both_cores([l_own])
    g_near, u_near, c_near = both_cores([gate_back]), both_cores([up_back]), both_cores([cots])
    scale = 1.0 / replicas
    token_grads = combine(returned, pick, local_back, choose)
    totals = weight_sums(
        ids,
        cores,
        part,
        terms_x(x_near, WHOLE, g_near, l_near, 0)
        + terms_x(x_near, WHOLE, u_near, l_near, 1)
        + terms_c(c_near, WHOLE, l_near, h_near),
        None,
        units,
        (0, 1, 2),
        None if chips > 1 else scale,
    )
    if chips > 1:
        up_back, g_far, totals = together((up_back, g_far, totals))
        u_far = to_others(up_back)
        x_far, h_far, l_far = both_cores(x_far), both_cores(h_far), both_cores(l_far)
        c_far, g_far = both_cores(c_far), both_cores(g_far)
        totals = weight_sums(
            ids,
            cores,
            part,
            terms_x(x_far, CHIP, g_far, l_far, 0) + terms_c(c_far, CHIP, l_far, h_far),
            totals,
            units,
            (2, 0),
            scale,
        )
        u_far, totals, token_grads = together((u_far, totals, token_grads))
        u_other = from_sibling(u_far)
        u_far = u_far + u_other
        totals = weight_sums(
            ids, cores, part, terms_x(x_far, CHIP, u_far, l_far, 1), totals, units, (1,), scale, u_other
        )
    return (token_grads, totals[None])


def solution(mesh):
    return jax.shard_map(
        on_device,
        mesh=mesh,
        in_specs=(
            P(("dp", "expert"), None),
            P(("dp", "expert"), None),
            P(("dp", "expert"), None),
            P(("dp", "expert")),
            P(("dp", "expert"), None),
            P("expert", None, None),
            P("expert", None, None),
            P("expert", None, None),
        ),
        out_specs=(P(("dp", "expert"), None), P("expert", "dp", None)),
        check_vma=False,
    )
```
